32 devices in a mesh: dp: 8 (over z, x), tensor: 4 (over y, core).
Axes of the slice: x: 2, y: 2, z: 4, core: 2. Of those that a mesh axis runs over, the one named last changes fastest.
Arguments:
- hidden_in: bfloat16 [16384, 768], P(('dp', 'tensor')), may hold values from -6 to 6
- out_grad: float32 [16384, 768], P(('dp', 'tensor')), may hold values from -11 to 11
- positions: int32 [16384], P('dp'), may hold values from 0 to 2047, as said below
- query_weight: float32 [2, 768, 768], P(None, 'dp', 'tensor'), may hold values from -0.21875 to 0.21875
- keyval_weight: float32 [768, 128], P('dp'), may hold values from -0.21875 to 0.21875
- output_weight: float32 [2, 768, 768], P(None, 'tensor', 'dp'), may hold values from -0.625 to 0.625
- up_weight: float32 [2, 768, 3072], P(None, 'dp', 'tensor'), may hold values from -0.4330127 to 0.4330127
- down_weight: float32 [2, 3072, 768], P(None, 'tensor', 'dp'), may hold values from -0.109375 to 0.109375
- norm_params: float32 [2, 4, 768], P(None, None, 'dp'), may hold values from -2 to 3
- query_first: float32 [2, 768, 768], P(None, 'dp', 'tensor'), may hold values from -768 to 768
- query_second: float32 [2, 768, 768], P(None, 'dp', 'tensor'), may hold values from 8192 to 65536
- keyval_first: float32 [768, 128], P('dp'), may hold values from -2048 to 2048
- keyval_second: float32 [768, 128], P('dp'), may hold values from 65536 to 524288
- output_first: float32 [2, 768, 768], P(None, 'tensor', 'dp'), may hold values from -384 to 384
- output_second: float32 [2, 768, 768], P(None, 'tensor', 'dp'), may hold values from 2048 to 16384
- up_first: float32 [2, 768, 3072], P(None, 'dp', 'tensor'), may hold values from -384 to 384
- up_second: float32 [2, 768, 3072], P(None, 'dp', 'tensor'), may hold values from 2048 to 16384
- down_first: float32 [2, 3072, 768], P(None, 'tensor', 'dp'), may hold values from -448 to 448
- down_second: float32 [2, 3072, 768], P(None, 'tensor', 'dp'), may hold values from 3276.8 to 26214.4
- norm_first: float32 [2, 4, 768], P(None, None, 'dp'), may hold values from -768 to 768
- norm_second: float32 [2, 4, 768], P(None, None, 'dp'), may hold values from 8192 to 65536
Outputs:
- block_out: float32 [16384, 768], P(('dp', 'tensor'))
- input_grad: float32 [16384, 768], P(('dp', 'tensor'))
- query_first_next: float32 [2, 768, 768], P(None, 'dp', 'tensor')
- query_second_next: float32 [2, 768, 768], P(None, 'dp', 'tensor')
- query_next: float32 [2, 768, 768], P(None, 'dp', 'tensor')
- query_low: bfloat16 [2, 768, 768], P(None, 'dp', 'tensor')
- keyval_first_next: float32 [768, 128], P('dp')
- keyval_second_next: float32 [768, 128], P('dp')
- keyval_next: float32 [768, 128], P('dp')
- keyval_low: bfloat16 [768, 128], P('dp')
- output_first_next: float32 [2, 768, 768], P(None, 'tensor', 'dp')
- output_second_next: float32 [2, 768, 768], P(None, 'tensor', 'dp')
- output_next: float32 [2, 768, 768], P(None, 'tensor', 'dp')
- output_low: bfloat16 [2, 768, 768], P(None, 'tensor', 'dp')
- up_first_next: float32 [2, 768, 3072], P(None, 'dp', 'tensor')
- up_second_next: float32 [2, 768, 3072], P(None, 'dp', 'tensor')
- up_next: float32 [2, 768, 3072], P(None, 'dp', 'tensor')
- up_low: bfloat16 [2, 768, 3072], P(None, 'dp', 'tensor')
- down_first_next: float32 [2, 3072, 768], P(None, 'tensor', 'dp')
- down_second_next: float32 [2, 3072, 768], P(None, 'tensor', 'dp')
- down_next: float32 [2, 3072, 768], P(None, 'tensor', 'dp')
- down_low: bfloat16 [2, 3072, 768], P(None, 'tensor', 'dp')
- norm_first_next: float32 [2, 4, 768], P(None, None, 'dp')
- norm_second_next: float32 [2, 4, 768], P(None, None, 'dp')
- norm_next: float32 [2, 4, 768], P(None, None, 'dp')
- norm_low: bfloat16 [2, 4, 768], P(None, None, 'dp')
- update_norms: float32 [17], replicated
- trust_ratios: float32 [17], replicated
The draws below stay inside these ranges and needn't reach their ends.
Inputs may be any that keep to these rules, and one draw needn't show every extreme that they name: Within each sequence of 2048 rows positions count up by one from 0 at its first row and restart at 0 where a packed document begins; one sequence, which one drawn from the seed, holds a single document, so its last row has position 2047.
All inputs are finite; a program needn't handle non-finite values.
Results may differ from the reference program's by a relative error of at most 0.024.
The reference program's roundings to bfloat16 on the way count: a program that leaves them out, or rounds other values in their place, can miss the bound.
Values may be sent and summed in bfloat16 or wider, within the bound.
A program may use at most 192 MiB of HBM per device.

```python
import math
import jax
import jax.numpy as jnp
from jax import lax

D = 768
HEADS = 12
HD = 64
FF = 3072
ROT = 16
LEN = 2048
STEP = 5
TOKENS = 16384
N_DP = 8


def draw_out_grad(key, part):
    key = jax.random.fold_in(key, 11)
    rising = jnp.arange(D).astype(jnp.float32) / D
    base = jnp.clip(jax.random.normal(key, (TOKENS, D), jnp.float32), -6.0, 6.0)
    scale = 0.6 + 1.2 * rising
    return base * scale[None, :]


def draw_positions(key, part):
    key = jax.random.fold_in(key, 12)
    mark_key, pick_key = jax.random.split(key)
    count = TOKENS // LEN
    every = max(LEN // 8, 4)
    marks = jax.random.randint(mark_key, (count, LEN), 0, every) == 0
    chosen = jax.random.randint(pick_key, (), 0, count)
    sequence = jnp.arange(count).astype(jnp.int32)
    marks = marks & (sequence != chosen)[:, None]
    index = jnp.arange(LEN).astype(jnp.int32)
    starts = lax.cummax(jnp.where(marks, index[None, :], 0), axis=1)
    return (index[None, :] - starts).reshape(TOKENS).astype(jnp.int32)


def draw_up_weight(key, part):
    key = jax.random.fold_in(key, 13)
    rising = jnp.arange(FF).astype(jnp.float32) / FF
    base = jnp.clip(jax.random.normal(key, (2, D, FF), jnp.float32), -6.0, 6.0)
    scale = 0.6 + 1.2 * rising
    return base * scale[None, None, :] * D ** (-0.5)


def draw_norm_params(key, part):
    key = jax.random.fold_in(key, 14)
    gain_key, bias_key = jax.random.split(key)
    rising = jnp.arange(D).astype(jnp.float32) / D
    jitter = jax.random.uniform(gain_key, (2, 2, D), jnp.float32, 0.85, 1.15)
    gains = (0.7 + 1.4 * rising)[None, None, :] * jitter
    biases = 0.3 * jnp.clip(jax.random.normal(bias_key, (2, 2, D), jnp.float32), -6.0, 6.0)
    return jnp.stack([gains[:, 0], biases[:, 0], gains[:, 1], biases[:, 1]], axis=1)


def block_levels(stream_key, dims, cuts, low, largest):
    def one(dim, blocks):
        draws = jax.random.uniform(jax.random.fold_in(jax.random.fold_in(stream_key, 6), dim), (blocks,), jnp.float32, low / len(cuts), largest / len(cuts))
        return jnp.repeat(jnp.exp(draws), dims[dim] // blocks).reshape((-1,) + (1,) * (len(dims) - dim - 1))

    level = one(*cuts[0])
    for cut in cuts[1:]:
        level = level * one(*cut)
    return level


def noise(key, extent, width, limit, pieces=(), dtype=jnp.bfloat16):
    entries = jax.random.normal(key, extent, jnp.float32) * width
    if len(pieces) > 0:
        entries = block_levels(key, extent, pieces, -0.22, 0.18) * entries
    return jnp.clip(entries, min=-limit, max=limit).astype(dtype)


def setup_inputs(seed: int = 0) -> dict:
    keys = jax.random.split(jax.random.key(seed), 22)
    return {
        "hidden_in": noise(keys[0], (TOKENS, D), 1.0, 6.0, ((0, 32),)),
        "out_grad": draw_out_grad(jax.random.fold_in(keys[21], 71), 0),
        "positions": draw_positions(jax.random.fold_in(keys[21], 71), 0),
        "query_weight": noise(keys[3], (2, D, D), D ** -0.5, 0.21875, ((1, 8), (2, 4)), jnp.float32),
        "keyval_weight": noise(keys[4], (D, 2 * HD), D ** -0.5, 0.21875, ((0, 8),), jnp.float32),
        "output_weight": noise(keys[5], (2, D, D), (D // 8) ** -0.5, 0.625, ((1, 4), (2, 8)), jnp.float32),
        "up_weight": draw_up_weight(jax.random.fold_in(keys[21], 71), 0),
        "down_weight": noise(keys[7], (2, FF, D), FF ** -0.5, 0.109375, ((1, 4), (2, 8)), jnp.float32),
        "norm_params": draw_norm_params(jax.random.fold_in(keys[21], 71), 0),
        "query_first": noise(keys[9], (2, D, D), (1.0 * TOKENS ** 0.5), 768.0, ((1, 8), (2, 4)), jnp.float32),
        "query_second": jnp.clip(jnp.exp(math.log(65536.0) - 2.0794415 * jax.random.uniform(keys[10], (2, D, D), jnp.float32) ** block_levels(keys[10], (2, D, D), ((1, 8), (2, 4)), -0.2, 0.2)), 8192.0, 65536.0),
        "keyval_first": noise(keys[11], (D, 2 * HD), (3.0 * TOKENS ** 0.5), 2048.0, ((0, 8),), jnp.float32),
        "keyval_second": jnp.clip(jnp.exp(math.log(524288.0) - 2.0794415 * jax.random.uniform(keys[12], (D, 2 * HD), jnp.float32) ** block_levels(keys[12], (D, 2 * HD), ((0, 8),), -0.2, 0.2)), 65536.0, 524288.0),
        "output_first": noise(keys[13], (2, D, D), (0.5 * TOKENS ** 0.5), 384.0, ((1, 4), (2, 8)), jnp.float32),
        "output_second": jnp.clip(jnp.exp(math.log(16384.0) - 2.0794415 * jax.random.uniform(keys[14], (2, D, D), jnp.float32) ** block_levels(keys[14], (2, D, D), ((1, 4), (2, 8)), -0.2, 0.2)), 2048.0, 16384.0),
        "up_first": noise(keys[15], (2, D, FF), (0.5 * TOKENS ** 0.5), 384.0, ((1, 8), (2, 4)), jnp.float32),
        "up_second": jnp.clip(jnp.exp(math.log(16384.0) - 2.0794415 * jax.random.uniform(keys[16], (2, D, FF), jnp.float32) ** block_levels(keys[16], (2, D, FF), ((1, 8), (2, 4)), -0.2, 0.2)), 2048.0, 16384.0),
        "down_first": noise(keys[17], (2, FF, D), (0.6 * TOKENS ** 0.5), 448.0, ((1, 4), (2, 8)), jnp.float32),
        "down_second": jnp.clip(jnp.exp(math.log(26214.4) - 2.0794415 * jax.random.uniform(keys[18], (2, FF, D), jnp.float32) ** block_levels(keys[18], (2, FF, D), ((1, 4), (2, 8)), -0.2, 0.2)), 3276.8, 26214.4),
        "norm_first": noise(keys[19], (2, 4, D), (1.0 * TOKENS ** 0.5), 768.0, ((2, 8),), jnp.float32),
        "norm_second": jnp.clip(jnp.exp(math.log(65536.0) - 2.0794415 * jax.random.uniform(keys[20], (2, 4, D), jnp.float32) ** block_levels(keys[20], (2, 4, D), ((2, 8),), -0.2, 0.2)), 8192.0, 65536.0),
    }


HIGHEST = lax.Precision.HIGHEST
NORM_EPSILON = 1e-05
BETA_FIRST = 0.5
BETA_SECOND = 0.55
ADAM_EPSILON = 1e-06
WEIGHT_DECAY = 0.01
LEARN_RATE = 0.5

@jax.custom_vjp
def low(v):
    return lax.optimization_barrier(v.astype(jnp.bfloat16)).astype(jnp.float32)

@jax.custom_vjp
def low_back(v):
    return v

def low_keep(v):
    return (low(v), None)

def low_pass(kept, grad):
    return (grad,)

def back_keep(v):
    return (v, None)

def back_low(kept, grad):
    return (low(grad),)
low.defvjp(low_keep, low_pass)
low_back.defvjp(back_keep, back_low)

def matmul(left, right):
    return jnp.dot(left, right, precision=HIGHEST, preferred_element_type=jnp.float32)

def layer_norm(values, gain, bias):
    center = values - lax.optimization_barrier(jnp.mean(values, axis=-1, keepdims=True))
    spread = lax.optimization_barrier(jnp.mean(center * center, axis=-1, keepdims=True))
    return center * lax.rsqrt(spread + NORM_EPSILON) * gain + bias

def angles(places):
    steps = jnp.arange(ROT // 2).astype(jnp.float32)
    inverse = jnp.exp(steps * (-2.0 * math.log(10000.0) / ROT))
    phase = places.astype(jnp.float32)[:, None] * (0.25 * inverse)[None, :]
    return (jnp.cos(phase), jnp.sin(phase))

def rotate(values, cosine, sine):
    half = ROT // 2
    first = values[..., :half]
    second = values[..., half:ROT]
    cos_rows = cosine[:, None, :]
    sin_rows = sine[:, None, :]
    return jnp.concatenate([first * cos_rows - second * sin_rows, second * cos_rows + first * sin_rows, values[..., ROT:]], axis=-1)

def attend(query, key, value):
    block = min(512, LEN)
    count = LEN // block
    scale = HD ** (-0.5)

    def one(start):
        query_block = lax.dynamic_slice_in_dim(query, start, block, 0)
        scores = jnp.einsum('qhd,kd->hqk', query_block, key, precision=HIGHEST) * scale
        scores = low_back(scores)
        rows = start + jnp.arange(block).astype(jnp.int32)
        columns = jnp.arange(LEN).astype(jnp.int32)
        scores = jnp.where((columns[None, :] <= rows[:, None])[None], scores, -1e+30)
        peak = lax.optimization_barrier(jnp.max(scores, axis=-1, keepdims=True))
        weights = jnp.exp(scores - peak)
        probs = low(weights / lax.optimization_barrier(jnp.sum(weights, axis=-1, keepdims=True)))
        return jnp.einsum('hqk,kd->qhd', probs, value, precision=HIGHEST)
    starts = (jnp.arange(count) * block).astype(jnp.int32)
    outs = lax.map(jax.checkpoint(one), starts)
    return outs.reshape(LEN, HEADS * HD)

def forward(hidden, masters, cosine, sine):
    query_low, keyval_low, output_low, up_low, down_low, norm_low = [low(array) for array in masters]
    key = None
    value = None
    for layer in range(2):
        normed_attn = low(layer_norm(hidden, norm_low[layer, 0], norm_low[layer, 1]))
        normed_mlp = low(layer_norm(hidden, norm_low[layer, 2], norm_low[layer, 3]))
        query_lin = low_back(matmul(normed_attn, query_low[layer]))
        query = low(rotate(query_lin.reshape(LEN, HEADS, HD), cosine, sine))
        if layer == 0:
            shared = low_back(matmul(normed_attn, keyval_low))
            key = low(rotate(shared[:, None, :HD], cosine, sine)[:, 0])
            value = low(shared[:, HD:])
        attended = low(low_back(attend(query, key, value)))
        active = low(jax.nn.gelu(low_back(matmul(normed_mlp, up_low[layer])), approximate=False))
        branch = low_back(matmul(attended, output_low[layer]) + matmul(active, down_low[layer]))
        hidden = hidden + branch
    return hidden

def param_squares(arrays, leader):
    query, keyval, output, upward, downward, norms = arrays
    return jnp.concatenate([lax.optimization_barrier(jnp.sum(query * query, axis=(1, 2))), (jnp.sum(keyval * keyval) * leader)[None], lax.optimization_barrier(jnp.sum(output * output, axis=(1, 2))), lax.optimization_barrier(jnp.sum(upward * upward, axis=(1, 2))), lax.optimization_barrier(jnp.sum(downward * downward, axis=(1, 2))), lax.optimization_barrier(jnp.sum(norms * norms, axis=2)).reshape(8) * leader])

def lamb_parts(weight, first, second, grad):
    first_new = BETA_FIRST * first + (1.0 - BETA_FIRST) * grad
    second_new = BETA_SECOND * second + (1.0 - BETA_SECOND) * grad * grad
    update = first_new / (1.0 - BETA_FIRST ** STEP) / (jnp.sqrt(second_new / (1.0 - BETA_SECOND ** STEP)) + ADAM_EPSILON) + WEIGHT_DECAY * weight
    return (first_new, second_new, update)

def apply_trust(masters, updates, trust):
    factors = (trust[0:2][:, None, None], trust[2], trust[3:5][:, None, None], trust[5:7][:, None, None], trust[7:9][:, None, None], trust[9:17].reshape(2, 4, 1))
    return tuple((weight - LEARN_RATE * factor * update for weight, factor, update in zip(masters, factors, updates)))

def reference(hidden_in, out_grad, positions, query_weight, keyval_weight, output_weight, up_weight, down_weight, norm_params, query_first, query_second, keyval_first, keyval_second, output_first, output_second, up_first, up_second, down_first, down_second, norm_first, norm_second):
    masters = (query_weight, keyval_weight, output_weight, up_weight, down_weight, norm_params)
    inputs = hidden_in.astype(jnp.float32).reshape(N_DP, LEN, D)
    cotangents = out_grad.reshape(N_DP, LEN, D)
    places = positions.reshape(N_DP, LEN)
    zeros = tuple((jnp.zeros(array.shape, jnp.float32) for array in masters))

    def one_sequence(totals, item):
        sequence, cotangent, place = item
        cosine, sine = angles(place)
        result, backward = jax.vjp(lambda state, params: forward(state, params, cosine, sine), sequence, masters)
        grad_in, grad_params = backward(cotangent)
        return (tuple((total + grad for total, grad in zip(totals, grad_params))), (result, grad_in))
    grads, (results, input_grads) = lax.scan(one_sequence, zeros, (inputs, cotangents, places))
    firsts = (query_first, keyval_first, output_first, up_first, down_first, norm_first)
    seconds = (query_second, keyval_second, output_second, up_second, down_second, norm_second)
    parts = [lamb_parts(weight, first, second, grad) for weight, first, second, grad in zip(masters, firsts, seconds, grads)]
    updates = tuple((part[2] for part in parts))
    weight_norm = jnp.sqrt(param_squares(masters, 1.0))
    update_norms = jnp.sqrt(param_squares(updates, 1.0))
    trust_ratios = weight_norm / update_norms
    query_next, keyval_next, output_next, up_next, down_next, norm_next = apply_trust(masters, updates, trust_ratios)
    return (results.reshape(TOKENS, D), input_grads.reshape(TOKENS, D), parts[0][0], parts[0][1], query_next, query_next.astype(jnp.bfloat16), parts[1][0], parts[1][1], keyval_next, keyval_next.astype(jnp.bfloat16), parts[2][0], parts[2][1], output_next, output_next.astype(jnp.bfloat16), parts[3][0], parts[3][1], up_next, up_next.astype(jnp.bfloat16), parts[4][0], parts[4][1], down_next, down_next.astype(jnp.bfloat16), parts[5][0], parts[5][1], norm_next, norm_next.astype(jnp.bfloat16), update_norms, trust_ratios)
```

```python
import functools
import math

import jax
import jax.numpy as jnp
from jax import lax
from jax.experimental import pallas as pl
from jax.experimental.pallas import tpu as pltpu
from jax.sharding import PartitionSpec as P

F32 = jnp.float32
BF16 = jnp.bfloat16
MESH = pl.DeviceIdType.MESH

HD = 64
ROT = 16
HALF = ROT // 2
STEP = 5
HEADS_HERE = 3
QW = 192

NORM_EPSILON = 1e-05
BETA_FIRST = 0.5
BETA_SECOND = 0.55
ADAM_EPSILON = 1e-06
WEIGHT_DECAY = 0.01
LEARN_RATE = 0.5
SCALE = HD**-0.5
MIB = 2**20


def dot(a, b):
    return jnp.dot(a, b, preferred_element_type=F32)


def dot_nt(a, b):
    return lax.dot_general(a, b, (((1,), (1,)), ((), ())), preferred_element_type=F32)


def turn(a):
    return jnp.transpose(a.astype(F32), (1, 0))


def standard(values):
    center = values - jnp.mean(values, axis=-1, keepdims=True)
    spread = jnp.mean(center * center, axis=-1, keepdims=True)
    inverse = lax.rsqrt(spread + NORM_EPSILON)
    return center * inverse, inverse


def gelu_parts(v):
    x = jnp.abs(v) * (2.0**-0.5)
    bell = jnp.exp(-x * x)
    t = 1.0 / (1.0 + 0.3275911 * x)
    series = t * (
        0.254829592
        + t * (-0.284496736 + t * (1.421413741 + t * (-1.453152027 + t * 1.061405429)))
    )
    tail = 0.5 * series * bell
    cumulative = jnp.where(v < 0.0, tail, 1.0 - tail)
    return cumulative, bell * (1.0 / math.sqrt(2.0 * math.pi))


def rotated(low, cos, sin):
    first, second = low[:HALF], low[HALF:ROT]
    return jnp.concatenate([first * cos - second * sin, second * cos + first * sin], axis=0)


def qkv_kernel(first, x_ref, norm_ref, trig_ref, qk_ref, *rest):
    if first:
        ov_ref, qt_ref, kv_ref, normed = rest
    else:
        qt_ref, normed = rest
    t = pl.program_id(0)

    @pl.when(t == 0)
    def _():
        x = x_ref[...].astype(F32)
        normed[...] = (standard(x)[0] * norm_ref[0:1] + norm_ref[1:2]).astype(BF16)

    cos, sin = trig_ref[0:HALF], trig_ref[HALF:ROT]
    lin = turn(dot(normed[...], qk_ref[0]))
    for head in range(HEADS_HERE):
        base = head * HD
        low = rotated(lin[base : base + ROT], cos, sin)
        qt_ref[0, base : base + ROT] = (low.astype(BF16).astype(F32) * SCALE).astype(BF16)
        qt_ref[0, base + ROT : base + HD] = (
            lin[base + ROT : base + HD].astype(BF16).astype(F32) * SCALE
        ).astype(BF16)
    qt_ref[0, QW:] = jnp.zeros_like(qt_ref[0, QW:])
    if first:

        @pl.when(t == 0)
        def _():
            value = turn(dot(normed[...], ov_ref[0]))[QW:]
            key = jnp.concatenate(
                [rotated(lin[QW : QW + ROT], cos, sin), lin[QW + ROT :]], axis=0
            )
            kv_ref[...] = turn(jnp.concatenate([key, value], axis=0)).astype(BF16)


def qkv_call(first, x, norms, trig, weights):
    rows, width = x.shape
    tens = weights.shape[0]
    whole = pl.BlockSpec(memory_space=pltpu.VMEM)
    in_specs = [whole, whole, whole, pl.BlockSpec((1, width, 256), lambda t: (t, 0, 6))]
    out_shape = [jax.ShapeDtypeStruct((tens, 256, rows), BF16)]
    out_specs = [pl.BlockSpec((1, 256, rows), lambda t: (t, 0, 0))]
    args = [x, norms, trig, weights]
    if first:
        in_specs.append(pl.BlockSpec((1, width, 256), lambda t: (0, 0, 7)))
        args.append(weights)
        out_shape.append(jax.ShapeDtypeStruct((rows, 2 * HD), BF16))
        out_specs.append(whole)
    return pl.pallas_call(
        functools.partial(qkv_kernel, first),
        grid=(tens,),
        in_specs=in_specs,
        out_specs=out_specs,
        out_shape=out_shape,
        scratch_shapes=[pltpu.VMEM((rows, width), BF16)],
        compiler_params=pltpu.CompilerParams(vmem_limit_bytes=32 * MIB),
    )(*args)


def attend_kernel(qt_ref, kv_ref, at_ref, lse_ref, keys, values_t):
    t = pl.program_id(0)
    rows = qt_ref.shape[2]
    place = lax.axis_index("tensor")

    @pl.when(t == 0)
    def _():
        keys[...] = kv_ref[:, :HD]
        values_t[...] = turn(kv_ref[...])[HD:].astype(BF16)

    def block(index, carry, diagonal):
        key = keys[pl.ds(pl.multiple_of(index * rows, rows), rows), :]
        value_t = values_t[:, pl.ds(pl.multiple_of(index * rows, rows), rows)]
        out = []
        for head in range(HEADS_HERE):
            scores = dot(key, qt_ref[0, head * HD : (head + 1) * HD])
            if diagonal:
                below = lax.broadcasted_iota(jnp.int32, scores.shape, 0)
                across = lax.broadcasted_iota(jnp.int32, scores.shape, 1)
                scores = jnp.where(below <= across, scores, -1e30)
            peak = jnp.max(scores, axis=0, keepdims=True)
            if carry is not None:
                peak = jnp.maximum(peak, carry[head][0])
            weights = jnp.exp(scores - peak)
            total = jnp.sum(weights, axis=0, keepdims=True)
            mixed = dot(value_t, weights.astype(BF16))
            if carry is not None:
                fade = jnp.exp(carry[head][0] - peak)
                total = total + carry[head][1] * fade
                mixed = mixed + carry[head][2] * fade
            out.append((peak, total, mixed))
        return tuple(out)

    carry = block(place, None, True)
    carry = lax.fori_loop(0, place, lambda i, c: block(i, c, False), carry)
    lse_ref[...] = jnp.zeros_like(lse_ref)
    for head in range(HEADS_HERE):
        peak, total, mixed = carry[head]
        at_ref[0, head * HD : (head + 1) * HD] = (mixed / total).astype(BF16)
        lse_ref[0, head : head + 1] = peak + jnp.log(total)
    at_ref[0, QW:] = jnp.zeros_like(at_ref[0, QW:])


def attend_call(qt, kv):
    tens, _, rows = qt.shape
    length = kv.shape[0]
    whole = pl.BlockSpec(memory_space=pltpu.VMEM)
    part = pl.BlockSpec((1, 256, rows), lambda t: (t, 0, 0))
    return pl.pallas_call(
        attend_kernel,
        grid=(tens,),
        in_specs=[part, whole],
        out_specs=[part, pl.BlockSpec((1, 8, rows), lambda t: (t, 0, 0))],
        out_shape=[
            jax.ShapeDtypeStruct((tens, 256, rows), BF16),
            jax.ShapeDtypeStruct((tens, 8, rows), F32),
        ],
        scratch_shapes=[pltpu.VMEM((length, HD), BF16), pltpu.VMEM((HD, length), BF16)],
        compiler_params=pltpu.CompilerParams(vmem_limit_bytes=48 * MIB),
    )(qt, kv)


def mix_kernel(x_ref, norm_ref, at_ref, o_ref, up_ref, down_ref, out_ref, act_ref, slope_ref, normed, total):
    t = pl.program_id(0)

    @pl.when(t == 0)
    def _():
        x = x_ref[...].astype(F32)
        normed[...] = (standard(x)[0] * norm_ref[2:3] + norm_ref[3:4]).astype(BF16)
        total[...] = x

    attended = turn(at_ref[0, :QW]).astype(BF16)
    step = 256
    for start in range(0, up_ref.shape[2], step):
        cols = pl.ds(start, step)
        pre = dot(normed[...], up_ref[0, :, cols])
        cumulative, bell = gelu_parts(pre)
        act_ref[0, :, cols] = (pre * cumulative).astype(BF16)
        slope_ref[0, :, cols] = (cumulative + pre * bell).astype(BF16)
    total[...] += dot_nt(attended, o_ref[0, :, :QW]) + dot_nt(act_ref[0], down_ref[0])

    @pl.when(t == pl.num_programs(0) - 1)
    def _():
        out_ref[...] = total[...]


def mix_call(x, norms, at, weights):
    rows, width = x.shape
    tens = weights.shape[0]
    hidden = 768
    whole = pl.BlockSpec(memory_space=pltpu.VMEM)
    wide = pl.BlockSpec((1, rows, hidden), lambda t: (t, 0, 0))
    return pl.pallas_call(
        mix_kernel,
        grid=(tens,),
        in_specs=[
            whole,
            whole,
            pl.BlockSpec((1, 256, rows), lambda t: (t, 0, 0)),
            pl.BlockSpec((1, width, 256), lambda t: (t, 0, 7)),
            pl.BlockSpec((1, width, hidden), lambda t: (t, 0, 0)),
            pl.BlockSpec((1, width, hidden), lambda t: (t, 0, 1)),
        ],
        out_specs=[whole, wide, wide],
        out_shape=[
            jax.ShapeDtypeStruct((rows, width), F32),
            jax.ShapeDtypeStruct((tens, rows, hidden), BF16),
            jax.ShapeDtypeStruct((tens, rows, hidden), BF16),
        ],
        scratch_shapes=[pltpu.VMEM((rows, width), BF16), pltpu.VMEM((rows, width), F32)],
        compiler_params=pltpu.CompilerParams(vmem_limit_bytes=48 * MIB),
    )(x, norms, at, weights, weights, weights)


def mix_back_kernel(
    gx_ref, x_ref, norm_ref, at_ref, act_ref, slope_ref, o_ref, up_ref, down_ref,
    pack_ref, dot_ref, mlp_ref, low, low_t, normed_t,
):
    t = pl.program_id(0)

    @pl.when(t == 0)
    def _():
        grad = gx_ref[...].astype(BF16)
        low[...] = grad
        low_t[...] = turn(grad).astype(BF16)
        x = x_ref[...].astype(F32)
        normed = (standard(x)[0] * norm_ref[2:3] + norm_ref[3:4]).astype(BF16)
        normed_t[...] = turn(normed).astype(BF16)
        mlp_ref[...] = jnp.zeros_like(mlp_ref)

    hidden = up_ref.shape[2]
    grad_attended = dot(low[...], o_ref[0, :, :QW])
    dot_ref[0, :QW] = turn(grad_attended).astype(BF16)
    dot_ref[0, QW:] = jnp.zeros_like(dot_ref[0, QW:])
    pack_ref[0, :, 2 * hidden :] = dot_nt(low_t[...], at_ref[0]).astype(BF16)
    pack_ref[0, :, hidden : 2 * hidden] = dot(low_t[...], act_ref[0]).astype(BF16)
    grad_pre = (dot(low[...], down_ref[0]) * slope_ref[0].astype(F32)).astype(BF16)
    pack_ref[0, :, :hidden] = dot(normed_t[...], grad_pre).astype(BF16)
    mlp_ref[...] += dot_nt(grad_pre, up_ref[0])


def mix_back_call(gx, x, norms, at, act, slope, weights):
    rows, width = x.shape
    tens = weights.shape[0]
    hidden = act.shape[2]
    whole = pl.BlockSpec(memory_space=pltpu.VMEM)
    wide = pl.BlockSpec((1, rows, hidden), lambda t: (t, 0, 0))
    part = pl.BlockSpec((1, 256, rows), lambda t: (t, 0, 0))
    return pl.pallas_call(
        mix_back_kernel,
        grid=(tens,),
        in_specs=[
            whole,
            whole,
            whole,
            part,
            wide,
            wide,
            pl.BlockSpec((1, width, 256), lambda t: (t, 0, 7)),
            pl.BlockSpec((1, width, hidden), lambda t: (t, 0, 0)),
            pl.BlockSpec((1, width, hidden), lambda t: (t, 0, 1)),
        ],
        out_specs=[
            pl.BlockSpec((1, width, 2 * hidden + 256), lambda t: (t, 0, 0)),
            part,
            whole,
        ],
        out_shape=[
            jax.ShapeDtypeStruct((tens, width, 2 * hidden + 256), BF16),
            jax.ShapeDtypeStruct((tens, 256, rows), BF16),
            jax.ShapeDtypeStruct((rows, width), F32),
        ],
        scratch_shapes=[
            pltpu.VMEM((rows, width), BF16),
            pltpu.VMEM((width, rows), BF16),
            pltpu.VMEM((width, rows), BF16),
        ],
        compiler_params=pltpu.CompilerParams(vmem_limit_bytes=56 * MIB),
    )(gx, x, norms, at, act, slope, weights, weights, weights)


def attend_back_kernel(
    start_given, qt_ref, dot_ref, at_ref, lse_ref, kv_ref, trig_ref, *rest
):
    if start_given:
        before_ref, gqt_ref, dkv_ref, keys, values, keys_t, dkeys, dvalues = rest
    else:
        gqt_ref, dkv_ref, keys, values, keys_t, dkeys, dvalues = rest
    t = pl.program_id(0)
    rows = qt_ref.shape[2]
    place = lax.axis_index("tensor")

    @pl.when(t == 0)
    def _():
        both_t = turn(kv_ref[...])
        keys[...] = kv_ref[:, :HD]
        keys_t[...] = both_t[:HD].astype(BF16)
        values[...] = turn(both_t[HD:]).astype(BF16)
        dkeys[...] = jnp.zeros_like(dkeys)
        dvalues[...] = jnp.zeros_like(dvalues)

    inner = []
    for head in range(HEADS_HERE):
        span = slice(head * HD, (head + 1) * HD)
        inner.append(
            jnp.sum(
                dot_ref[0, span].astype(F32) * at_ref[0, span].astype(F32), axis=0, keepdims=True
            )
        )

    def block(index, carry, diagonal):
        here = pl.ds(pl.multiple_of(index * rows, rows), rows)
        key = keys[here, :]
        value = values[here, :]
        key_t = keys_t[:, here]
        out = []
        dkey = None
        for head in range(HEADS_HERE):
            span = slice(head * HD, (head + 1) * HD)
            query_t = qt_ref[0, span]
            grad_t = dot_ref[0, span]
            scores = dot(key, query_t)
            probs = jnp.exp(scores - lse_ref[0, head : head + 1])
            if diagonal:
                below = lax.broadcasted_iota(jnp.int32, scores.shape, 0)
                across = lax.broadcasted_iota(jnp.int32, scores.shape, 1)
                probs = jnp.where(below <= across, probs, 0.0)
            grad_probs = dot(value, grad_t)
            grad_scores = (probs * (grad_probs - inner[head])).astype(BF16)
            part_v = dot_nt(probs.astype(BF16), grad_t)
            part_k = dot_nt(grad_scores, query_t)
            dkey = part_k if dkey is None else dkey + part_k
            dvalue = part_v if head == 0 else dvalue + part_v
            part_q = dot(key_t, grad_scores)
            out.append(part_q if carry is None else carry[head] + part_q)
        dkeys[here, :] += dkey
        dvalues[here, :] += dvalue
        return tuple(out)

    carry = block(place, None, True)
    carry = lax.fori_loop(0, place, lambda i, c: block(i, c, False), carry)
    cos, sin = trig_ref[0:HALF], trig_ref[HALF:ROT]
    for head in range(HEADS_HERE):
        base = head * HD
        grad = carry[head] * SCALE
        gqt_ref[0, base : base + ROT] = rotated(grad[:ROT], cos, -sin).astype(BF16)
        gqt_ref[0, base + ROT : base + HD] = grad[ROT:].astype(BF16)
    gqt_ref[0, QW:] = jnp.zeros_like(gqt_ref[0, QW:])

    @pl.when(t == pl.num_programs(0) - 1)
    def _():
        both = jnp.concatenate([turn(dkeys[...]), turn(dvalues[...])], axis=0)
        for part in range(dkv_ref.shape[0]):
            piece = both[:, part * rows : (part + 1) * rows]
            if start_given:
                piece = piece + before_ref[part]
            dkv_ref[part] = piece


def attend_back_call(qt, dout, at, lse, kv, trig, before=None):
    tens, _, rows = qt.shape
    length = kv.shape[0]
    whole = pl.BlockSpec(memory_space=pltpu.VMEM)
    part = pl.BlockSpec((1, 256, rows), lambda t: (t, 0, 0))
    args = [qt, dout, at, lse, kv, trig]
    in_specs = [part, part, part, pl.BlockSpec((1, 8, rows), lambda t: (t, 0, 0)), whole, whole]
    if before is not None:
        args.append(before)
        in_specs.append(whole)
    return pl.pallas_call(
        functools.partial(attend_back_kernel, before is not None),
        grid=(tens,),
        in_specs=in_specs,
        out_specs=[part, whole],
        out_shape=[
            jax.ShapeDtypeStruct((tens, 256, rows), BF16),
            jax.ShapeDtypeStruct((length // rows, 2 * HD, rows), F32),
        ],
        scratch_shapes=[
            pltpu.VMEM((length, HD), BF16),
            pltpu.VMEM((length, HD), BF16),
            pltpu.VMEM((HD, length), BF16),
            pltpu.VMEM((length, HD), F32),
            pltpu.VMEM((length, HD), F32),
        ],
        compiler_params=pltpu.CompilerParams(vmem_limit_bytes=56 * MIB),
    )(*args)


def norm_back_kernel(first, gx_ref, x_ref, norm_ref, mlp_ref, gqt_ref, qk_ref, *rest):
    if first:
        ov_ref, dkv_ref, trig_ref, out_ref, pack_ref, sums_ref, normed_t, attn, shared = rest
    else:
        out_ref, pack_ref, sums_ref, normed_t, attn = rest
    t = pl.program_id(0)

    @pl.when(t == 0)
    def _():
        x = x_ref[...].astype(F32)
        normed = (standard(x)[0] * norm_ref[0:1] + norm_ref[1:2]).astype(BF16)
        normed_t[...] = turn(normed).astype(BF16)
        if first:
            cos, sin = trig_ref[0:HALF], trig_ref[HALF:ROT]
            grad = dkv_ref[...]
            shared[:ROT] = rotated(grad[:ROT], cos, -sin).astype(BF16)
            shared[ROT:] = grad[ROT:].astype(BF16)
            attn[...] = dot_nt(turn(shared[:HD]).astype(BF16), qk_ref[0, :, QW:]) + dot_nt(
                turn(shared[HD:]).astype(BF16), ov_ref[0, :, QW:]
            )
        else:
            attn[...] = jnp.zeros_like(attn)

    grad_t = gqt_ref[0, :QW]
    attn[...] += dot_nt(turn(grad_t).astype(BF16), qk_ref[0, :, :QW])
    if first:
        left = jnp.concatenate([grad_t, shared[:HD]], axis=0)
        pack_ref[0, :, :256] = dot_nt(normed_t[...], left).astype(BF16)
        right = jnp.concatenate([shared[HD:], jnp.zeros((HD, grad_t.shape[1]), BF16)], axis=0)
        pack_ref[0, :, 256:] = dot_nt(normed_t[...], right).astype(BF16)
    else:
        pack_ref[0] = dot_nt(normed_t[...], gqt_ref[0]).astype(BF16)

    @pl.when(t == pl.num_programs(0) - 1)
    def _():
        unit, inverse = standard(x_ref[...].astype(F32))
        attn_grad, mlp_grad = attn[...], mlp_ref[...]
        sums_ref[0:1] = jnp.sum(attn_grad * unit, axis=0, keepdims=True)
        sums_ref[1:2] = jnp.sum(attn_grad, axis=0, keepdims=True)
        sums_ref[2:3] = jnp.sum(mlp_grad * unit, axis=0, keepdims=True)
        sums_ref[3:4] = jnp.sum(mlp_grad, axis=0, keepdims=True)
        grad = attn_grad * norm_ref[0:1] + mlp_grad * norm_ref[2:3]
        mean = jnp.mean(grad, axis=-1, keepdims=True)
        slant = jnp.mean(grad * unit, axis=-1, keepdims=True)
        out_ref[...] = gx_ref[...] + inverse * (grad - mean - unit * slant)


def norm_back_call(first, gx, x, norms, mlp, gqt, weights, dkv=None, trig=None):
    rows, width = x.shape
    tens = weights.shape[0]
    whole = pl.BlockSpec(memory_space=pltpu.VMEM)
    part = pl.BlockSpec((1, 256, rows), lambda t: (t, 0, 0))
    args = [gx, x, norms, mlp, gqt, weights]
    in_specs = [whole] * 4 + [part, pl.BlockSpec((1, width, 256), lambda t: (t, 0, 6))]
    scratch = [pltpu.VMEM((width, rows), BF16), pltpu.VMEM((rows, width), F32)]
    cols = 256
    if first:
        args += [weights, dkv, trig]
        in_specs += [pl.BlockSpec((1, width, 256), lambda t: (0, 0, 7)), whole, whole]
        scratch.append(pltpu.VMEM((2 * HD, rows), BF16))
        cols = 384
    return pl.pallas_call(
        functools.partial(norm_back_kernel, first),
        grid=(tens,),
        in_specs=in_specs,
        out_specs=[whole, pl.BlockSpec((1, width, cols), lambda t: (t, 0, 0)), whole],
        out_shape=[
            jax.ShapeDtypeStruct((rows, width), F32),
            jax.ShapeDtypeStruct((tens, width, cols), BF16),
            jax.ShapeDtypeStruct((4, width), F32),
        ],
        scratch_shapes=scratch,
        compiler_params=pltpu.CompilerParams(vmem_limit_bytes=48 * MIB),
    )(*args)


def tensor_barrier(count):
    me = lax.axis_index("tensor")
    barrier = pltpu.get_barrier_semaphore()
    for shift in range(1, count):
        pl.semaphore_signal(
            barrier, inc=1, device_id={"tensor": lax.rem(me + shift, count)}, device_id_type=MESH
        )
    pl.semaphore_wait(barrier, count - 1)


def share_kernel(count, mine_ref, out_ref, here_sem, send_sem, recv_sem):
    me = lax.axis_index("tensor")
    tensor_barrier(count)
    copies = []
    for shift in range(1, count):
        copies.append(
            pltpu.make_async_remote_copy(
                src_ref=mine_ref,
                dst_ref=out_ref.at[me],
                send_sem=send_sem.at[shift],
                recv_sem=recv_sem.at[shift],
                device_id={"tensor": lax.rem(me + shift, count)},
                device_id_type=MESH,
            )
        )
        copies[-1].start()
    own = pltpu.make_async_copy(mine_ref, out_ref.at[me], here_sem)
    own.start()
    own.wait()
    for copy in copies:
        copy.wait()


def share_call(mine, count):
    return pl.pallas_call(
        functools.partial(share_kernel, count),
        in_specs=[pl.BlockSpec(memory_space=pltpu.VMEM)],
        out_specs=pl.BlockSpec(memory_space=pltpu.VMEM),
        out_shape=jax.ShapeDtypeStruct((count,) + mine.shape, mine.dtype),
        scratch_shapes=[
            pltpu.SemaphoreType.DMA,
            pltpu.SemaphoreType.DMA((count,)),
            pltpu.SemaphoreType.DMA((count,)),
        ],
        compiler_params=pltpu.CompilerParams(collective_id=1, has_side_effects=True),
    )(mine)


def merge_kernel(count, parts_ref, out_ref, low, landed, send_sem, recv_sem):
    me = lax.axis_index("tensor")
    low[...] = parts_ref[...].astype(BF16)
    tensor_barrier(count)
    copies = []
    for shift in range(1, count):
        to = lax.rem(me + shift, count)
        copies.append(
            pltpu.make_async_remote_copy(
                src_ref=low.at[to],
                dst_ref=landed.at[shift],
                send_sem=send_sem.at[shift],
                recv_sem=recv_sem.at[shift],
                device_id={"tensor": to},
                device_id_type=MESH,
            )
        )
        copies[-1].start()
    total = parts_ref[me]
    for shift, copy in enumerate(copies, 1):
        copy.wait()
        total = total + landed[shift].astype(F32)
    out_ref[...] = total


def merge_call(parts):
    count = parts.shape[0]
    vmem = pl.BlockSpec(memory_space=pltpu.VMEM)
    return pl.pallas_call(
        functools.partial(merge_kernel, count),
        in_specs=[vmem],
        out_specs=vmem,
        out_shape=jax.ShapeDtypeStruct(parts.shape[1:], F32),
        scratch_shapes=[
            pltpu.VMEM(parts.shape, BF16),
            pltpu.VMEM(parts.shape, BF16),
            pltpu.SemaphoreType.DMA((count,)),
            pltpu.SemaphoreType.DMA((count,)),
        ],
        compiler_params=pltpu.CompilerParams(collective_id=2, has_side_effects=True),
    )(parts)


class Place:
    def __init__(self):
        dp, tensor = lax.axis_index("dp"), lax.axis_index("tensor")
        self.z, self.x = dp // 2, lax.rem(dp, 2)
        self.y, self.core = tensor // 2, lax.rem(tensor, 2)

    def at(self, z=None, x=None, y=None, core=None):
        z = self.z if z is None else z
        x = self.x if x is None else x
        y = self.y if y is None else y
        core = self.core if core is None else core
        return (z * 2 + x, y * 2 + core)

    def peers(self):
        near = [self.at(x=1 - self.x), self.at(y=1 - self.y), self.at(core=1 - self.core)]
        return near + [self.at(z=lax.rem(self.z + d, 4)) for d in (1, 2, 3)]

    def greet(self):
        barrier = pltpu.get_barrier_semaphore()
        for peer in self.peers():
            pl.semaphore_signal(barrier, inc=1, device_id=peer, device_id_type=MESH)
        pl.semaphore_wait(barrier, 6)


def push(src, dst, send, recv, to):
    copy = pltpu.make_async_remote_copy(
        src_ref=src, dst_ref=dst, send_sem=send, recv_sem=recv, device_id=to, device_id_type=MESH
    )
    copy.start()
    return copy


def gather_kernel(packs, *refs):
    sources, small = refs[:packs], refs[packs]
    outs, small_out = refs[packs + 1 : 2 * packs + 1], refs[2 * packs + 1]
    own_sem, send, recv, small_send, small_recv = refs[2 * packs + 2 :]
    me = Place()
    tensor = me.y * 2 + me.core
    other = (1 - me.y) * 2 + me.core
    ahead = [lax.rem(me.z + 4 - d, 4) for d in range(4)]
    to_x, to_y, to_core = me.at(x=1 - me.x), me.at(y=1 - me.y), me.at(core=1 - me.core)
    half = sources[0].shape[0] // 2
    me.greet()

    small_copies = [
        push(
            small, small_out.at[me.x, me.z], small_send.at[d], small_recv.at[d],
            me.at(z=lax.rem(me.z + d, 4)),
        )
        for d in (1, 2, 3)
    ]
    own = [pltpu.make_async_copy(small, small_out.at[me.x, me.z], own_sem.at[packs])]
    own[0].start()
    along = []
    for k in range(packs):
        copy = pltpu.make_async_copy(sources[k], outs[k].at[tensor, me.z, me.x], own_sem.at[k])
        copy.start()
        own.append(copy)
        along.append(
            [
                push(
                    sources[k], outs[k].at[tensor, me.z, me.x], send.at[k, d - 1],
                    recv.at[k, d - 1], me.at(z=lax.rem(me.z + d, 4)),
                )
                for d in (1, 2, 3)
            ]
        )
    for copy in own:
        copy.wait()
    done = []
    for copy in small_copies:
        copy.wait_recv()
    done += small_copies
    last = push(
        small_out.at[me.x], small_out.at[me.x], small_send.at[0], small_recv.at[0], to_x
    )
    for k in range(packs):
        out = outs[k]
        x_copies, y_copies, core_copies = [], [], []
        for d in range(4):
            z = ahead[d]
            if d > 0:
                along[k][d - 1].wait_recv()
            block = out.at[tensor, z, me.x]
            x_copies.append(push(block, block, send.at[k, 3 + d], recv.at[k, 3 + d], to_x))
            y_copies.append(push(block, block, send.at[k, 7 + d], recv.at[k, 7 + d], to_y))
            core_copies.append(push(block, block, send.at[k, 11 + d], recv.at[k, 11 + d], to_core))
        cross = []
        for d in range(4):
            z = ahead[d]
            x_copies[d].wait_recv()
            from_x = out.at[tensor, z, 1 - me.x]
            top = out.at[tensor, z, 1 - me.x, pl.ds(0, half)]
            cross.append(push(top, top, send.at[k, 15 + d], recv.at[k, 15 + d], to_y))
            core_copies.append(
                push(from_x, from_x, send.at[k, 19 + d], recv.at[k, 19 + d], to_core)
            )
            y_copies[d].wait_recv()
            from_y = out.at[other, z, me.x]
            low = out.at[other, z, me.x, pl.ds(half, half)]
            cross.append(push(low, low, send.at[k, 23 + d], recv.at[k, 23 + d], to_x))
            core_copies.append(
                push(from_y, from_y, send.at[k, 27 + d], recv.at[k, 27 + d], to_core)
            )
        for d in range(4):
            z = ahead[d]
            cross[2 * d].wait_recv()
            cross[2 * d + 1].wait_recv()
            block = out.at[other, z, 1 - me.x]
            core_copies.append(push(block, block, send.at[k, 31 + d], recv.at[k, 31 + d], to_core))
        for copy in core_copies:
            copy.wait_recv()
        done += along[k] + x_copies + y_copies + cross + core_copies
    last.wait_recv()
    done.append(last)
    for copy in done:
        copy.wait_send()


def gather_call(packs, small):
    count = len(packs)
    anywhere = pl.BlockSpec(memory_space=pl.ANY)
    outs = pl.pallas_call(
        functools.partial(gather_kernel, count),
        in_specs=[anywhere] * (count + 1),
        out_specs=[anywhere] * (count + 1),
        out_shape=[jax.ShapeDtypeStruct((4, 4, 2) + pack.shape, pack.dtype) for pack in packs]
        + [jax.ShapeDtypeStruct((2, 4) + small.shape, small.dtype)],
        scratch_shapes=[
            pltpu.SemaphoreType.DMA((count + 1,)),
            pltpu.SemaphoreType.DMA((count, 35)),
            pltpu.SemaphoreType.DMA((count, 35)),
            pltpu.SemaphoreType.DMA((4,)),
            pltpu.SemaphoreType.DMA((4,)),
        ],
        compiler_params=pltpu.CompilerParams(collective_id=3, has_side_effects=True),
    )(*packs, small)
    return outs[:count], jnp.swapaxes(outs[count], 0, 1)


def scatter_kernel(parts_ref, out_ref, total, from_core, from_x, from_y, turn_x, turn_y, from_z, send, recv):
    me = Place()
    half = parts_ref.shape[3] // 2
    to_x, to_y, to_core = me.at(x=1 - me.x), me.at(y=1 - me.y), me.at(core=1 - me.core)
    top, low = pl.ds(0, half), pl.ds(half, half)
    order = [lax.rem(me.z + d, 4) for d in (1, 2, 3, 0)]
    me.greet()
    core_copies, x_copies, y_copies, x_turns, y_turns, z_copies = [], [], [], [], [], []
    for d, z in enumerate(order):
        for y in range(2):
            core_copies.append(
                push(
                    parts_ref.at[2 * y + 1 - me.core, z], from_core.at[y, z],
                    send.at[2 * d + y], recv.at[2 * d + y], to_core,
                )
            )
    for d, z in enumerate(order):
        for y in range(2):
            core_copies[2 * d + y].wait_recv()
            for x in range(2):
                total[z, x, y] = parts_ref[2 * y + me.core, z, x] + from_core[y, z, x]
        x_copies.append(
            push(
                total.at[z, 1 - me.x, :, top], from_x.at[z], send.at[8 + d], recv.at[8 + d], to_x
            )
        )
        y_copies.append(
            push(
                total.at[z, :, 1 - me.y, low], from_y.at[z], send.at[12 + d], recv.at[12 + d], to_y
            )
        )
    for d, z in enumerate(order):
        x_copies[d].wait_recv()
        for y in range(2):
            total[z, me.x, y, top] += from_x[z, y]
        y_turns.append(
            push(
                total.at[z, me.x, 1 - me.y, top], turn_y.at[z],
                send.at[16 + d], recv.at[16 + d], to_y,
            )
        )
        y_copies[d].wait_recv()
        for x in range(2):
            total[z, x, me.y, low] += from_y[z, x]
        x_turns.append(
            push(
                total.at[z, 1 - me.x, me.y, low], turn_x.at[z],
                send.at[20 + d], recv.at[20 + d], to_x,
            )
        )
    for d, z in enumerate(order):
        y_turns[d].wait_recv()
        total[z, me.x, me.y, top] += turn_y[z]
        x_turns[d].wait_recv()
        total[z, me.x, me.y, low] += turn_x[z]
        if d < 3:
            z_copies.append(
                push(
                    total.at[z, me.x, me.y], from_z.at[d],
                    send.at[24 + d], recv.at[24 + d], me.at(z=z),
                )
            )
    result = total[me.z, me.x, me.y].astype(F32)
    for d, copy in enumerate(z_copies):
        copy.wait_recv()
        result = result + from_z[d].astype(F32)
    out_ref[...] = result
    for copy in core_copies + x_copies + y_copies + x_turns + y_turns + z_copies:
        copy.wait_send()


def scatter_call(parts, ident):
    tens, width, cols = parts.shape
    rows = width // 8
    half = rows // 2
    parts = parts.reshape(tens, 4, 2, rows, cols)
    vmem = pl.BlockSpec(memory_space=pltpu.VMEM)
    return pl.pallas_call(
        scatter_kernel,
        in_specs=[vmem],
        out_specs=vmem,
        out_shape=jax.ShapeDtypeStruct((rows, cols), F32),
        scratch_shapes=[
            pltpu.VMEM((4, 2, 2, rows, cols), BF16),
            pltpu.VMEM((2, 4, 2, rows, cols), BF16),
            pltpu.VMEM((4, 2, half, cols), BF16),
            pltpu.VMEM((4, 2, half, cols), BF16),
            pltpu.VMEM((4, half, cols), BF16),
            pltpu.VMEM((4, half, cols), BF16),
            pltpu.VMEM((3, rows, cols), BF16),
            pltpu.SemaphoreType.DMA((27,)),
            pltpu.SemaphoreType.DMA((27,)),
        ],
        compiler_params=pltpu.CompilerParams(
            collective_id=ident, has_side_effects=True, vmem_limit_bytes=56 * MIB
        ),
    )(parts)


def angles(places):
    steps = jnp.arange(HALF).astype(F32)
    inverse = jnp.exp(steps * (-2.0 * math.log(10000.0) / ROT))
    phase = (0.25 * inverse)[:, None] * places.astype(F32)[None, :]
    return jnp.concatenate([jnp.cos(phase), jnp.sin(phase)], axis=0)


def param_squares(arrays, leader):
    query, keyval, output, upward, downward, norms = arrays
    return jnp.concatenate(
        [
            jnp.sum(query * query, axis=(1, 2)),
            (jnp.sum(keyval * keyval) * leader)[None],
            jnp.sum(output * output, axis=(1, 2)),
            jnp.sum(upward * upward, axis=(1, 2)),
            jnp.sum(downward * downward, axis=(1, 2)),
            jnp.sum(norms * norms, axis=2).reshape(8) * leader,
        ]
    )


def lamb_parts(weight, first, second, grad):
    first_new = BETA_FIRST * first + (1.0 - BETA_FIRST) * grad
    second_new = BETA_SECOND * second + (1.0 - BETA_SECOND) * grad * grad
    update = (
        first_new
        / (1.0 - BETA_FIRST**STEP)
        / (jnp.sqrt(second_new / (1.0 - BETA_SECOND**STEP)) + ADAM_EPSILON)
        + WEIGHT_DECAY * weight
    )
    return (first_new, second_new, update)


def apply_trust(masters, updates, trust):
    factors = (
        trust[0:2][:, None, None],
        trust[2],
        trust[3:5][:, None, None],
        trust[5:7][:, None, None],
        trust[7:9][:, None, None],
        trust[9:17].reshape(2, 4, 1),
    )
    return tuple(
        (
            weight - LEARN_RATE * factor * update
            for weight, factor, update in zip(masters, factors, updates)
        )
    )


def shards(
    fast,
    hidden_in,
    out_grad,
    positions,
    query_weight,
    keyval_weight,
    output_weight,
    up_weight,
    down_weight,
    norm_params,
    query_first,
    query_second,
    keyval_first,
    keyval_second,
    output_first,
    output_second,
    up_first,
    up_second,
    down_first,
    down_second,
    norm_first,
    norm_second,
):
    masters = (query_weight, keyval_weight, output_weight, up_weight, down_weight, norm_params)
    tensor = lax.axis_index("tensor")
    leader = (tensor == 0).astype(F32)
    rows, width = hidden_in.shape
    tens = positions.shape[0] // rows
    depth = keyval_weight.shape[0]

    packs = []
    for layer in range(2):
        if layer == 0:
            keys, values = keyval_weight[:, :HD], keyval_weight[:, HD:]
        else:
            keys = values = jnp.zeros((depth, HD), F32)
        packs.append(
            jnp.concatenate(
                [
                    up_weight[layer],
                    down_weight[layer].T,
                    query_weight[layer],
                    keys,
                    output_weight[layer].T,
                    values,
                ],
                axis=1,
            ).astype(BF16)
        )
    norm_low = norm_params.astype(BF16).reshape(8, depth)
    if fast:
        norm_pack = jnp.pad(norm_low, ((0, 8), (0, 128 - depth)))
        weights, norm_all = gather_call(packs, norm_pack)
        weights = [w.reshape(tens, width, w.shape[-1]) for w in weights]
        norm_full = norm_all[:, :, :8, :depth].reshape(-1, 8, depth)
    else:
        weights = [
            lax.all_gather(pack, ("tensor", "dp"), axis=0).reshape(tens, width, pack.shape[1])
            for pack in packs
        ]
        norm_full = lax.all_gather(norm_low, "dp", axis=0)
    norm_full = jnp.swapaxes(norm_full, 0, 1).reshape(2, 4, width).astype(F32)
    trig = angles(lax.dynamic_slice_in_dim(positions, tensor * rows, rows, 0))

    current = hidden_in
    saved = []
    kv = None
    for layer in range(2):
        norms = norm_full[layer]
        if layer == 0:
            qt, kv_here = qkv_call(True, current, norms, trig, weights[layer])
            kv = share_call(kv_here, tens).reshape(-1, 2 * HD)
        else:
            (qt,) = qkv_call(False, current, norms, trig, weights[layer])
        at, lse = attend_call(qt, kv)
        after, act, slope = mix_call(current, norms, at, weights[layer])
        saved.append((current, qt, at, lse, act, slope))
        current = after

    grad = out_grad
    dkv = None
    early, late, sums = [None, None], [None, None], [None, None]
    for layer in (1, 0):
        norms = norm_full[layer]
        x, qt, at, lse, act, slope = saved[layer]
        early[layer], dout, mlp = mix_back_call(grad, x, norms, at, act, slope, weights[layer])
        gqt, dkv = attend_back_call(qt, dout, at, lse, kv, trig, dkv)
        if layer == 0:
            dkv = merge_call(dkv)
        grad, late[layer], sums[layer] = norm_back_call(
            layer == 0, grad, x, norms, mlp, gqt, weights[layer],
            dkv if layer == 0 else None, trig if layer == 0 else None,
        )
    sums_t = jnp.concatenate(sums, axis=0).T.astype(BF16)
    late[0] = lax.dynamic_update_slice(
        late[0], jnp.broadcast_to(sums_t[None], (tens,) + sums_t.shape), (0, 0, 256 + HD)
    )

    def scatter(parts, ident):
        if fast:
            return scatter_call(parts, ident)
        pieces = parts.reshape(-1, depth, parts.shape[-1])
        return lax.psum_scatter(
            pieces, ("tensor", "dp"), scatter_dimension=0, tiled=False
        ).astype(F32)

    early = [scatter(early[layer], 4) for layer in range(2)]
    late = [scatter(late[layer], 5 + layer) for layer in range(2)]
    hidden = up_weight.shape[2]
    query_g = jnp.stack([late[layer][:, :QW] for layer in range(2)])
    keyval_g = late[0][:, QW : QW + 2 * HD]
    output_g = jnp.stack([early[layer][:, 2 * hidden : 2 * hidden + QW].T for layer in range(2)])
    up_g = jnp.stack([early[layer][:, :hidden] for layer in range(2)])
    down_g = jnp.stack([early[layer][:, hidden : 2 * hidden].T for layer in range(2)])
    norm_g = late[0][:, QW + 2 * HD : QW + 2 * HD + 8].T.reshape(2, 4, depth)

    grads = (query_g, keyval_g, output_g, up_g, down_g, norm_g)
    firsts = (query_first, keyval_first, output_first, up_first, down_first, norm_first)
    seconds = (query_second, keyval_second, output_second, up_second, down_second, norm_second)
    parts = [
        lamb_parts(weight, first, second, grad)
        for weight, first, second, grad in zip(masters, firsts, seconds, grads)
    ]
    updates = tuple((part[2] for part in parts))
    weight_total, update_total = lax.psum(
        (param_squares(masters, leader), param_squares(updates, leader)), ("dp", "tensor")
    )
    weight_norm = jnp.sqrt(weight_total)
    update_norms = jnp.sqrt(update_total)
    trust_ratios = weight_norm / update_norms
    nexts = apply_trust(masters, updates, trust_ratios)
    outs = [current, grad]
    for index in range(6):
        low = nexts[index].astype(BF16)
        outs += [parts[index][0], parts[index][1], nexts[index], low]
    return tuple(outs) + (update_norms, trust_ratios)


def solution(mesh):
    fast = mesh.shape["dp"] == 8 and mesh.shape["tensor"] == 4
    columns = P(None, "dp", "tensor")
    across = P(None, "tensor", "dp")
    flat = P("dp", None)
    norm = P(None, None, "dp")
    state = P(("dp", "tensor"), None)
    in_specs = (
        (state, state, P("dp"), columns, flat, across, columns, across, norm)
        + (columns, columns, flat, flat, across, across, columns, columns, across, across)
        + (norm, norm)
    )
    out_specs = (
        (state, state)
        + (columns,) * 4
        + (flat,) * 4
        + (across,) * 4
        + (columns,) * 4
        + (across,) * 4
        + (norm,) * 4
        + (P(), P())
    )
    return jax.shard_map(
        functools.partial(shards, fast),
        mesh=mesh,
        in_specs=in_specs,
        out_specs=out_specs,
        check_vma=False,
    )
```

```python
import functools
import math

import jax
import jax.numpy as jnp
from jax import lax
from jax.experimental import pallas as pl
from jax.experimental.pallas import tpu as pltpu
from jax.sharding import PartitionSpec as P

F32 = jnp.float32
BF16 = jnp.bfloat16
MESH = pl.DeviceIdType.MESH

HD = 64
ROT = 16
HALF = ROT // 2
STEP = 5
HEADS_HERE = 3
QW = 192

NORM_EPSILON = 1e-05
BETA_FIRST = 0.5
BETA_SECOND = 0.55
ADAM_EPSILON = 1e-06
WEIGHT_DECAY = 0.01
LEARN_RATE = 0.5
SCALE = HD**-0.5
ROOM = 60 * 2**20


def dot(a, b):
    return jnp.dot(a, b, preferred_element_type=F32)


def dot_nt(a, b):
    return lax.dot_general(a, b, (((1,), (1,)), ((), ())), preferred_element_type=F32)


def turn(a):
    return jnp.transpose(a.astype(F32), (1, 0))


def standard(values):
    center = values - jnp.mean(values, axis=-1, keepdims=True)
    spread = jnp.mean(center * center, axis=-1, keepdims=True)
    inverse = lax.rsqrt(spread + NORM_EPSILON)
    return center * inverse, inverse


def gelu_parts(v):
    x = jnp.abs(v) * (2.0**-0.5)
    bell = jnp.exp(-x * x)
    t = 1.0 / (1.0 + 0.3275911 * x)
    series = t * (
        0.254829592
        + t * (-0.284496736 + t * (1.421413741 + t * (-1.453152027 + t * 1.061405429)))
    )
    tail = 0.5 * series * bell
    cumulative = jnp.where(v < 0.0, tail, 1.0 - tail)
    return cumulative, bell * (1.0 / math.sqrt(2.0 * math.pi))


class Place:
    def __init__(self):
        dp, tensor = lax.axis_index("dp"), lax.axis_index("tensor")
        self.z, self.x = lax.div(dp, 2), lax.rem(dp, 2)
        self.y, self.core = lax.div(tensor, 2), lax.rem(tensor, 2)
        self.tensor = tensor
        self.to_x = self.at(x=1 - self.x)
        self.to_y = self.at(y=1 - self.y)
        self.to_core = self.at(core=1 - self.core)
        self.to_corner = self.at(y=1 - self.y, core=1 - self.core)

    def at(self, z=None, x=None, y=None, core=None):
        z = self.z if z is None else z
        x = self.x if x is None else x
        y = self.y if y is None else y
        core = self.core if core is None else core
        return (z * 2 + x, y * 2 + core)

    def along(self, shift):
        return lax.rem(self.z + shift, 4)

    def near(self):
        return [
            (
                code,
                self.at(
                    x=lax.rem(self.x + code // 4, 2),
                    y=lax.rem(self.y + code // 2 % 2, 2),
                    core=lax.rem(self.core + code % 2, 2),
                ),
            )
            for code in range(1, 8)
        ]

    def greet(self, corner=False, near=False):
        peers = [self.at(z=self.along(shift)) for shift in (1, 2, 3)]
        if near:
            peers += [peer for _, peer in self.near()]
        else:
            peers += [self.to_x, self.to_y, self.to_core]
        if corner:
            peers.append(self.to_corner)
        barrier = pltpu.get_barrier_semaphore()
        for peer in peers:
            pl.semaphore_signal(barrier, inc=1, device_id=peer, device_id_type=MESH)
        pl.semaphore_wait(barrier, len(peers))


def remote(src, dst, send, recv, to):
    return pltpu.make_async_remote_copy(
        src_ref=src, dst_ref=dst, send_sem=send, recv_sem=recv, device_id=to, device_id_type=MESH
    )


def spread(steps, index, count):
    for place, step in enumerate(steps):
        pl.when(index == lax.div(place * count, len(steps)))(step)


class Gather:
    COUNT = 35

    @staticmethod
    def scratch(packs):
        return [
            pltpu.SemaphoreType.DMA((packs,)),
            pltpu.SemaphoreType.DMA((packs, Gather.COUNT)),
            pltpu.SemaphoreType.DMA((packs, Gather.COUNT)),
        ]

    @staticmethod
    def shapes(packs):
        return [jax.ShapeDtypeStruct((4, 4, 2) + pack.shape, pack.dtype) for pack in packs]

    def __init__(self, me, sources, outs, own_sem, send, recv):
        self.packs = [
            self.pack(me, source, out, own_sem.at[k], send.at[k], recv.at[k])
            for k, (source, out) in enumerate(zip(sources, outs))
        ]

    def pack(self, me, source, out, own_sem, send, recv):
        half = source.shape[0] // 2
        top, low = pl.ds(0, half), pl.ds(half, half)
        other = (1 - me.y) * 2 + me.core
        mine = out.at[me.tensor, me.z, me.x]

        def copy(slot, src, dst, to):
            return remote(src, dst, send.at[slot], recv.at[slot], to)

        parts = {"own": pltpu.make_async_copy(source, mine, own_sem)}
        for d in range(4):
            z = me.along(4 - d)
            block = out.at[me.tensor, z, me.x]
            origin = source if d == 0 else block
            if d > 0:
                parts["z", d] = copy(d - 1, source, mine, me.at(z=me.along(d)))
            parts["x", d] = copy(3 + d, origin, block, me.to_x)
            parts["y", d] = copy(7 + d, origin, block, me.to_y)
            parts["core", d] = copy(11 + d, origin, block, me.to_core)
            from_x, from_y = out.at[me.tensor, z, 1 - me.x], out.at[other, z, me.x]
            parts["xy", d] = copy(15 + d, from_x.at[top], from_x.at[top], me.to_y)
            parts["yx", d] = copy(19 + d, from_y.at[low], from_y.at[low], me.to_x)
            parts["core x", d] = copy(23 + d, from_x, from_x, me.to_core)
            parts["core y", d] = copy(27 + d, from_y, from_y, me.to_core)
            far = out.at[other, z, 1 - me.x]
            parts["core far", d] = copy(31 + d, far, far, me.to_core)
        return parts

    def begin(self):
        for parts in self.packs:
            for key in (("z", 1), ("x", 0), ("y", 0), ("core", 0), "own"):
                parts[key].start()

    def pass_on(self, d, following):
        for parts in self.packs:
            parts["z", d].wait()
            if following:
                parts["z", following].start()
            for way in ("x", "y", "core"):
                parts[way, d].start()

    def cross(self, d):
        for parts in self.packs:
            parts["x", d].wait_recv()
            parts["xy", d].start()
            parts["core x", d].start()
            parts["y", d].wait_recv()
            parts["yx", d].start()
            parts["core y", d].start()

    def far(self, d):
        for parts in self.packs:
            parts["xy", d].wait_recv()
            parts["yx", d].wait_recv()
            parts["core far", d].start()

    def end(self):
        for parts in self.packs:
            parts["own"].wait()
            for key, copy in parts.items():
                if key != "own" and key[0].startswith("core"):
                    copy.wait_recv()
            for key, copy in parts.items():
                if key != "own" and key[0] != "z":
                    copy.wait_send()

    def steps(self):
        return [
            functools.partial(self.pass_on, 1, 3),
            functools.partial(self.cross, 0),
            functools.partial(self.pass_on, 3, 2),
            functools.partial(self.cross, 1),
            functools.partial(self.far, 0),
            functools.partial(self.pass_on, 2, None),
            functools.partial(self.cross, 3),
            functools.partial(self.far, 1),
            functools.partial(self.cross, 2),
            functools.partial(self.far, 3),
            functools.partial(self.far, 2),
        ]


class Scatter:
    COUNT = 27

    @staticmethod
    def scratch(rows, cols):
        half = rows // 2
        return [
            pltpu.VMEM((4, 2, 2, rows, cols), BF16),
            pltpu.VMEM((2, 4, 2, rows, cols), BF16),
            pltpu.VMEM((4, 2, half, cols), BF16),
            pltpu.VMEM((4, 2, half, cols), BF16),
            pltpu.VMEM((4, half, cols), BF16),
            pltpu.VMEM((4, half, cols), BF16),
            pltpu.VMEM((3, rows, cols), BF16),
            pltpu.SemaphoreType.DMA((8,)),
            pltpu.SemaphoreType.DMA((Scatter.COUNT,)),
            pltpu.SemaphoreType.DMA((Scatter.COUNT,)),
        ]

    def __init__(
        self, me, source, out, total, from_core, from_x, from_y, turn_x, turn_y, from_z,
        load_sem, send, recv,
    ):
        self.me, self.out, self.total = me, out, total
        self.from_core, self.from_x, self.from_y = from_core, from_x, from_y
        self.turn_x, self.turn_y, self.from_z = turn_x, turn_y, from_z
        half = total.shape[3] // 2
        self.top, self.low = pl.ds(0, half), pl.ds(half, half)
        self.order = [me.along(d) for d in (2, 3, 1, 0)]
        self.parts = parts = {}

        def copy(slot, src, dst, to):
            return remote(src, dst, send.at[slot], recv.at[slot], to)

        for d, z in enumerate(self.order):
            for y in range(2):
                parts["load", d, y] = pltpu.make_async_copy(
                    source.at[2 * y + me.core, z], total.at[z, :, y], load_sem.at[2 * d + y]
                )
                parts["core", d, y] = copy(
                    2 * d + y, source.at[2 * y + 1 - me.core, z], from_core.at[y, z], me.to_core
                )
            parts["x", d] = copy(
                8 + d, total.at[z, 1 - me.x, :, self.top], from_x.at[z], me.to_x
            )
            parts["y", d] = copy(
                12 + d, total.at[z, :, 1 - me.y, self.low], from_y.at[z], me.to_y
            )
            parts["xy", d] = copy(
                16 + d, total.at[z, me.x, 1 - me.y, self.top], turn_y.at[z], me.to_y
            )
            parts["yx", d] = copy(
                20 + d, total.at[z, 1 - me.x, me.y, self.low], turn_x.at[z], me.to_x
            )
            if d < 3:
                parts["z", d] = copy(24 + d, total.at[z, me.x, me.y], from_z.at[d], me.at(z=z))

    def load(self, d):
        for y in range(2):
            self.parts["core", d, y].start()
            self.parts["load", d, y].start()

    def launch(self, d):
        self.parts["x", d].start()
        self.parts["y", d].start()

    def begin(self):
        self.load(0)
        self.load(1)

    def core(self, d):
        z = self.order[d]
        for y in range(2):
            self.parts["load", d, y].wait()
            self.parts["core", d, y].wait_recv()
            for x in range(2):
                self.total[z, x, y] += self.from_core[y, z, x]
        if d == 0:
            self.launch(0)
        if d < 2:
            self.load(d + 2)

    def cross(self, d):
        me, z = self.me, self.order[d]
        self.parts["x", d].wait_recv()
        self.parts["y", d].wait_recv()
        if d < 3:
            self.launch(d + 1)
        for y in range(2):
            self.total[z, me.x, y, self.top] += self.from_x[z, y]
        self.parts["xy", d].start()
        for x in range(2):
            self.total[z, x, me.y, self.low] += self.from_y[z, x]
        self.parts["yx", d].start()

    def far(self, d):
        me, z = self.me, self.order[d]
        self.parts["xy", d].wait_recv()
        self.total[z, me.x, me.y, self.top] += self.turn_y[z]
        self.parts["yx", d].wait_recv()
        self.total[z, me.x, me.y, self.low] += self.turn_x[z]
        if d < 3:
            self.parts["z", d].start()

    def end(self):
        me = self.me
        result = self.total[me.z, me.x, me.y].astype(F32)
        for d in range(3):
            self.parts["z", d].wait_recv()
            result = result + self.from_z[d].astype(F32)
        self.out[...] = result
        for key, copy in self.parts.items():
            if key[0] != "load":
                copy.wait_send()

    def steps(self):
        order = [
            (self.core, 0), (self.core, 1), (self.cross, 0), (self.core, 2), (self.cross, 1),
            (self.far, 0), (self.core, 3), (self.cross, 2), (self.far, 1), (self.cross, 3),
            (self.far, 2), (self.far, 3),
        ]
        return [functools.partial(step, d) for step, d in order]


def gather_kernel(packs, *refs):
    sources, small = refs[:packs], refs[packs]
    outs, small_out = refs[packs + 1 : 2 * packs + 1], refs[2 * packs + 1]
    sems, (small_own, small_send, small_recv) = refs[2 * packs + 2 : -3], refs[-3:]
    me = Place()
    gather = Gather(me, sources, outs, *sems)
    mine = small_out.at[me.x, me.z]
    own = pltpu.make_async_copy(small, mine, small_own)
    along = [
        remote(small, mine, small_send.at[d], small_recv.at[d], me.at(z=me.along(d)))
        for d in (1, 2, 3)
    ]
    row = small_out.at[me.x]
    across = remote(row, row, small_send.at[0], small_recv.at[0], me.to_x)
    me.greet()
    for copy in along + [own]:
        copy.start()
    gather.begin()
    own.wait()
    for copy in along:
        copy.wait_recv()
    across.start()
    for step in gather.steps():
        step()
    across.wait_recv()
    gather.end()
    for copy in along + [across]:
        copy.wait_send()


def gather_call(packs, small):
    count = len(packs)
    anywhere = pl.BlockSpec(memory_space=pl.ANY)
    outs = pl.pallas_call(
        functools.partial(gather_kernel, count),
        in_specs=[anywhere] * (count + 1),
        out_specs=[anywhere] * (count + 1),
        out_shape=Gather.shapes(packs)
        + [jax.ShapeDtypeStruct((2, 4) + small.shape, small.dtype)],
        scratch_shapes=Gather.scratch(count)
        + [
            pltpu.SemaphoreType.DMA,
            pltpu.SemaphoreType.DMA((4,)),
            pltpu.SemaphoreType.DMA((4,)),
        ],
        compiler_params=pltpu.CompilerParams(
            collective_id=3, has_side_effects=True, vmem_limit_bytes=ROOM
        ),
    )(*packs, small)
    return outs[:count], jnp.swapaxes(outs[count], 0, 1)


def tensor_barrier(count):
    me = lax.axis_index("tensor")
    barrier = pltpu.get_barrier_semaphore()
    for shift in range(1, count):
        pl.semaphore_signal(
            barrier, inc=1, device_id={"tensor": lax.rem(me + shift, count)}, device_id_type=MESH
        )
    pl.semaphore_wait(barrier, count - 1)


def share_kernel(count, mine_ref, out_ref, here_sem, send_sem, recv_sem):
    me = lax.axis_index("tensor")
    tensor_barrier(count)
    copies = []
    for shift in range(1, count):
        copies.append(
            pltpu.make_async_remote_copy(
                src_ref=mine_ref,
                dst_ref=out_ref.at[me],
                send_sem=send_sem.at[shift],
                recv_sem=recv_sem.at[shift],
                device_id={"tensor": lax.rem(me + shift, count)},
                device_id_type=MESH,
            )
        )
        copies[-1].start()
    own = pltpu.make_async_copy(mine_ref, out_ref.at[me], here_sem)
    own.start()
    own.wait()
    for copy in copies:
        copy.wait()


def share_call(mine, count):
    return pl.pallas_call(
        functools.partial(share_kernel, count),
        in_specs=[pl.BlockSpec(memory_space=pltpu.VMEM)],
        out_specs=pl.BlockSpec(memory_space=pltpu.VMEM),
        out_shape=jax.ShapeDtypeStruct((count,) + mine.shape, mine.dtype),
        scratch_shapes=[
            pltpu.SemaphoreType.DMA,
            pltpu.SemaphoreType.DMA((count,)),
            pltpu.SemaphoreType.DMA((count,)),
        ],
        compiler_params=pltpu.CompilerParams(collective_id=9, has_side_effects=True),
    )(mine)


def merge_kernel(count, parts_ref, out_ref, low, landed, send_sem, recv_sem):
    me = lax.axis_index("tensor")
    low[...] = parts_ref[...].astype(BF16)
    tensor_barrier(count)
    copies = []
    for shift in range(1, count):
        to = lax.rem(me + shift, count)
        copies.append(
            pltpu.make_async_remote_copy(
                src_ref=low.at[to],
                dst_ref=landed.at[shift],
                send_sem=send_sem.at[shift],
                recv_sem=recv_sem.at[shift],
                device_id={"tensor": to},
                device_id_type=MESH,
            )
        )
        copies[-1].start()
    total = parts_ref[me]
    for shift, copy in enumerate(copies, 1):
        copy.wait()
        total = total + landed[shift].astype(F32)
    out_ref[...] = total


def merge_call(parts):
    count = parts.shape[0]
    vmem = pl.BlockSpec(memory_space=pltpu.VMEM)
    return pl.pallas_call(
        functools.partial(merge_kernel, count),
        in_specs=[vmem],
        out_specs=vmem,
        out_shape=jax.ShapeDtypeStruct(parts.shape[1:], F32),
        scratch_shapes=[
            pltpu.VMEM(parts.shape, BF16),
            pltpu.VMEM(parts.shape, BF16),
            pltpu.SemaphoreType.DMA((count,)),
            pltpu.SemaphoreType.DMA((count,)),
        ],
        compiler_params=pltpu.CompilerParams(collective_id=10, has_side_effects=True),
    )(parts)


def blocks_of(parts):
    tens, width, cols = parts.shape
    return parts.reshape(tens, 4, 2, width // 8, cols)


def rotated(low, cos, sin):
    first, second = low[:HALF], low[HALF:ROT]
    return jnp.concatenate([first * cos - second * sin, second * cos + first * sin], axis=0)


def qkv_kernel(first, x_ref, norm_ref, trig_ref, qk_ref, *rest):
    if first:
        ov_ref, qt_ref, kv_ref, normed = rest
    else:
        qt_ref, normed = rest
    t = pl.program_id(0)

    @pl.when(t == 0)
    def _():
        x = x_ref[...].astype(F32)
        normed[...] = (standard(x)[0] * norm_ref[0:1] + norm_ref[1:2]).astype(BF16)

    cos, sin = trig_ref[0:HALF], trig_ref[HALF:ROT]
    lin = turn(dot(normed[...], qk_ref[0]))
    for head in range(HEADS_HERE):
        base = head * HD
        low = rotated(lin[base : base + ROT], cos, sin)
        qt_ref[0, base : base + ROT] = (low.astype(BF16).astype(F32) * SCALE).astype(BF16)
        qt_ref[0, base + ROT : base + HD] = (
            lin[base + ROT : base + HD].astype(BF16).astype(F32) * SCALE
        ).astype(BF16)
    qt_ref[0, QW:] = jnp.zeros_like(qt_ref[0, QW:])
    if first:

        @pl.when(t == 0)
        def _():
            value = turn(dot(normed[...], ov_ref[0]))[QW:]
            key = jnp.concatenate(
                [rotated(lin[QW : QW + ROT], cos, sin), lin[QW + ROT :]], axis=0
            )
            kv_ref[...] = turn(jnp.concatenate([key, value], axis=0)).astype(BF16)


def qkv_call(first, x, norms, trig, weights):
    rows, width = x.shape
    tens = weights.shape[0]
    whole = pl.BlockSpec(memory_space=pltpu.VMEM)
    in_specs = [whole, whole, whole, pl.BlockSpec((1, width, 256), lambda t: (t, 0, 0))]
    out_shape = [jax.ShapeDtypeStruct((tens, 256, rows), BF16)]
    out_specs = [pl.BlockSpec((1, 256, rows), lambda t: (t, 0, 0))]
    args = [x, norms, trig, weights]
    if first:
        in_specs.append(pl.BlockSpec((1, width, 256), lambda t: (0, 0, 1)))
        args.append(weights)
        out_shape.append(jax.ShapeDtypeStruct((rows, 2 * HD), BF16))
        out_specs.append(whole)
    return pl.pallas_call(
        functools.partial(qkv_kernel, first),
        grid=(tens,),
        in_specs=in_specs,
        out_specs=out_specs,
        out_shape=out_shape,
        scratch_shapes=[pltpu.VMEM((rows, width), BF16)],
        compiler_params=pltpu.CompilerParams(vmem_limit_bytes=ROOM),
    )(*args)


class Refs:
    def __init__(self, refs):
        self.refs = list(refs)

    def take(self, count):
        taken, self.refs = self.refs[:count], self.refs[count:]
        return taken


def attend_kernel(share, packs, *refs):
    refs = Refs(refs)
    qt_ref, kv_ref = refs.take(2)
    sources = refs.take(packs)
    at_ref, lse_ref = refs.take(2)
    all_ref = refs.take(1)[0] if share else None
    outs = refs.take(packs)
    keys, values_t = refs.take(2)
    steps = []
    if packs:
        me = Place()
        gather = Gather(me, sources, outs, *refs.take(3))
        steps = gather.steps()
    t = pl.program_id(0)
    tens = pl.num_programs(0)
    rows = qt_ref.shape[2]
    place = lax.axis_index("tensor")
    count = tens * (place + 1)
    if share:
        landed, send, recv = refs.take(3)
        peers = (me.to_core, me.to_y, me.to_corner)
        copies = [
            remote(kv_ref, landed.at[place], send.at[k], recv.at[k], peer)
            for k, peer in enumerate(peers)
        ]

    @pl.when(t == 0)
    def _():
        if packs:
            me.greet(corner=share)
        if share:
            for copy in copies:
                copy.start()
        if packs:
            gather.begin()
        if share:
            here = pl.ds(pl.multiple_of(place * rows, rows), rows)
            landed[place] = kv_ref[...]
            keys[here, :] = kv_ref[:, :HD]
            values_t[:, here] = turn(kv_ref[...])[HD:].astype(BF16)
        else:
            keys[...] = kv_ref[:, :HD]
            values_t[...] = turn(kv_ref[...])[HD:].astype(BF16)

    def block(index, carry, diagonal):
        here = pl.ds(pl.multiple_of(index * rows, rows), rows)
        key = keys[here, :]
        value_t = values_t[:, here]
        out = []
        for head in range(HEADS_HERE):
            scores = dot(key, qt_ref[0, head * HD : (head + 1) * HD])
            if diagonal:
                below = lax.broadcasted_iota(jnp.int32, scores.shape, 0)
                across = lax.broadcasted_iota(jnp.int32, scores.shape, 1)
                scores = jnp.where(below <= across, scores, -1e30)
            peak = jnp.max(scores, axis=0, keepdims=True)
            if carry is not None:
                peak = jnp.maximum(peak, carry[head][0])
            weights = jnp.exp(scores - peak)
            total = jnp.sum(weights, axis=0, keepdims=True)
            mixed = dot(value_t, weights.astype(BF16))
            if carry is not None:
                fade = jnp.exp(carry[head][0] - peak)
                total = total + carry[head][1] * fade
                mixed = mixed + carry[head][2] * fade
            out.append((peak, total, mixed))
        return tuple(out)

    spread(steps, t * (place + 1), count)
    carry = block(place, None, True)
    if share:

        @pl.when(t == 0)
        def _():
            for copy in copies:
                copy.wait()
            for part in range(landed.shape[0]):
                here = pl.ds(part * rows, rows)
                keys[here, :] = landed[part, :, :HD]
                values_t[:, here] = turn(landed[part])[HD:].astype(BF16)
            all_ref[...] = landed[...]

    def later(i, carry):
        spread(steps, t * (place + 1) + 1 + i, count)
        return block(i, carry, False)

    carry = lax.fori_loop(0, place, later, carry)
    lse_ref[...] = jnp.zeros_like(lse_ref)
    for head in range(HEADS_HERE):
        peak, total, mixed = carry[head]
        at_ref[0, head * HD : (head + 1) * HD] = (mixed / total).astype(BF16)
        lse_ref[0, head : head + 1] = peak + jnp.log(total)
    at_ref[0, QW:] = jnp.zeros_like(at_ref[0, QW:])
    if packs:
        pl.when(t == tens - 1)(gather.end)


def comm_params(ident):
    if ident is None:
        return pltpu.CompilerParams(vmem_limit_bytes=ROOM)
    return pltpu.CompilerParams(
        collective_id=ident, has_side_effects=True, vmem_limit_bytes=ROOM
    )


def attend_call(qt, kv, length, packs=(), share=False, ident=None):
    tens, _, rows = qt.shape
    whole = pl.BlockSpec(memory_space=pltpu.VMEM)
    anywhere = pl.BlockSpec(memory_space=pl.ANY)
    part = pl.BlockSpec((1, 256, rows), lambda t: (t, 0, 0))
    out_specs = [part, pl.BlockSpec((1, 8, rows), lambda t: (t, 0, 0))]
    out_shape = [
        jax.ShapeDtypeStruct((tens, 256, rows), BF16),
        jax.ShapeDtypeStruct((tens, 8, rows), F32),
    ]
    scratch = [pltpu.VMEM((length, HD), BF16), pltpu.VMEM((HD, length), BF16)]
    if packs:
        scratch += Gather.scratch(len(packs))
    if share:
        out_specs.append(whole)
        out_shape.append(jax.ShapeDtypeStruct((tens,) + kv.shape, BF16))
        scratch += [
            pltpu.VMEM((tens,) + kv.shape, BF16),
            pltpu.SemaphoreType.DMA((3,)),
            pltpu.SemaphoreType.DMA((3,)),
        ]
    out_specs += [anywhere] * len(packs)
    out_shape += Gather.shapes(packs) if packs else []
    return pl.pallas_call(
        functools.partial(attend_kernel, share, len(packs)),
        grid=(tens,),
        in_specs=[part, whole] + [anywhere] * len(packs),
        out_specs=out_specs,
        out_shape=out_shape,
        scratch_shapes=scratch,
        compiler_params=comm_params(ident),
    )(qt, kv, *packs)


def mix_kernel(packs, *refs):
    refs = Refs(refs)
    x_ref, norm_ref, at_ref, o_ref, up_ref, down_ref = refs.take(6)
    sources = refs.take(packs)
    out_ref, act_ref, slope_ref = refs.take(3)
    outs = refs.take(packs)
    normed, total = refs.take(2)
    t = pl.program_id(0)
    tens = pl.num_programs(0)
    steps = []
    if packs:
        me = Place()
        gather = Gather(me, sources, outs, *refs.take(3))
        steps = gather.steps()

    @pl.when(t == 0)
    def _():
        if packs:
            me.greet()
            gather.begin()
        x = x_ref[...].astype(F32)
        normed[...] = (standard(x)[0] * norm_ref[2:3] + norm_ref[3:4]).astype(BF16)
        total[...] = x

    attended = turn(at_ref[0, :QW]).astype(BF16)
    step = 256
    parts = up_ref.shape[2] // step
    for part in range(parts):
        spread(steps, t * (parts + 1) + part, tens * (parts + 1))
        cols = pl.ds(part * step, step)
        pre = dot(normed[...], up_ref[0, :, cols])
        cumulative, bell = gelu_parts(pre)
        act_ref[0, :, cols] = (pre * cumulative).astype(BF16)
        slope_ref[0, :, cols] = (cumulative + pre * bell).astype(BF16)
    spread(steps, t * (parts + 1) + parts, tens * (parts + 1))
    total[...] += dot_nt(attended, o_ref[0, :, :QW]) + dot_nt(act_ref[0], down_ref[0])

    @pl.when(t == tens - 1)
    def _():
        out_ref[...] = total[...]
        if packs:
            gather.end()


def mix_call(x, norms, at, outward, feed, packs=(), ident=None):
    rows, width = x.shape
    tens = feed.shape[0]
    hidden = feed.shape[2] // 2
    whole = pl.BlockSpec(memory_space=pltpu.VMEM)
    anywhere = pl.BlockSpec(memory_space=pl.ANY)
    wide = pl.BlockSpec((1, rows, hidden), lambda t: (t, 0, 0))
    return pl.pallas_call(
        functools.partial(mix_kernel, len(packs)),
        grid=(tens,),
        in_specs=[
            whole,
            whole,
            pl.BlockSpec((1, 256, rows), lambda t: (t, 0, 0)),
            pl.BlockSpec((1, width, 256), lambda t: (t, 0, 1)),
            pl.BlockSpec((1, width, hidden), lambda t: (t, 0, 0)),
            pl.BlockSpec((1, width, hidden), lambda t: (t, 0, 1)),
        ]
        + [anywhere] * len(packs),
        out_specs=[whole, wide, wide] + [anywhere] * len(packs),
        out_shape=[
            jax.ShapeDtypeStruct((rows, width), F32),
            jax.ShapeDtypeStruct((tens, rows, hidden), BF16),
            jax.ShapeDtypeStruct((tens, rows, hidden), BF16),
        ]
        + (Gather.shapes(packs) if packs else []),
        scratch_shapes=[pltpu.VMEM((rows, width), BF16), pltpu.VMEM((rows, width), F32)]
        + (Gather.scratch(len(packs)) if packs else []),
        compiler_params=comm_params(ident),
    )(x, norms, at, outward, feed, feed, *packs)


def mix_back_kernel(sends, *refs):
    refs = Refs(refs)
    gx_ref, x_ref, norm_ref, at_ref, act_ref, slope_ref, o_ref, up_ref, down_ref = refs.take(9)
    sent = refs.take(sends)
    pack_ref, dot_ref, mlp_ref = refs.take(3)
    summed = refs.take(sends)
    low, low_t, normed_t = refs.take(3)
    t = pl.program_id(0)
    tens = pl.num_programs(0)
    steps = []
    if sends:
        me = Place()
        scatter = Scatter(me, sent[0], summed[0], *refs.take(10))
        steps = scatter.steps()

    @pl.when(t == 0)
    def _():
        if sends:
            me.greet()
            scatter.begin()
        grad = gx_ref[...].astype(BF16)
        low[...] = grad
        low_t[...] = turn(grad).astype(BF16)
        x = x_ref[...].astype(F32)
        normed = (standard(x)[0] * norm_ref[2:3] + norm_ref[3:4]).astype(BF16)
        normed_t[...] = turn(normed).astype(BF16)
        mlp_ref[...] = jnp.zeros_like(mlp_ref)

    def poll(part):
        spread(steps, t * 4 + part, tens * 4)

    hidden = up_ref.shape[2]
    poll(0)
    grad_attended = dot(low[...], o_ref[0, :, :QW])
    dot_ref[0, :QW] = turn(grad_attended).astype(BF16)
    dot_ref[0, QW:] = jnp.zeros_like(dot_ref[0, QW:])
    pack_ref[0, :, 2 * hidden :] = dot_nt(low_t[...], at_ref[0]).astype(BF16)
    poll(1)
    pack_ref[0, :, hidden : 2 * hidden] = dot(low_t[...], act_ref[0]).astype(BF16)
    poll(2)
    grad_pre = (dot(low[...], down_ref[0]) * slope_ref[0].astype(F32)).astype(BF16)
    poll(3)
    pack_ref[0, :, :hidden] = dot(normed_t[...], grad_pre).astype(BF16)
    mlp_ref[...] += dot_nt(grad_pre, up_ref[0])
    if sends:
        pl.when(t == tens - 1)(scatter.end)


def mix_back_call(gx, x, norms, at, act, slope, outward, feed, sent=None, ident=None):
    rows, width = x.shape
    tens = feed.shape[0]
    hidden = act.shape[2]
    whole = pl.BlockSpec(memory_space=pltpu.VMEM)
    wide = pl.BlockSpec((1, rows, hidden), lambda t: (t, 0, 0))
    part = pl.BlockSpec((1, 256, rows), lambda t: (t, 0, 0))
    args = [gx, x, norms, at, act, slope, outward, feed, feed]
    in_specs = [
        whole,
        whole,
        whole,
        part,
        wide,
        wide,
        pl.BlockSpec((1, width, 256), lambda t: (t, 0, 1)),
        pl.BlockSpec((1, width, hidden), lambda t: (t, 0, 0)),
        pl.BlockSpec((1, width, hidden), lambda t: (t, 0, 1)),
    ]
    out_specs = [pl.BlockSpec((1, width, 2 * hidden + 256), lambda t: (t, 0, 0)), part, whole]
    out_shape = [
        jax.ShapeDtypeStruct((tens, width, 2 * hidden + 256), BF16),
        jax.ShapeDtypeStruct((tens, 256, rows), BF16),
        jax.ShapeDtypeStruct((rows, width), F32),
    ]
    scratch = [
        pltpu.VMEM((rows, width), BF16),
        pltpu.VMEM((width, rows), BF16),
        pltpu.VMEM((width, rows), BF16),
    ]
    if sent is not None:
        sent = blocks_of(sent)
        args.append(sent)
        in_specs.append(pl.BlockSpec(memory_space=pl.ANY))
        out_specs.append(whole)
        out_shape.append(jax.ShapeDtypeStruct(sent.shape[3:], F32))
        scratch += Scatter.scratch(*sent.shape[3:])
    return pl.pallas_call(
        functools.partial(mix_back_kernel, int(sent is not None)),
        grid=(tens,),
        in_specs=in_specs,
        out_specs=out_specs,
        out_shape=out_shape,
        scratch_shapes=scratch,
        compiler_params=comm_params(ident),
    )(*args)


def attend_back_kernel(start_given, sends, merge, *refs):
    refs = Refs(refs)
    qt_ref, dot_ref, at_ref, lse_ref, kv_ref, trig_ref = refs.take(6)
    before_ref = refs.take(1)[0] if start_given else None
    sent = refs.take(sends)
    gqt_ref, dkv_ref = refs.take(2)
    summed = refs.take(sends)
    keys, values, keys_t, dkeys, dvalues = refs.take(5)
    t = pl.program_id(0)
    tens = pl.num_programs(0)
    rows = qt_ref.shape[2]
    parts = kv_ref.shape[0] // rows
    place = lax.axis_index("tensor")
    count = tens * (place + 1)
    steps = []
    if sends:
        me = Place()
        scatter = Scatter(me, sent[0], summed[0], *refs.take(10))
        steps = scatter.steps()
    if merge:
        low, landed, send, recv = refs.take(4)
        peers = (me.to_core, me.to_y, me.to_corner)
        copies = [
            remote(low.at[peer[1]], landed.at[k], send.at[k], recv.at[k], peer)
            for k, peer in enumerate(peers)
        ]

    @pl.when(t == 0)
    def _():
        if sends:
            me.greet(corner=merge)
            scatter.begin()
        both_t = turn(kv_ref[...])
        keys[...] = kv_ref[:, :HD]
        keys_t[...] = both_t[:HD].astype(BF16)
        values[...] = turn(both_t[HD:]).astype(BF16)
        dkeys[...] = jnp.zeros_like(dkeys)
        dvalues[...] = jnp.zeros_like(dvalues)

    inner = []
    for head in range(HEADS_HERE):
        span = slice(head * HD, (head + 1) * HD)
        inner.append(
            jnp.sum(
                dot_ref[0, span].astype(F32) * at_ref[0, span].astype(F32), axis=0, keepdims=True
            )
        )

    def block(index, carry, diagonal):
        here = pl.ds(pl.multiple_of(index * rows, rows), rows)
        key = keys[here, :]
        value = values[here, :]
        key_t = keys_t[:, here]
        out = []
        dkey = None
        for head in range(HEADS_HERE):
            span = slice(head * HD, (head + 1) * HD)
            query_t = qt_ref[0, span]
            grad_t = dot_ref[0, span]
            scores = dot(key, query_t)
            probs = jnp.exp(scores - lse_ref[0, head : head + 1])
            if diagonal:
                below = lax.broadcasted_iota(jnp.int32, scores.shape, 0)
                across = lax.broadcasted_iota(jnp.int32, scores.shape, 1)
                probs = jnp.where(below <= across, probs, 0.0)
            grad_probs = dot(value, grad_t)
            grad_scores = (probs * (grad_probs - inner[head])).astype(BF16)
            part_v = dot_nt(probs.astype(BF16), grad_t)
            part_k = dot_nt(grad_scores, query_t)
            dkey = part_k if dkey is None else dkey + part_k
            dvalue = part_v if head == 0 else dvalue + part_v
            part_q = dot(key_t, grad_scores)
            out.append(part_q if carry is None else carry[head] + part_q)
        dkeys[here, :] += dkey
        dvalues[here, :] += dvalue
        return tuple(out)

    def later(i, carry):
        spread(steps, t * (place + 1) + 1 + i, count)
        return block(i, carry, False)

    spread(steps, t * (place + 1), count)
    carry = block(place, None, True)
    carry = lax.fori_loop(0, place, later, carry)
    cos, sin = trig_ref[0:HALF], trig_ref[HALF:ROT]
    for head in range(HEADS_HERE):
        base = head * HD
        grad = carry[head] * SCALE
        gqt_ref[0, base : base + ROT] = rotated(grad[:ROT], cos, -sin).astype(BF16)
        gqt_ref[0, base + ROT : base + HD] = grad[ROT:].astype(BF16)
    gqt_ref[0, QW:] = jnp.zeros_like(gqt_ref[0, QW:])

    @pl.when(t == tens - 1)
    def _():
        both = jnp.concatenate([turn(dkeys[...]), turn(dvalues[...])], axis=0)
        for part in range(parts):
            piece = both[:, part * rows : (part + 1) * rows]
            if start_given:
                piece = piece + before_ref[part]
            if not merge:
                dkv_ref[part] = piece
            else:
                low[part] = piece.astype(BF16)

                @pl.when(place == part)
                def _(piece=piece):
                    dkv_ref[...] = piece

        if merge:
            for copy in copies:
                copy.start()
        if sends:
            scatter.end()
        if merge:
            for copy in copies:
                copy.wait_recv()
            dkv_ref[...] += (
                landed[0].astype(F32) + landed[1].astype(F32) + landed[2].astype(F32)
            )
            for copy in copies:
                copy.wait_send()


def attend_back_call(
    qt, dout, at, lse, kv, trig, before=None, sent=None, merge=False, ident=None
):
    tens, _, rows = qt.shape
    length = kv.shape[0]
    whole = pl.BlockSpec(memory_space=pltpu.VMEM)
    part = pl.BlockSpec((1, 256, rows), lambda t: (t, 0, 0))
    args = [qt, dout, at, lse, kv, trig]
    in_specs = [part, part, part, pl.BlockSpec((1, 8, rows), lambda t: (t, 0, 0)), whole, whole]
    pieces = (length // rows, 2 * HD, rows)
    out_specs = [part, whole]
    out_shape = [
        jax.ShapeDtypeStruct((tens, 256, rows), BF16),
        jax.ShapeDtypeStruct(pieces[1:] if merge else pieces, F32),
    ]
    scratch = [
        pltpu.VMEM((length, HD), BF16),
        pltpu.VMEM((length, HD), BF16),
        pltpu.VMEM((HD, length), BF16),
        pltpu.VMEM((length, HD), F32),
        pltpu.VMEM((length, HD), F32),
    ]
    if before is not None:
        args.append(before)
        in_specs.append(whole)
    if sent is not None:
        sent = blocks_of(sent)
        args.append(sent)
        in_specs.append(pl.BlockSpec(memory_space=pl.ANY))
        out_specs.append(whole)
        out_shape.append(jax.ShapeDtypeStruct(sent.shape[3:], F32))
        scratch += Scatter.scratch(*sent.shape[3:])
    if merge:
        scratch += [
            pltpu.VMEM(pieces, BF16),
            pltpu.VMEM((3,) + pieces[1:], BF16),
            pltpu.SemaphoreType.DMA((3,)),
            pltpu.SemaphoreType.DMA((3,)),
        ]
    return pl.pallas_call(
        functools.partial(attend_back_kernel, before is not None, int(sent is not None), merge),
        grid=(tens,),
        in_specs=in_specs,
        out_specs=out_specs,
        out_shape=out_shape,
        scratch_shapes=scratch,
        compiler_params=comm_params(ident),
    )(*args)


def norm_back_kernel(first, gx_ref, x_ref, norm_ref, mlp_ref, gqt_ref, qk_ref, *rest):
    if first:
        ov_ref, dkv_ref, trig_ref, other_ref, out_ref, pack_ref, normed_t, attn, shared = rest
    else:
        out_ref, pack_ref, sums_ref, normed_t, attn = rest
    t = pl.program_id(0)

    @pl.when(t == 0)
    def _():
        x = x_ref[...].astype(F32)
        normed = (standard(x)[0] * norm_ref[0:1] + norm_ref[1:2]).astype(BF16)
        normed_t[...] = turn(normed).astype(BF16)
        if first:
            cos, sin = trig_ref[0:HALF], trig_ref[HALF:ROT]
            grad = dkv_ref[...]
            shared[:ROT] = rotated(grad[:ROT], cos, -sin).astype(BF16)
            shared[ROT:] = grad[ROT:].astype(BF16)
            attn[...] = dot_nt(turn(shared[:HD]).astype(BF16), qk_ref[0, :, QW:]) + dot_nt(
                turn(shared[HD:]).astype(BF16), ov_ref[0, :, QW:]
            )
        else:
            attn[...] = jnp.zeros_like(attn)

    grad_t = gqt_ref[0, :QW]
    attn[...] += dot_nt(turn(grad_t).astype(BF16), qk_ref[0, :, :QW])
    if first:
        left = jnp.concatenate([grad_t, shared[:HD]], axis=0)
        pack_ref[t, :, :256] = dot_nt(normed_t[...], left).astype(BF16)
    else:
        pack_ref[0] = dot_nt(normed_t[...], gqt_ref[0]).astype(BF16)

    @pl.when(t == pl.num_programs(0) - 1)
    def _():
        unit, inverse = standard(x_ref[...].astype(F32))
        attn_grad, mlp_grad = attn[...], mlp_ref[...]
        sums = jnp.concatenate(
            [
                jnp.sum(attn_grad * unit, axis=0, keepdims=True),
                jnp.sum(attn_grad, axis=0, keepdims=True),
                jnp.sum(mlp_grad * unit, axis=0, keepdims=True),
                jnp.sum(mlp_grad, axis=0, keepdims=True),
            ],
            axis=0,
        )
        if first:
            pad = jnp.zeros((HD, sums.shape[1]), F32)
            lower = turn(jnp.concatenate([pad, sums, other_ref[...], pad[8:]], axis=0))
            upper = jnp.concatenate([shared[HD:], jnp.zeros_like(shared[HD:])], axis=0)
            right = (dot_nt(normed_t[...], upper) + lower).astype(BF16)
            for part in range(pack_ref.shape[0]):
                pack_ref[part, :, 256:] = right
        else:
            sums_ref[...] = sums
        grad = attn_grad * norm_ref[0:1] + mlp_grad * norm_ref[2:3]
        mean = jnp.mean(grad, axis=-1, keepdims=True)
        slant = jnp.mean(grad * unit, axis=-1, keepdims=True)
        out_ref[...] = gx_ref[...] + inverse * (grad - mean - unit * slant)


def norm_back_call(first, gx, x, norms, mlp, gqt, weights, dkv=None, trig=None, other=None):
    rows, width = x.shape
    tens = weights.shape[0]
    whole = pl.BlockSpec(memory_space=pltpu.VMEM)
    part = pl.BlockSpec((1, 256, rows), lambda t: (t, 0, 0))
    args = [gx, x, norms, mlp, gqt, weights]
    in_specs = [whole] * 4 + [part, pl.BlockSpec((1, width, 256), lambda t: (t, 0, 0))]
    scratch = [pltpu.VMEM((width, rows), BF16), pltpu.VMEM((rows, width), F32)]
    out_shape = [jax.ShapeDtypeStruct((rows, width), F32)]
    if first:
        args += [weights, dkv, trig, other]
        in_specs += [pl.BlockSpec((1, width, 256), lambda t: (0, 0, 1)), whole, whole, whole]
        scratch.append(pltpu.VMEM((2 * HD, rows), BF16))
        out_shape.append(jax.ShapeDtypeStruct((tens, width, 384), BF16))
        out_specs = [whole, whole]
    else:
        out_shape.append(jax.ShapeDtypeStruct((tens, width, 256), BF16))
        out_shape.append(jax.ShapeDtypeStruct((4, width), F32))
        out_specs = [whole, pl.BlockSpec((1, width, 256), lambda t: (t, 0, 0)), whole]
    return pl.pallas_call(
        functools.partial(norm_back_kernel, first),
        grid=(tens,),
        in_specs=in_specs,
        out_specs=out_specs,
        out_shape=out_shape,
        scratch_shapes=scratch,
        compiler_params=comm_params(None),
    )(*args)


def lamb_parts(weight, first, second, grad):
    first_new = BETA_FIRST * first + (1.0 - BETA_FIRST) * grad
    second_new = BETA_SECOND * second + (1.0 - BETA_SECOND) * grad * grad
    update = (
        first_new
        / (1.0 - BETA_FIRST**STEP)
        / (jnp.sqrt(second_new / (1.0 - BETA_SECOND**STEP)) + ADAM_EPSILON)
        + WEIGHT_DECAY * weight
    )
    return (first_new, second_new, update)


def keyval_grad(late):
    lane = lax.broadcasted_iota(jnp.int32, (late.shape[0], 2 * HD), 1)
    left = pltpu.roll(late[:, 128:256], HD, 1)
    right = pltpu.roll(late[:, 256:384], HD, 1)
    return jnp.where(lane < HD, left, right)


def norm_grad(late):
    return turn(late[:, 256:384])[HD : HD + 8]


def square(value):
    total = jnp.sum(value * value, axis=1, keepdims=True)
    return jnp.sum(total, axis=0, keepdims=True)


def lanes(pairs):
    lane = lax.broadcasted_iota(jnp.int32, (1, 128), 1)
    row = jnp.zeros((1, 128), F32)
    for place, value in pairs:
        row = jnp.where(lane == place, value, row)
    return row


class Tensors:
    def __init__(self, refs, early, late):
        self.refs = refs
        self.early, self.late = early, late

    def early_grad(self, layer, which):
        pack = self.early[layer]
        hidden = (pack.shape[1] - 256) // 2
        if which == "up":
            return pack[:, :hidden]
        if which == "down":
            return turn(pack[:, hidden : 2 * hidden])
        return turn(pack[:, 2 * hidden :])[:QW]

    def parts(self, array, index, grad):
        weight, first, second = (ref[...] if index is None else ref[index] for ref in array)
        return (weight,) + lamb_parts(weight, first, second, grad)

    def each(self, late0):
        query, keyval, output, upward, downward, norms = range(6)
        for layer in range(2):
            yield 5 + layer, upward, layer, lambda: self.early_grad(layer, "up")
            yield 7 + layer, downward, layer, lambda: self.early_grad(layer, "down")
            yield 3 + layer, output, layer, lambda: self.early_grad(layer, "output")
        yield 1, query, 1, lambda: self.late[1][:, :QW]
        yield 0, query, 0, lambda: late0()[:, :QW]
        yield 2, keyval, None, lambda: keyval_grad(late0())
        for layer in range(2):
            yield 9 + 4 * layer, norms, layer, lambda: norm_grad(late0())[4 * layer : 4 * layer + 4]


def norms_kernel(*refs):
    refs = Refs(refs)
    parts_ref, early0, early1, late1 = refs.take(4)
    arrays = [refs.take(3) for _ in range(6)]
    late0_ref, sums_ref = refs.take(2)
    scatter_refs = refs.take(10)
    near_land, along_land, send, recv = refs.take(4)
    me = Place()
    scatter = Scatter(me, parts_ref, late0_ref, *scatter_refs)
    steps = scatter.steps()
    me.greet(near=True)
    scatter.begin()
    tensors = Tensors(arrays, (early0, early1), (None, late1))
    leader = (me.tensor == 0).astype(F32)
    old, new = [], []

    def late0():
        return late0_ref[...]

    waiting = list(steps)
    for place, array, index, grad in tensors.each(late0):
        if place == 0:
            for step in waiting:
                step()
            scatter.end()
        elif place != 2 and place < 9 and place != 1 and waiting:
            waiting.pop(0)()
            waiting.pop(0)()
        weight, _, _, update = tensors.parts(arrays[array], index, grad())
        if place >= 9:
            for row in range(4):
                old.append((place + row, square(weight[row : row + 1]) * leader))
                new.append((place + row, square(update[row : row + 1]) * leader))
        else:
            scale = leader if place == 2 else 1.0
            old.append((place, square(weight) * scale))
            new.append((place, square(update) * scale))

    near_land[0] = jnp.concatenate([lanes(old), lanes(new), jnp.zeros((6, 128), F32)], axis=0)
    copies = []
    for code, peer in me.near():
        copies.append(
            remote(near_land.at[0], near_land.at[code], send.at[code], recv.at[code], peer)
        )
        copies[-1].start()
    for copy in copies:
        copy.wait()
    total = jnp.zeros((8, 128), F32)
    for x in range(2):
        for y in range(2):
            for core in range(2):
                code = lax.rem(x + me.x, 2) * 4 + lax.rem(y + me.y, 2) * 2
                total = total + near_land[code + lax.rem(core + me.core, 2)]
    along_land[0] = total
    copies = []
    for shift in (1, 2, 3):
        copies.append(
            remote(
                along_land.at[0], along_land.at[shift], send.at[7 + shift],
                recv.at[7 + shift], me.at(z=me.along(shift)),
            )
        )
        copies[-1].start()
    for copy in copies:
        copy.wait()
    total = jnp.zeros((8, 128), F32)
    for z in range(4):
        total = total + along_land[me.along(4 - z)]
    sums_ref[...] = total


def norms_call(parts, early, late1, arrays):
    parts = blocks_of(parts)
    rows, cols = parts.shape[3:]
    vmem = pl.BlockSpec(memory_space=pltpu.VMEM)
    flat = [ref for array in arrays for ref in array]
    return pl.pallas_call(
        norms_kernel,
        in_specs=[pl.BlockSpec(memory_space=pl.ANY)] + [vmem] * (3 + len(flat)),
        out_specs=[vmem, vmem],
        out_shape=[
            jax.ShapeDtypeStruct((rows, cols), F32),
            jax.ShapeDtypeStruct((8, 128), F32),
        ],
        scratch_shapes=Scatter.scratch(rows, cols)
        + [
            pltpu.VMEM((8, 8, 128), F32),
            pltpu.VMEM((4, 8, 128), F32),
            pltpu.SemaphoreType.DMA((11,)),
            pltpu.SemaphoreType.DMA((11,)),
        ],
        compiler_params=comm_params(8),
    )(parts, *early, late1, *flat)


def lamb_kernel(*refs):
    refs = Refs(refs)
    sums_ref, early0, early1, late0_ref, late1 = refs.take(5)
    arrays = [refs.take(3) for _ in range(6)]
    outs = [refs.take(4) for _ in range(6)]
    norm_out, ratio_out = refs.take(2)
    weight_norm = jnp.sqrt(sums_ref[0:1])
    update_norms = jnp.sqrt(sums_ref[1:2])
    used = lax.broadcasted_iota(jnp.int32, (1, 128), 1) < 17
    ratios = jnp.where(used, weight_norm / jnp.where(used, update_norms, 1.0), 0.0)
    norm_out[...] = update_norms
    ratio_out[...] = ratios
    tensors = Tensors(arrays, (early0, early1), (None, late1))
    for place, array, index, grad in tensors.each(lambda: late0_ref[...]):
        weight, first, second, update = tensors.parts(arrays[array], index, grad())
        if place >= 9:
            factor = jnp.concatenate(
                [ratios[:, place + row : place + row + 1] for row in range(4)], axis=0
            )
        else:
            factor = ratios[:, place : place + 1]
        after = weight - LEARN_RATE * factor * update
        where = Ellipsis if index is None else index
        for ref, value in zip(outs[array], (first, second, after, after.astype(BF16))):
            ref[where] = value


def lamb_call(sums, early, late, arrays):
    vmem = pl.BlockSpec(memory_space=pltpu.VMEM)
    flat = [ref for array in arrays for ref in array]
    shapes = []
    for array in arrays:
        shape = array[0].shape
        shapes += [jax.ShapeDtypeStruct(shape, F32)] * 3 + [jax.ShapeDtypeStruct(shape, BF16)]
    shapes += [jax.ShapeDtypeStruct((1, 128), F32)] * 2
    return pl.pallas_call(
        lamb_kernel,
        in_specs=[vmem] * (5 + len(flat)),
        out_specs=[vmem] * len(shapes),
        out_shape=shapes,
        compiler_params=comm_params(None),
    )(sums, *early, *late, *flat)


def angles(places):
    steps = jnp.arange(HALF).astype(F32)
    inverse = jnp.exp(steps * (-2.0 * math.log(10000.0) / ROT))
    phase = (0.25 * inverse)[:, None] * places.astype(F32)[None, :]
    return jnp.concatenate([jnp.cos(phase), jnp.sin(phase)], axis=0)


def param_squares(arrays, leader):
    query, keyval, output, upward, downward, norms = arrays
    return jnp.concatenate(
        [
            jnp.sum(query * query, axis=(1, 2)),
            (jnp.sum(keyval * keyval) * leader)[None],
            jnp.sum(output * output, axis=(1, 2)),
            jnp.sum(upward * upward, axis=(1, 2)),
            jnp.sum(downward * downward, axis=(1, 2)),
            jnp.sum(norms * norms, axis=2).reshape(8) * leader,
        ]
    )


def apply_trust(masters, updates, trust):
    factors = (
        trust[0:2][:, None, None],
        trust[2],
        trust[3:5][:, None, None],
        trust[5:7][:, None, None],
        trust[7:9][:, None, None],
        trust[9:17].reshape(2, 4, 1),
    )
    return tuple(
        (
            weight - LEARN_RATE * factor * update
            for weight, factor, update in zip(masters, factors, updates)
        )
    )


def plain_scatter(parts, depth):
    pieces = parts.reshape(-1, depth, parts.shape[-1])
    return lax.psum_scatter(pieces, ("tensor", "dp"), scatter_dimension=0).astype(F32)


def shards(
    fast,
    hidden_in,
    out_grad,
    positions,
    query_weight,
    keyval_weight,
    output_weight,
    up_weight,
    down_weight,
    norm_params,
    query_first,
    query_second,
    keyval_first,
    keyval_second,
    output_first,
    output_second,
    up_first,
    up_second,
    down_first,
    down_second,
    norm_first,
    norm_second,
):
    masters = (query_weight, keyval_weight, output_weight, up_weight, down_weight, norm_params)
    tensor = lax.axis_index("tensor")
    leader = (tensor == 0).astype(F32)
    rows, width = hidden_in.shape
    tens = positions.shape[0] // rows
    depth = keyval_weight.shape[0]

    narrow, wide = [], []
    for layer in range(2):
        if layer == 0:
            keys, values = keyval_weight[:, :HD], keyval_weight[:, HD:]
        else:
            keys = values = jnp.zeros((depth, HD), F32)
        pieces = [query_weight[layer], keys, output_weight[layer].T, values]
        narrow.append(jnp.concatenate(pieces, axis=1).astype(BF16))
        wide.append(
            jnp.concatenate([up_weight[layer], down_weight[layer].T], axis=1).astype(BF16)
        )
    norm_low = norm_params.astype(BF16).reshape(8, depth)

    def joined(pack):
        return pack.reshape(tens, width, pack.shape[-1])

    if fast:
        norm_pack = jnp.pad(norm_low, ((0, 8), (0, 128 - depth)))
        (first_narrow,), norm_all = gather_call([narrow[0]], norm_pack)
        norm_full = norm_all[:, :, :8, :depth].reshape(-1, 8, depth)
        attn_all = [joined(first_narrow), None]
        feed_all = [None, None]
    else:
        attn_all, feed_all = (
            [joined(lax.all_gather(pack, ("tensor", "dp"), axis=0)) for pack in packs]
            for packs in (narrow, wide)
        )
        norm_full = lax.all_gather(norm_low, "dp", axis=0)
    norm_full = jnp.swapaxes(norm_full, 0, 1).reshape(2, 4, width).astype(F32)
    trig = angles(lax.dynamic_slice_in_dim(positions, tensor * rows, rows, 0))
    length = positions.shape[0]

    current = hidden_in
    saved = []
    kv = None
    for layer in range(2):
        norms = norm_full[layer]
        if layer == 0:
            qt, kv_here = qkv_call(True, current, norms, trig, attn_all[layer])
        else:
            (qt,) = qkv_call(False, current, norms, trig, attn_all[layer])
        if fast and layer == 0:
            at, lse, kv, feed = attend_call(
                qt, kv_here, length, [wide[layer]], share=True, ident=1
            )
            kv = kv.reshape(length, 2 * HD)
            feed_all[layer] = joined(feed)
        elif fast:
            at, lse, feed = attend_call(qt, kv, length, [wide[layer]], ident=4)
            feed_all[layer] = joined(feed)
        else:
            if layer == 0:
                kv = share_call(kv_here, tens).reshape(length, 2 * HD)
            at, lse = attend_call(qt, kv, length)
        if fast and layer == 0:
            after, act, slope, second = mix_call(
                current, norms, at, attn_all[layer], feed_all[layer], [narrow[1]], ident=2
            )
            attn_all[1] = joined(second)
        else:
            after, act, slope = mix_call(current, norms, at, attn_all[layer], feed_all[layer])
        saved.append((current, qt, at, lse, act, slope))
        current = after

    x, qt, at, lse, act, slope = saved[1]
    norms = norm_full[1]
    early, late = [None, None], [None, None]
    pack, dout, mlp = mix_back_call(
        out_grad, x, norms, at, act, slope, attn_all[1], feed_all[1]
    )
    if fast:
        gqt, dkv, early[1] = attend_back_call(qt, dout, at, lse, kv, trig, sent=pack, ident=5)
    else:
        gqt, dkv = attend_back_call(qt, dout, at, lse, kv, trig)
        early[1] = plain_scatter(pack, depth)
    grad, pack, sums = norm_back_call(False, out_grad, x, norms, mlp, gqt, attn_all[1])

    x, qt, at, lse, act, slope = saved[0]
    norms = norm_full[0]
    if fast:
        early_pack, dout, mlp, late[1] = mix_back_call(
            grad, x, norms, at, act, slope, attn_all[0], feed_all[0], pack, ident=6
        )
        gqt, dkv, early[0] = attend_back_call(
            qt, dout, at, lse, kv, trig, dkv, early_pack, True, ident=7
        )
    else:
        late[1] = plain_scatter(pack, depth)
        pack, dout, mlp = mix_back_call(
            grad, x, norms, at, act, slope, attn_all[0], feed_all[0]
        )
        early[0] = plain_scatter(pack, depth)
        gqt, dkv = attend_back_call(qt, dout, at, lse, kv, trig, dkv)
        dkv = merge_call(dkv)
    grad, pack = norm_back_call(
        True, grad, x, norms, mlp, gqt, attn_all[0], dkv, trig, sums
    )
    arrays = (
        (query_weight, query_first, query_second),
        (keyval_weight, keyval_first, keyval_second),
        (output_weight, output_first, output_second),
        (up_weight, up_first, up_second),
        (down_weight, down_first, down_second),
        (norm_params, norm_first, norm_second),
    )
    if fast:
        late[0], totals = norms_call(pack, early, late[1], arrays)
        *nexts, update_norms, trust_ratios = lamb_call(totals, early, late, arrays)
        return (current, grad, *nexts, update_norms[0, :17], trust_ratios[0, :17])
    late[0] = plain_scatter(pack, depth)
    hidden = up_weight.shape[2]
    query_g = jnp.stack([late[layer][:, :QW] for layer in range(2)])
    keyval_g = late[0][:, QW : QW + 2 * HD]
    output_g = jnp.stack([early[layer][:, 2 * hidden : 2 * hidden + QW].T for layer in range(2)])
    up_g = jnp.stack([early[layer][:, :hidden] for layer in range(2)])
    down_g = jnp.stack([early[layer][:, hidden : 2 * hidden].T for layer in range(2)])
    norm_g = late[0][:, QW + 2 * HD : QW + 2 * HD + 8].T.reshape(2, 4, depth)

    grads = (query_g, keyval_g, output_g, up_g, down_g, norm_g)
    parts = [lamb_parts(*array, grad) for array, grad in zip(arrays, grads)]
    updates = tuple((part[2] for part in parts))
    weight_total, update_total = lax.psum(
        (param_squares(masters, leader), param_squares(updates, leader)), ("dp", "tensor")
    )
    weight_norm = jnp.sqrt(weight_total)
    update_norms = jnp.sqrt(update_total)
    trust_ratios = weight_norm / update_norms
    nexts = apply_trust(masters, updates, trust_ratios)
    outs = [current, grad]
    for index in range(6):
        low = nexts[index].astype(BF16)
        outs += [parts[index][0], parts[index][1], nexts[index], low]
    return tuple(outs) + (update_norms, trust_ratios)


def solution(mesh):
    fast = mesh.shape["dp"] == 8 and mesh.shape["tensor"] == 4
    columns = P(None, "dp", "tensor")
    across = P(None, "tensor", "dp")
    flat = P("dp", None)
    norm = P(None, None, "dp")
    state = P(("dp", "tensor"), None)
    in_specs = (
        (state, state, P("dp"), columns, flat, across, columns, across, norm)
        + (columns, columns, flat, flat, across, across, columns, columns, across, across)
        + (norm, norm)
    )
    out_specs = (
        (state, state)
        + (columns,) * 4
        + (flat,) * 4
        + (across,) * 4
        + (columns,) * 4
        + (across,) * 4
        + (norm,) * 4
        + (P(), P())
    )
    return jax.shard_map(
        functools.partial(shards, fast),
        mesh=mesh,
        in_specs=in_specs,
        out_specs=out_specs,
        check_vma=False,
    )
```

```python
import functools
import math

import jax
import jax.numpy as jnp
from jax import lax
from jax.experimental import pallas as pl
from jax.experimental.pallas import tpu as pltpu
from jax.sharding import PartitionSpec as P

F32 = jnp.float32
BF16 = jnp.bfloat16
MESH = pl.DeviceIdType.MESH

HD = 64
ROT = 16
HALF = ROT // 2
STEP = 5
HEADS_HERE = 3
QW = 192

NORM_EPSILON = 1e-05
BETA_FIRST = 0.5
BETA_SECOND = 0.55
ADAM_EPSILON = 1e-06
WEIGHT_DECAY = 0.01
LEARN_RATE = 0.5
SCALE = HD**-0.5
ROOM = 63 * 2**20


def dot(a, b):
    return jnp.dot(a, b, preferred_element_type=F32)


def dot_nt(a, b):
    return lax.dot_general(a, b, (((1,), (1,)), ((), ())), preferred_element_type=F32)


def turn(a):
    return jnp.transpose(a.astype(F32), (1, 0))


def standard(values):
    center = values - jnp.mean(values, axis=-1, keepdims=True)
    spread = jnp.mean(center * center, axis=-1, keepdims=True)
    inverse = lax.rsqrt(spread + NORM_EPSILON)
    return center * inverse, inverse


def gelu_parts(v):
    x = jnp.abs(v) * (2.0**-0.5)
    bell = jnp.exp(-x * x)
    t = 1.0 / (1.0 + 0.3275911 * x)
    series = t * (
        0.254829592
        + t * (-0.284496736 + t * (1.421413741 + t * (-1.453152027 + t * 1.061405429)))
    )
    tail = 0.5 * series * bell
    cumulative = jnp.where(v < 0.0, tail, 1.0 - tail)
    return cumulative, bell * (1.0 / math.sqrt(2.0 * math.pi))


class Place:
    def __init__(self):
        dp, tensor = lax.axis_index("dp"), lax.axis_index("tensor")
        self.z, self.x = lax.div(dp, 2), lax.rem(dp, 2)
        self.y, self.core = lax.div(tensor, 2), lax.rem(tensor, 2)
        self.tensor = tensor
        self.to_x = self.at(x=1 - self.x)
        self.to_y = self.at(y=1 - self.y)
        self.to_core = self.at(core=1 - self.core)
        self.to_corner = self.at(y=1 - self.y, core=1 - self.core)

    def at(self, z=None, x=None, y=None, core=None):
        z = self.z if z is None else z
        x = self.x if x is None else x
        y = self.y if y is None else y
        core = self.core if core is None else core
        return (z * 2 + x, y * 2 + core)

    def along(self, shift):
        return lax.rem(self.z + shift, 4)

    def near(self):
        return [
            (
                code,
                self.at(
                    x=lax.rem(self.x + code // 4, 2),
                    y=lax.rem(self.y + code // 2 % 2, 2),
                    core=lax.rem(self.core + code % 2, 2),
                ),
            )
            for code in range(1, 8)
        ]

    def greet(self, corner=False, near=False):
        peers = [self.at(z=self.along(shift)) for shift in (1, 2, 3)]
        if near:
            peers += [peer for _, peer in self.near()]
        else:
            peers += [self.to_x, self.to_y, self.to_core]
        if corner:
            peers.append(self.to_corner)
        barrier = pltpu.get_barrier_semaphore()
        for peer in peers:
            pl.semaphore_signal(barrier, inc=1, device_id=peer, device_id_type=MESH)
        pl.semaphore_wait(barrier, len(peers))


class Refs:
    def __init__(self, refs):
        self.refs = list(refs)

    def take(self, count):
        taken, self.refs = self.refs[:count], self.refs[count:]
        return taken


def comm_params(ident):
    if ident is None:
        return pltpu.CompilerParams(vmem_limit_bytes=ROOM)
    return pltpu.CompilerParams(
        collective_id=ident, has_side_effects=True, vmem_limit_bytes=ROOM
    )


def remote(src, dst, send, recv, to):
    return pltpu.make_async_remote_copy(
        src_ref=src, dst_ref=dst, send_sem=send, recv_sem=recv, device_id=to, device_id_type=MESH
    )


def spread(steps, index, count):
    for place, step in enumerate(steps):
        pl.when(index == lax.div(place * count, len(steps)))(step)


def timed(steps, now, span):
    for due, step in steps:
        pl.when((now <= due) & (due < now + span))(step)


class Gather:
    COUNT = 35

    def __init__(self, me, source, out, own_sem, send, recv):
        half = source.shape[0] // 2
        top, low = pl.ds(0, half), pl.ds(half, half)
        other = (1 - me.y) * 2 + me.core
        mine = out.at[me.tensor, me.z, me.x]

        def copy(slot, src, dst, to):
            return remote(src, dst, send.at[slot], recv.at[slot], to)

        parts = {"own": pltpu.make_async_copy(source, mine, own_sem)}
        for d in range(4):
            z = me.along(4 - d)
            block = out.at[me.tensor, z, me.x]
            origin = source if d == 0 else block
            if d > 0:
                parts["z", d] = copy(d - 1, source, mine, me.at(z=me.along(d)))
            parts["x", d] = copy(3 + d, origin, block, me.to_x)
            parts["y", d] = copy(7 + d, origin, block, me.to_y)
            parts["core", d] = copy(11 + d, origin, block, me.to_core)
            from_x, from_y = out.at[me.tensor, z, 1 - me.x], out.at[other, z, me.x]
            parts["xy", d] = copy(15 + d, from_x.at[top], from_x.at[top], me.to_y)
            parts["yx", d] = copy(19 + d, from_y.at[low], from_y.at[low], me.to_x)
            parts["core x", d] = copy(23 + d, from_x, from_x, me.to_core)
            parts["core y", d] = copy(27 + d, from_y, from_y, me.to_core)
            far = out.at[other, z, 1 - me.x]
            parts["core far", d] = copy(31 + d, far, far, me.to_core)
        self.parts = parts

    def begin(self):
        for key in (("z", 1), ("x", 0), ("y", 0), ("core", 0), "own"):
            self.parts[key].start()

    def pass_on(self, d, following):
        self.parts["z", d].wait()
        if following:
            self.parts["z", following].start()
        for way in ("x", "y", "core"):
            self.parts[way, d].start()

    def cross(self, d):
        self.parts["x", d].wait_recv()
        self.parts["xy", d].start()
        self.parts["core x", d].start()
        self.parts["y", d].wait_recv()
        self.parts["yx", d].start()
        self.parts["core y", d].start()

    def far(self, d):
        self.parts["xy", d].wait_recv()
        self.parts["yx", d].wait_recv()
        self.parts["core far", d].start()

    def arrive(self):
        self.parts["own"].wait()
        for key, copy in self.parts.items():
            if key != "own" and key[0].startswith("core"):
                copy.wait_recv()

    def end(self):
        for key, copy in self.parts.items():
            if key != "own" and key[0] != "z":
                copy.wait_send()

    def steps(self):
        return [
            functools.partial(self.pass_on, 1, 3),
            functools.partial(self.cross, 0),
            functools.partial(self.pass_on, 3, 2),
            functools.partial(self.cross, 1),
            functools.partial(self.far, 0),
            functools.partial(self.pass_on, 2, None),
            functools.partial(self.cross, 3),
            functools.partial(self.far, 1),
            functools.partial(self.cross, 2),
            functools.partial(self.far, 3),
            functools.partial(self.far, 2),
        ]


def add_rows(total, part):
    def one(i, _):
        rows = pl.ds(pl.multiple_of(i * 16, 16), 16)
        total[rows, :] += part[rows, :]
        return 0

    lax.fori_loop(0, total.shape[0] // 16, one, 0)


class Scatter:
    COUNT = 27

    @staticmethod
    def scratch(rows, cols):
        half = rows // 2
        return [
            pltpu.VMEM((4, 2, 2, rows, cols), BF16),
            pltpu.VMEM((2, 4, 2, rows, cols), BF16),
            pltpu.VMEM((4, 2, half, cols), BF16),
            pltpu.VMEM((4, 2, half, cols), BF16),
            pltpu.VMEM((4, half, cols), BF16),
            pltpu.VMEM((4, half, cols), BF16),
            pltpu.VMEM((3, rows, cols), BF16),
            pltpu.SemaphoreType.DMA((8,)),
            pltpu.SemaphoreType.DMA((Scatter.COUNT,)),
            pltpu.SemaphoreType.DMA((Scatter.COUNT,)),
        ]

    def __init__(
        self, me, source, out, total, from_core, from_x, from_y, turn_x, turn_y, from_z,
        load_sem, send, recv,
    ):
        self.me, self.out, self.total = me, out, total
        self.from_core, self.from_x, self.from_y = from_core, from_x, from_y
        self.turn_x, self.turn_y, self.from_z = turn_x, turn_y, from_z
        half = total.shape[3] // 2
        self.top, self.low = pl.ds(0, half), pl.ds(half, half)
        self.order = [me.along(d) for d in (2, 3, 1, 0)]
        self.parts = parts = {}

        def copy(slot, src, dst, to):
            return remote(src, dst, send.at[slot], recv.at[slot], to)

        for d, z in enumerate(self.order):
            for y in range(2):
                parts["load", d, y] = pltpu.make_async_copy(
                    source.at[2 * y + me.core, z], total.at[z, :, y], load_sem.at[2 * d + y]
                )
                parts["core", d, y] = copy(
                    2 * d + y, source.at[2 * y + 1 - me.core, z], from_core.at[y, z], me.to_core
                )
            parts["x", d] = copy(
                8 + d, total.at[z, 1 - me.x, :, self.top], from_x.at[z], me.to_x
            )
            parts["y", d] = copy(
                12 + d, total.at[z, :, 1 - me.y, self.low], from_y.at[z], me.to_y
            )
            parts["xy", d] = copy(
                16 + d, total.at[z, me.x, 1 - me.y, self.top], turn_y.at[z], me.to_y
            )
            parts["yx", d] = copy(
                20 + d, total.at[z, 1 - me.x, me.y, self.low], turn_x.at[z], me.to_x
            )
            if d < 3:
                parts["z", d] = copy(24 + d, total.at[z, me.x, me.y], from_z.at[d], me.at(z=z))

    def load(self, d):
        for y in range(2):
            self.parts["core", d, y].start()
            self.parts["load", d, y].start()

    def launch(self, d):
        self.parts["x", d].start()
        self.parts["y", d].start()

    def begin(self):
        self.load(0)
        self.load(1)

    def core(self, d):
        z = self.order[d]
        for y in range(2):
            self.parts["load", d, y].wait()
            self.parts["core", d, y].wait_recv()
            for x in range(2):
                add_rows(self.total.at[z, x, y], self.from_core.at[y, z, x])
        if d < 2:
            self.launch(d)
            self.load(d + 2)

    def cross(self, d):
        me, z = self.me, self.order[d]
        self.parts["x", d].wait_recv()
        self.parts["y", d].wait_recv()
        if d < 2:
            self.launch(d + 2)
        for y in range(2):
            add_rows(self.total.at[z, me.x, y, self.top], self.from_x.at[z, y])
        self.parts["xy", d].start()
        for x in range(2):
            add_rows(self.total.at[z, x, me.y, self.low], self.from_y.at[z, x])
        self.parts["yx", d].start()

    def far(self, d):
        me, z = self.me, self.order[d]
        self.parts["xy", d].wait_recv()
        add_rows(self.total.at[z, me.x, me.y, self.top], self.turn_y.at[z])
        self.parts["yx", d].wait_recv()
        add_rows(self.total.at[z, me.x, me.y, self.low], self.turn_x.at[z])
        if d < 3:
            self.parts["z", d].start()

    def end(self):
        me = self.me
        for d in range(3):
            self.parts["z", d].wait_recv()

        def one(i, _):
            rows = pl.ds(pl.multiple_of(i * 16, 16), 16)
            result = self.total[me.z, me.x, me.y, rows, :].astype(F32)
            for d in range(3):
                result = result + self.from_z[d, rows, :].astype(F32)
            self.out[rows, :] = result
            return 0

        lax.fori_loop(0, self.out.shape[0] // 16, one, 0)
        for key, copy in self.parts.items():
            if key[0] != "load":
                copy.wait_send()

    def steps(self):
        order = [
            (self.core, 0), (self.core, 1), (self.core, 2), (self.core, 3), (self.cross, 0),
            (self.cross, 1), (self.far, 0), (self.far, 1), (self.cross, 2), (self.cross, 3),
            (self.far, 2), (self.far, 3),
        ]
        return [functools.partial(step, d) for step, d in order] + [self.end]


def tensor_barrier(count):
    me = lax.axis_index("tensor")
    barrier = pltpu.get_barrier_semaphore()
    for shift in range(1, count):
        pl.semaphore_signal(
            barrier, inc=1, device_id={"tensor": lax.rem(me + shift, count)}, device_id_type=MESH
        )
    pl.semaphore_wait(barrier, count - 1)


def share_kernel(count, mine_ref, out_ref, here_sem, send_sem, recv_sem):
    me = lax.axis_index("tensor")
    tensor_barrier(count)
    copies = []
    for shift in range(1, count):
        copies.append(
            pltpu.make_async_remote_copy(
                src_ref=mine_ref,
                dst_ref=out_ref.at[me],
                send_sem=send_sem.at[shift],
                recv_sem=recv_sem.at[shift],
                device_id={"tensor": lax.rem(me + shift, count)},
                device_id_type=MESH,
            )
        )
        copies[-1].start()
    own = pltpu.make_async_copy(mine_ref, out_ref.at[me], here_sem)
    own.start()
    own.wait()
    for copy in copies:
        copy.wait()


def share_call(mine, count):
    return pl.pallas_call(
        functools.partial(share_kernel, count),
        in_specs=[pl.BlockSpec(memory_space=pltpu.VMEM)],
        out_specs=pl.BlockSpec(memory_space=pltpu.VMEM),
        out_shape=jax.ShapeDtypeStruct((count,) + mine.shape, mine.dtype),
        scratch_shapes=[
            pltpu.SemaphoreType.DMA,
            pltpu.SemaphoreType.DMA((count,)),
            pltpu.SemaphoreType.DMA((count,)),
        ],
        compiler_params=pltpu.CompilerParams(collective_id=9, has_side_effects=True),
    )(mine)


def merge_kernel(count, parts_ref, out_ref, low, landed, send_sem, recv_sem):
    me = lax.axis_index("tensor")
    low[...] = parts_ref[...].astype(BF16)
    tensor_barrier(count)
    copies = []
    for shift in range(1, count):
        to = lax.rem(me + shift, count)
        copies.append(
            pltpu.make_async_remote_copy(
                src_ref=low.at[to],
                dst_ref=landed.at[shift],
                send_sem=send_sem.at[shift],
                recv_sem=recv_sem.at[shift],
                device_id={"tensor": to},
                device_id_type=MESH,
            )
        )
        copies[-1].start()
    total = parts_ref[me]
    for shift, copy in enumerate(copies, 1):
        copy.wait()
        total = total + landed[shift].astype(F32)
    out_ref[...] = total


def merge_call(parts):
    count = parts.shape[0]
    vmem = pl.BlockSpec(memory_space=pltpu.VMEM)
    return pl.pallas_call(
        functools.partial(merge_kernel, count),
        in_specs=[vmem],
        out_specs=vmem,
        out_shape=jax.ShapeDtypeStruct(parts.shape[1:], F32),
        scratch_shapes=[
            pltpu.VMEM(parts.shape, BF16),
            pltpu.VMEM(parts.shape, BF16),
            pltpu.SemaphoreType.DMA((count,)),
            pltpu.SemaphoreType.DMA((count,)),
        ],
        compiler_params=pltpu.CompilerParams(collective_id=10, has_side_effects=True),
    )(parts)


def blocks_of(parts):
    tens, width, cols = parts.shape
    return parts.reshape(tens, 4, 2, width // 8, cols)


def rotated(low, cos, sin):
    first, second = low[:HALF], low[HALF:ROT]
    return jnp.concatenate([first * cos - second * sin, second * cos + first * sin], axis=0)


def put_query(lin, cos, sin, qt_ref):
    for head in range(HEADS_HERE):
        base = head * HD
        low = rotated(lin[base : base + ROT], cos, sin)
        qt_ref[base : base + ROT] = (low.astype(BF16).astype(F32) * SCALE).astype(BF16)
        qt_ref[base + ROT : base + HD] = (
            lin[base + ROT : base + HD].astype(BF16).astype(F32) * SCALE
        ).astype(BF16)
    qt_ref[QW:] = jnp.zeros_like(qt_ref[QW:])


def keyval_rows(lin, value, cos, sin):
    key = jnp.concatenate([rotated(lin[QW : QW + ROT], cos, sin), lin[QW + ROT :]], axis=0)
    return turn(jnp.concatenate([key, value], axis=0)).astype(BF16)


def normed_rows(x, gain, bias):
    return (standard(x)[0] * gain + bias).astype(BF16)


def qkv_kernel(first, x_ref, norm_ref, trig_ref, qk_ref, *rest):
    if first:
        ov_ref, qt_ref, kv_ref, normed = rest
    else:
        qt_ref, normed = rest
    t = pl.program_id(0)

    @pl.when(t == 0)
    def _():
        normed[...] = normed_rows(x_ref[...].astype(F32), norm_ref[0:1], norm_ref[1:2])

    cos, sin = trig_ref[0:HALF], trig_ref[HALF:ROT]
    lin = turn(dot(normed[...], qk_ref[0]))
    put_query(lin, cos, sin, qt_ref.at[0])
    if first:

        @pl.when(t == 0)
        def _():
            value = turn(dot(normed[...], ov_ref[0]))[QW:]
            kv_ref[...] = keyval_rows(lin, value, cos, sin)


def qkv_call(first, x, norms, trig, weights):
    rows, width = x.shape
    tens = weights.shape[0]
    whole = pl.BlockSpec(memory_space=pltpu.VMEM)
    in_specs = [whole, whole, whole, pl.BlockSpec((1, width, 256), lambda t: (t, 0, 0))]
    out_shape = [jax.ShapeDtypeStruct((tens, 256, rows), BF16)]
    out_specs = [pl.BlockSpec((1, 256, rows), lambda t: (t, 0, 0))]
    args = [x, norms, trig, weights]
    if first:
        in_specs.append(pl.BlockSpec((1, width, 256), lambda t: (0, 0, 1)))
        args.append(weights)
        out_shape.append(jax.ShapeDtypeStruct((rows, 2 * HD), BF16))
        out_specs.append(whole)
    return pl.pallas_call(
        functools.partial(qkv_kernel, first),
        grid=(tens,),
        in_specs=in_specs,
        out_specs=out_specs,
        out_shape=out_shape,
        scratch_shapes=[pltpu.VMEM((rows, width), BF16)],
        compiler_params=pltpu.CompilerParams(vmem_limit_bytes=ROOM),
    )(*args)


def attend_part(place, qt_ref, keys, values_t, at_ref, lse_ref, poll=None, between=None):
    rows = qt_ref.shape[1]

    def block(index, carry, diagonal):
        here = pl.ds(pl.multiple_of(index * rows, rows), rows)
        key = keys[here, :]
        value_t = values_t[:, here]
        out = []
        for head in range(HEADS_HERE):
            scores = dot(key, qt_ref[head * HD : (head + 1) * HD])
            if diagonal:
                below = lax.broadcasted_iota(jnp.int32, scores.shape, 0)
                across = lax.broadcasted_iota(jnp.int32, scores.shape, 1)
                scores = jnp.where(below <= across, scores, -1e30)
            peak = jnp.max(scores, axis=0, keepdims=True)
            if carry is not None:
                peak = jnp.maximum(peak, carry[head][0])
            weights = jnp.exp(scores - peak)
            total = jnp.sum(weights, axis=0, keepdims=True)
            mixed = dot(value_t, weights.astype(BF16))
            if carry is not None:
                fade = jnp.exp(carry[head][0] - peak)
                total = total + carry[head][1] * fade
                mixed = mixed + carry[head][2] * fade
            out.append((peak, total, mixed))
        return tuple(out)

    if poll:
        poll(0)
    carry = block(place, None, True)
    if between:
        between()

    def later(i, carry):
        if poll:
            poll(1 + i)
        return block(i, carry, False)

    carry = lax.fori_loop(0, place, later, carry)
    lse_ref[...] = jnp.zeros_like(lse_ref)
    for head in range(HEADS_HERE):
        peak, total, mixed = carry[head]
        at_ref[head * HD : (head + 1) * HD] = (mixed / total).astype(BF16)
        lse_ref[head : head + 1] = peak + jnp.log(total)
    at_ref[QW:] = jnp.zeros_like(at_ref[QW:])


def attend_kernel(qt_ref, kv_ref, at_ref, lse_ref, keys, values_t):
    @pl.when(pl.program_id(0) == 0)
    def _():
        keys[...] = kv_ref[:, :HD]
        values_t[...] = turn(kv_ref[...])[HD:].astype(BF16)

    attend_part(
        lax.axis_index("tensor"), qt_ref.at[0], keys, values_t, at_ref.at[0], lse_ref.at[0]
    )


def attend_call(qt, kv):
    tens, _, rows = qt.shape
    length = kv.shape[0]
    whole = pl.BlockSpec(memory_space=pltpu.VMEM)
    part = pl.BlockSpec((1, 256, rows), lambda t: (t, 0, 0))
    return pl.pallas_call(
        attend_kernel,
        grid=(tens,),
        in_specs=[part, whole],
        out_specs=[part, pl.BlockSpec((1, 8, rows), lambda t: (t, 0, 0))],
        out_shape=[
            jax.ShapeDtypeStruct((tens, 256, rows), BF16),
            jax.ShapeDtypeStruct((tens, 8, rows), F32),
        ],
        scratch_shapes=[pltpu.VMEM((length, HD), BF16), pltpu.VMEM((HD, length), BF16)],
        compiler_params=comm_params(None),
    )(qt, kv)


def mix_part(normed, at_ref, outward, upward, down, act_ref, slope_ref, poll=None):
    attended = turn(at_ref[:QW]).astype(BF16)
    step = 256
    parts = act_ref.shape[1] // step
    for part in range(parts):
        if poll:
            poll(part)
        cols = slice(part * step, (part + 1) * step)
        pre = dot(normed[...], upward(cols))
        cumulative, bell = gelu_parts(pre)
        act_ref[:, cols] = (pre * cumulative).astype(BF16)
        slope_ref[:, cols] = (cumulative + pre * bell).astype(BF16)
    if poll:
        poll(parts)
    return dot_nt(attended, outward()) + dot_nt(act_ref[...], down())


def mix_kernel(
    x_ref, norm_ref, at_ref, o_ref, up_ref, down_ref, out_ref, act_ref, slope_ref, normed, total
):
    t = pl.program_id(0)

    @pl.when(t == 0)
    def _():
        x = x_ref[...].astype(F32)
        normed[...] = normed_rows(x, norm_ref[2:3], norm_ref[3:4])
        total[...] = x

    total[...] += mix_part(
        normed, at_ref.at[0], lambda: o_ref[0, :, :QW], lambda cols: up_ref[0, :, cols],
        lambda: down_ref[0], act_ref.at[0], slope_ref.at[0],
    )

    @pl.when(t == pl.num_programs(0) - 1)
    def _():
        out_ref[...] = total[...]


def mix_call(x, norms, at, outward, feed):
    rows, width = x.shape
    tens = feed.shape[0]
    hidden = feed.shape[2] // 2
    whole = pl.BlockSpec(memory_space=pltpu.VMEM)
    wide = pl.BlockSpec((1, rows, hidden), lambda t: (t, 0, 0))
    return pl.pallas_call(
        mix_kernel,
        grid=(tens,),
        in_specs=[
            whole,
            whole,
            pl.BlockSpec((1, 256, rows), lambda t: (t, 0, 0)),
            pl.BlockSpec((1, width, 256), lambda t: (t, 0, 1)),
            pl.BlockSpec((1, width, hidden), lambda t: (t, 0, 0)),
            pl.BlockSpec((1, width, hidden), lambda t: (t, 0, 1)),
        ],
        out_specs=[whole, wide, wide],
        out_shape=[
            jax.ShapeDtypeStruct((rows, width), F32),
            jax.ShapeDtypeStruct((tens, rows, hidden), BF16),
            jax.ShapeDtypeStruct((tens, rows, hidden), BF16),
        ],
        scratch_shapes=[pltpu.VMEM((rows, width), BF16), pltpu.VMEM((rows, width), F32)],
        compiler_params=comm_params(None),
    )(x, norms, at, outward, feed, feed)


def mix_back_part(
    low, low_t, normed_t, at_ref, act_ref, slope_ref, outward, upward, down, dot_ref, pack_put,
    poll=None,
):
    hidden = act_ref.shape[1]
    if poll:
        poll(0)
    grad_attended = dot(low[...], outward())
    dot_ref[:QW] = turn(grad_attended).astype(BF16)
    dot_ref[QW:] = jnp.zeros_like(dot_ref[QW:])
    pack_put(2 * hidden, dot_nt(low_t[...], at_ref[...]).astype(BF16))
    if poll:
        poll(1)
    for start in range(0, hidden, 256):
        cols = slice(start, start + 256)
        pack_put(hidden + start, dot(low_t[...], act_ref[:, cols]).astype(BF16))
    if poll:
        poll(2)
    grad_pre = []
    for start in range(0, hidden, 256):
        cols = slice(start, start + 256)
        grad = (dot(low[...], down(cols)) * slope_ref[:, cols].astype(F32)).astype(BF16)
        pack_put(start, dot(normed_t[...], grad).astype(BF16))
        grad_pre.append(grad)
    if poll:
        poll(3)
    return dot_nt(jnp.concatenate(grad_pre, axis=1), upward())


def mix_back_start(gx_ref, x, norm_ref, low, low_t, normed_t):
    grad = gx_ref[...].astype(BF16)
    low[...] = grad
    low_t[...] = turn(grad).astype(BF16)
    normed_t[...] = turn(normed_rows(x, norm_ref[2:3], norm_ref[3:4])).astype(BF16)


def mix_back_kernel(
    gx_ref, x_ref, norm_ref, at_ref, act_ref, slope_ref, o_ref, up_ref, down_ref,
    pack_ref, dot_ref, mlp_ref, low, low_t, normed_t,
):
    @pl.when(pl.program_id(0) == 0)
    def _():
        mix_back_start(gx_ref, x_ref[...].astype(F32), norm_ref, low, low_t, normed_t)
        mlp_ref[...] = jnp.zeros_like(mlp_ref)

    def pack_put(start, value):
        pack_ref[0, :, start : start + value.shape[1]] = value

    mlp_ref[...] += mix_back_part(
        low, low_t, normed_t, at_ref.at[0], act_ref.at[0], slope_ref.at[0],
        lambda: o_ref[0, :, :QW], lambda: up_ref[0], lambda cols: down_ref[0, :, cols],
        dot_ref.at[0], pack_put,
    )


def mix_back_call(gx, x, norms, at, act, slope, outward, feed):
    rows, width = x.shape
    tens = feed.shape[0]
    hidden = act.shape[2]
    whole = pl.BlockSpec(memory_space=pltpu.VMEM)
    wide = pl.BlockSpec((1, rows, hidden), lambda t: (t, 0, 0))
    part = pl.BlockSpec((1, 256, rows), lambda t: (t, 0, 0))
    return pl.pallas_call(
        mix_back_kernel,
        grid=(tens,),
        in_specs=[
            whole,
            whole,
            whole,
            part,
            wide,
            wide,
            pl.BlockSpec((1, width, 256), lambda t: (t, 0, 1)),
            pl.BlockSpec((1, width, hidden), lambda t: (t, 0, 0)),
            pl.BlockSpec((1, width, hidden), lambda t: (t, 0, 1)),
        ],
        out_specs=[pl.BlockSpec((1, width, 2 * hidden + 256), lambda t: (t, 0, 0)), part, whole],
        out_shape=[
            jax.ShapeDtypeStruct((tens, width, 2 * hidden + 256), BF16),
            jax.ShapeDtypeStruct((tens, 256, rows), BF16),
            jax.ShapeDtypeStruct((rows, width), F32),
        ],
        scratch_shapes=[
            pltpu.VMEM((rows, width), BF16),
            pltpu.VMEM((width, rows), BF16),
            pltpu.VMEM((width, rows), BF16),
        ],
        compiler_params=comm_params(None),
    )(gx, x, norms, at, act, slope, outward, feed, feed)


def attend_back_start(kv, keys, values, keys_t):
    both_t = turn(kv)
    keys[...] = kv[:, :HD]
    keys_t[...] = both_t[:HD].astype(BF16)
    values[...] = turn(both_t[HD:]).astype(BF16)


def attend_back_part(
    place, qt_ref, dot_ref, at_ref, lse_ref, keys, values, keys_t, dkeys, dvalues, gqt_ref,
    cos, sin, poll=None,
):
    rows = qt_ref.shape[1]
    inner = []
    for head in range(HEADS_HERE):
        span = slice(head * HD, (head + 1) * HD)
        inner.append(
            jnp.sum(
                dot_ref[span].astype(F32) * at_ref[span].astype(F32), axis=0, keepdims=True
            )
        )

    def block(index, carry, diagonal):
        here = pl.ds(pl.multiple_of(index * rows, rows), rows)
        key = keys[here, :]
        value = values[here, :]
        key_t = keys_t[:, here]
        out = []
        dkey = dvalue = None
        for head in range(HEADS_HERE):
            span = slice(head * HD, (head + 1) * HD)
            query_t = qt_ref[span]
            grad_t = dot_ref[span]
            scores = dot(key, query_t)
            probs = jnp.exp(scores - lse_ref[head : head + 1])
            if diagonal:
                below = lax.broadcasted_iota(jnp.int32, scores.shape, 0)
                across = lax.broadcasted_iota(jnp.int32, scores.shape, 1)
                probs = jnp.where(below <= across, probs, 0.0)
            grad_probs = dot(value, grad_t)
            grad_scores = (probs * (grad_probs - inner[head])).astype(BF16)
            part_v = dot_nt(probs.astype(BF16), grad_t)
            part_k = dot_nt(grad_scores, query_t)
            dkey = part_k if head == 0 else dkey + part_k
            dvalue = part_v if head == 0 else dvalue + part_v
            part_q = dot(key_t, grad_scores)
            out.append(part_q if carry is None else carry[head] + part_q)
        dkeys[here, :] += dkey
        dvalues[here, :] += dvalue
        return tuple(out)

    def later(i, carry):
        if poll:
            poll(1 + i)
        return block(i, carry, False)

    if poll:
        poll(0)
    carry = block(place, None, True)
    carry = lax.fori_loop(0, place, later, carry)
    for head in range(HEADS_HERE):
        base = head * HD
        grad = carry[head] * SCALE
        gqt_ref[base : base + ROT] = rotated(grad[:ROT], cos, -sin).astype(BF16)
        gqt_ref[base + ROT : base + HD] = grad[ROT:].astype(BF16)
    gqt_ref[QW:] = jnp.zeros_like(gqt_ref[QW:])


def attend_back_kernel(start_given, *refs):
    refs = Refs(refs)
    qt_ref, dot_ref, at_ref, lse_ref, kv_ref, trig_ref = refs.take(6)
    before_ref = refs.take(1)[0] if start_given else None
    gqt_ref, dkv_ref, keys, values, keys_t, dkeys, dvalues = refs.take(7)
    t = pl.program_id(0)
    rows = qt_ref.shape[2]

    @pl.when(t == 0)
    def _():
        attend_back_start(kv_ref[...], keys, values, keys_t)
        dkeys[...] = jnp.zeros_like(dkeys)
        dvalues[...] = jnp.zeros_like(dvalues)

    attend_back_part(
        lax.axis_index("tensor"), qt_ref.at[0], dot_ref.at[0], at_ref.at[0], lse_ref.at[0],
        keys, values, keys_t, dkeys, dvalues, gqt_ref.at[0],
        trig_ref[0:HALF], trig_ref[HALF:ROT],
    )

    @pl.when(t == pl.num_programs(0) - 1)
    def _():
        both = jnp.concatenate([turn(dkeys[...]), turn(dvalues[...])], axis=0)
        for part in range(dkv_ref.shape[0]):
            piece = both[:, part * rows : (part + 1) * rows]
            if start_given:
                piece = piece + before_ref[part]
            dkv_ref[part] = piece


def attend_back_call(qt, dout, at, lse, kv, trig, before=None):
    tens, _, rows = qt.shape
    length = kv.shape[0]
    whole = pl.BlockSpec(memory_space=pltpu.VMEM)
    part = pl.BlockSpec((1, 256, rows), lambda t: (t, 0, 0))
    args = [qt, dout, at, lse, kv, trig]
    in_specs = [part, part, part, pl.BlockSpec((1, 8, rows), lambda t: (t, 0, 0)), whole, whole]
    if before is not None:
        args.append(before)
        in_specs.append(whole)
    return pl.pallas_call(
        functools.partial(attend_back_kernel, before is not None),
        grid=(tens,),
        in_specs=in_specs,
        out_specs=[part, whole],
        out_shape=[
            jax.ShapeDtypeStruct((tens, 256, rows), BF16),
            jax.ShapeDtypeStruct((length // rows, 2 * HD, rows), F32),
        ],
        scratch_shapes=[
            pltpu.VMEM((length, HD), BF16),
            pltpu.VMEM((length, HD), BF16),
            pltpu.VMEM((HD, length), BF16),
            pltpu.VMEM((length, HD), F32),
            pltpu.VMEM((length, HD), F32),
        ],
        compiler_params=comm_params(None),
    )(*args)


def shared_rows(grad, cos, sin, shared):
    shared[:ROT] = rotated(grad[:ROT], cos, -sin).astype(BF16)
    shared[ROT:] = grad[ROT:].astype(BF16)


def shared_back(shared, key_weight, value_weight):
    return dot_nt(turn(shared[:HD]).astype(BF16), key_weight) + dot_nt(
        turn(shared[HD:]).astype(BF16), value_weight
    )


def right_columns(shared, normed_t, sums, other):
    pad = jnp.zeros((HD, sums.shape[1]), F32)
    lower = turn(jnp.concatenate([pad, sums, other, pad[8:]], axis=0))
    upper = jnp.concatenate([shared[HD:], jnp.zeros_like(shared[HD:])], axis=0)
    return (dot_nt(normed_t[...], upper) + lower).astype(BF16)


def norm_back(x, attn_grad, mlp_grad, norm_ref):
    unit, inverse = standard(x)
    sums = jnp.concatenate(
        [
            jnp.sum(attn_grad * unit, axis=0, keepdims=True),
            jnp.sum(attn_grad, axis=0, keepdims=True),
            jnp.sum(mlp_grad * unit, axis=0, keepdims=True),
            jnp.sum(mlp_grad, axis=0, keepdims=True),
        ],
        axis=0,
    )
    grad = attn_grad * norm_ref[0:1] + mlp_grad * norm_ref[2:3]
    mean = jnp.mean(grad, axis=-1, keepdims=True)
    slant = jnp.mean(grad * unit, axis=-1, keepdims=True)
    return sums, inverse * (grad - mean - unit * slant)


def norm_back_kernel(first, gx_ref, x_ref, norm_ref, mlp_ref, gqt_ref, qk_ref, *rest):
    if first:
        ov_ref, dkv_ref, trig_ref, other_ref, out_ref, pack_ref, normed_t, attn, shared = rest
    else:
        out_ref, pack_ref, sums_ref, normed_t, attn = rest
    t = pl.program_id(0)

    @pl.when(t == 0)
    def _():
        x = x_ref[...].astype(F32)
        normed = (standard(x)[0] * norm_ref[0:1] + norm_ref[1:2]).astype(BF16)
        normed_t[...] = turn(normed).astype(BF16)
        if first:
            cos, sin = trig_ref[0:HALF], trig_ref[HALF:ROT]
            shared_rows(dkv_ref[...], cos, sin, shared)
            attn[...] = shared_back(shared, qk_ref[0, :, QW:], ov_ref[0, :, QW:])
        else:
            attn[...] = jnp.zeros_like(attn)

    grad_t = gqt_ref[0, :QW]
    attn[...] += dot_nt(turn(grad_t).astype(BF16), qk_ref[0, :, :QW])
    if first:
        left = jnp.concatenate([grad_t, shared[:HD]], axis=0)
        pack_ref[t, :, :256] = dot_nt(normed_t[...], left).astype(BF16)
    else:
        pack_ref[0] = dot_nt(normed_t[...], gqt_ref[0]).astype(BF16)

    @pl.when(t == pl.num_programs(0) - 1)
    def _():
        sums, change = norm_back(x_ref[...].astype(F32), attn[...], mlp_ref[...], norm_ref)
        if first:
            right = right_columns(shared, normed_t, sums, other_ref[...])
            for part in range(pack_ref.shape[0]):
                pack_ref[part, :, 256:] = right
        else:
            sums_ref[...] = sums
        out_ref[...] = gx_ref[...] + change


def norm_back_call(first, gx, x, norms, mlp, gqt, weights, dkv=None, trig=None, other=None):
    rows, width = x.shape
    tens = weights.shape[0]
    whole = pl.BlockSpec(memory_space=pltpu.VMEM)
    part = pl.BlockSpec((1, 256, rows), lambda t: (t, 0, 0))
    args = [gx, x, norms, mlp, gqt, weights]
    in_specs = [whole] * 4 + [part, pl.BlockSpec((1, width, 256), lambda t: (t, 0, 0))]
    scratch = [pltpu.VMEM((width, rows), BF16), pltpu.VMEM((rows, width), F32)]
    out_shape = [jax.ShapeDtypeStruct((rows, width), F32)]
    if first:
        args += [weights, dkv, trig, other]
        in_specs += [pl.BlockSpec((1, width, 256), lambda t: (0, 0, 1)), whole, whole, whole]
        scratch.append(pltpu.VMEM((2 * HD, rows), BF16))
        out_shape.append(jax.ShapeDtypeStruct((tens, width, 384), BF16))
        out_specs = [whole, whole]
    else:
        out_shape.append(jax.ShapeDtypeStruct((tens, width, 256), BF16))
        out_shape.append(jax.ShapeDtypeStruct((4, width), F32))
        out_specs = [whole, pl.BlockSpec((1, width, 256), lambda t: (t, 0, 0)), whole]
    return pl.pallas_call(
        functools.partial(norm_back_kernel, first),
        grid=(tens,),
        in_specs=in_specs,
        out_specs=out_specs,
        out_shape=out_shape,
        scratch_shapes=scratch,
        compiler_params=comm_params(None),
    )(*args)


def forward_kernel(*refs):
    refs = Refs(refs)
    x_ref, trig_ref, small_ref = refs.take(3)
    sources = refs.take(4)
    norm_ref, kv_out, state_out, act_out, slope_out = refs.take(5)
    qt_outs, at_outs, lse_outs = refs.take(2), refs.take(2), refs.take(2)
    packs = refs.take(4)
    own_sem, send, recv = refs.take(3)
    small_land, small_own, small_send, small_recv = refs.take(4)
    kv_here, landed, kv_send, kv_recv = refs.take(4)
    narrow, wide, load_sem = refs.take(3)
    normed, total, qt, at, lse, act, slope, keys, values_t, save_sem = refs.take(10)

    me = Place()
    place = me.tensor
    tens, rows = qt.shape[1], qt.shape[3]
    width = total.shape[1]
    hidden = act.shape[2]
    gathers = [
        Gather(me, sources[k], packs[k], own_sem.at[k], send.at[k], recv.at[k]) for k in range(4)
    ]
    steps = [gather.steps() for gather in gathers]
    mine = small_land.at[me.z, me.x]
    small_mine = pltpu.make_async_copy(small_ref, mine, small_own)
    small_along = [
        remote(small_ref, mine, small_send.at[d], small_recv.at[d], me.at(z=me.along(d)))
        for d in (1, 2, 3)
    ]
    column = small_land.at[:, me.x]
    small_across = remote(column, column, small_send.at[0], small_recv.at[0], me.to_x)
    kv_copies = [
        remote(kv_here, landed.at[place], kv_send.at[k], kv_recv.at[k], peer)
        for k, peer in enumerate((me.to_core, me.to_y, me.to_corner))
    ]
    saves = []

    def save(src, dst):
        copy = pltpu.make_async_copy(src, dst, save_sem.at[len(saves)])
        copy.start()
        saves.append(copy)

    def load(k, buffer, slot):
        return [
            pltpu.make_async_copy(packs[k].at[t], buffer.at[t], load_sem.at[slot, t])
            for t in range(tens)
        ]

    def joined(buffer, t, cols):
        value = buffer[t, :, :, :, cols]
        return value.reshape(width, value.shape[-1])

    me.greet(corner=True)
    small_mine.start()
    for copy in small_along:
        copy.start()
    gathers[0].begin()
    x = x_ref[...].astype(F32)
    total[...] = standard(x)[0]
    small_mine.wait()
    for copy in small_along:
        copy.wait_recv()
    small_across.start()
    for step in steps[0][:6]:
        step()
    gathers[1].begin()
    small_across.wait_recv()
    norm_ref[...] = turn(small_land[...].reshape(width, 128))[:8]
    normed[...] = (total[...] * norm_ref[0:1] + norm_ref[1:2]).astype(BF16)
    for step in steps[0][6:]:
        step()
    gathers[0].arrive()
    loads = load(0, narrow.at[0], 0)
    for copy in loads:
        copy.start()
    for copy in small_along + [small_across]:
        copy.wait_send()
    gathers[0].end()

    cos, sin = trig_ref[0:HALF], trig_ref[HALF:ROT]

    def qkv(layer):
        def one(t, _):
            lin = turn(dot(normed[...], joined(narrow.at[layer], t, slice(0, 256))))
            put_query(lin, cos, sin, qt.at[layer, t])
            if layer == 0:

                @pl.when(t == 0)
                def _():
                    value = turn(dot(normed[...], joined(narrow.at[0], 0, slice(384, 512))))
                    kv_here[...] = keyval_rows(lin, value[HD:], cos, sin)
                    for copy in kv_copies:
                        copy.start()

            return 0

        lax.fori_loop(0, tens, one, 0)

    def attention(layer, steps, between=None):
        def one(t, _):
            def first():
                if between:
                    pl.when(t == 0)(between)

            attend_part(
                place, qt.at[layer, t], keys, values_t, at.at[layer, t], lse.at[layer, t],
                lambda i: spread(steps, t * (place + 1) + i, tens * (place + 1)), first,
            )
            return 0

        lax.fori_loop(0, tens, one, 0)
        save(qt.at[layer], qt_outs[layer])
        save(at.at[layer], at_outs[layer])
        save(lse.at[layer], lse_outs[layer])

    for copy in loads:
        copy.wait()
    qkv(0)
    here = pl.ds(pl.multiple_of(place * rows, rows), rows)
    landed[place] = kv_here[...]
    keys[here, :] = kv_here[:, :HD]
    values_t[:, here] = turn(kv_here[...])[HD:].astype(BF16)

    def meet():
        for copy in kv_copies:
            copy.wait()
        for part in range(tens):
            span = pl.ds(part * rows, rows)
            keys[span, :] = landed[part, :, :HD]
            values_t[:, span] = turn(landed[part])[HD:].astype(BF16)

    def turn_over():
        steps[1][5]()
        gathers[2].begin()

    attention(0, steps[1][:5] + [turn_over], meet)
    save(landed, kv_out)
    for step in steps[1][6:]:
        step()
    gathers[1].arrive()
    loads = load(1, wide, 1)
    for copy in loads:
        copy.start()
    gathers[1].end()
    x = x_ref[...].astype(F32)
    normed[...] = normed_rows(x, norm_ref[2:3], norm_ref[3:4])
    total[...] = x
    for copy in loads:
        copy.wait()

    def next_over():
        steps[2][5]()
        gathers[3].begin()

    mix_steps = steps[2][:5] + [next_over] + steps[2][6:]

    def mix(t, _):
        total[...] += mix_part(
            normed, at.at[0, t], lambda: joined(narrow.at[0], t, slice(256, 256 + QW)),
            lambda cols: joined(wide, t, cols),
            lambda: joined(wide, t, slice(hidden, 2 * hidden)), act.at[t], slope.at[t],
            lambda i: spread(mix_steps, t * 4 + i, tens * 4),
        )
        return 0

    lax.fori_loop(0, tens, mix, 0)
    save(total, state_out)
    save(act, act_out)
    save(slope, slope_out)
    gathers[2].arrive()
    loads = load(2, narrow.at[1], 2)
    for copy in loads:
        copy.start()
    gathers[2].end()
    normed[...] = normed_rows(total[...], norm_ref[4:5], norm_ref[5:6])
    for copy in loads:
        copy.wait()
    qkv(1)
    attention(1, steps[3])
    gathers[3].arrive()
    gathers[3].end()
    for copy in saves:
        copy.wait()


def forward_call(x, trig, small, packs):
    rows, width = x.shape
    tens = 4
    depth = packs[0].shape[0]
    hidden = packs[1].shape[1] // 2
    vmem = pl.BlockSpec(memory_space=pltpu.VMEM)
    anywhere = pl.BlockSpec(memory_space=pl.ANY)
    heads = jax.ShapeDtypeStruct((tens, 256, rows), BF16)
    sums = jax.ShapeDtypeStruct((tens, 8, rows), F32)
    feed = jax.ShapeDtypeStruct((tens, rows, hidden), BF16)
    out_shape = [
        jax.ShapeDtypeStruct((8, width), F32),
        jax.ShapeDtypeStruct((tens, rows, 2 * HD), BF16),
        jax.ShapeDtypeStruct((rows, width), F32),
        feed,
        feed,
        heads,
        heads,
        heads,
        heads,
        sums,
        sums,
    ] + [jax.ShapeDtypeStruct((4, 4, 2) + pack.shape, BF16) for pack in packs]
    return pl.pallas_call(
        forward_kernel,
        in_specs=[vmem, vmem] + [anywhere] * 5,
        out_specs=[vmem] + [anywhere] * (len(out_shape) - 1),
        out_shape=out_shape,
        scratch_shapes=[
            pltpu.SemaphoreType.DMA((4,)),
            pltpu.SemaphoreType.DMA((4, Gather.COUNT)),
            pltpu.SemaphoreType.DMA((4, Gather.COUNT)),
            pltpu.VMEM((4, 2) + small.shape, BF16),
            pltpu.SemaphoreType.DMA,
            pltpu.SemaphoreType.DMA((4,)),
            pltpu.SemaphoreType.DMA((4,)),
            pltpu.VMEM((rows, 2 * HD), BF16),
            pltpu.VMEM((tens, rows, 2 * HD), BF16),
            pltpu.SemaphoreType.DMA((3,)),
            pltpu.SemaphoreType.DMA((3,)),
            pltpu.VMEM((2, tens, 4, 2, depth, 512), BF16),
            pltpu.VMEM((tens, 4, 2, depth, 2 * hidden), BF16),
            pltpu.SemaphoreType.DMA((3, tens)),
            pltpu.VMEM((rows, width), BF16),
            pltpu.VMEM((rows, width), F32),
            pltpu.VMEM((2, tens, 256, rows), BF16),
            pltpu.VMEM((2, tens, 256, rows), BF16),
            pltpu.VMEM((2, tens, 8, rows), F32),
            pltpu.VMEM((tens, rows, hidden), BF16),
            pltpu.VMEM((tens, rows, hidden), BF16),
            pltpu.VMEM((tens * rows, HD), BF16),
            pltpu.VMEM((HD, tens * rows), BF16),
            pltpu.SemaphoreType.DMA((10,)),
        ],
        compiler_params=comm_params(1),
    )(x, trig, small, *packs)


EARLY_TIMES = (40, 70, 100, 130, 190, 220, 320, 350, 360, 450, 470, 520, 590)
LATE_TIMES = (500, 510, 515, 520, 530, 540, 550, 555, 560, 570, 580, 590, 640)


def backward_kernel(*refs):
    refs = Refs(refs)
    norm_ref, trig_ref, kv_ref, x0_ref, early1 = refs.take(5)
    gx_in, x1_in, mlp_in = refs.take(3)
    qt_in, at_in, lse_in, dot_in = refs.take(2), refs.take(2), refs.take(2), refs.take(1)[0]
    act_in, slope_in = refs.take(2)
    narrow0, narrow1, wide0 = refs.take(3)
    early_out, late1_out = refs.take(2), refs.take(1)[0]
    grad_out, late0_out, early0 = refs.take(3)
    early_scratch, late_scratch = refs.take(10), refs.take(10)
    free_sem = refs.take(1)[0]
    gx, x1, mlp, attn = refs.take(4)
    qt, at, lse, dout, gqt = refs.take(5)
    keys, values, keys_t, dkeys, dvalues = refs.take(5)
    low, low_t, normed_t = refs.take(3)
    narrow, wide, act, slope = refs.take(4)
    staging, late1, late0, right_ref, shared, other = refs.take(6)
    merge_low, merge_land, merged, merge_send, merge_recv = refs.take(5)
    in_sem, narrow_sem, feed_sem, stage_sem, late_sem = refs.take(5)

    me = Place()
    place = me.tensor
    tens, rows = qt.shape[0], qt.shape[2]
    width = gx.shape[1]
    hidden = act.shape[2]
    cos, sin = trig_ref[0:HALF], trig_ref[HALF:ROT]
    norms0, norms1 = norm_ref.at[0:4], norm_ref.at[4:8]

    def joined(ref, cols):
        value = ref[:, :, :, cols]
        return value.reshape(width, value.shape[-1])

    def put(ref, start, value):
        cols = value.shape[1]
        ref[:, :, :, start : start + cols] = value.reshape(ref.shape[:3] + (cols,))

    def copies_of(pairs, sem):
        return [
            pltpu.make_async_copy(src, dst, sem.at[k]) for k, (src, dst) in enumerate(pairs)
        ]

    scatter1 = Scatter(me, early1, early_out[1], *early_scratch)
    scatter0 = Scatter(me, early0, early_out[0], *early_scratch)
    scatter_late = Scatter(me, late1, late1_out, *late_scratch)
    steps1 = list(zip(EARLY_TIMES, scatter1.steps())) + list(zip(LATE_TIMES, scatter_late.steps()))
    steps1.sort(key=lambda entry: entry[0])
    steps0 = list(zip(EARLY_TIMES, scatter0.steps()))

    loads = copies_of(
        [
            (qt_in[1], qt), (at_in[1], at), (lse_in[1], lse), (dot_in, dout), (gx_in, gx),
            (x1_in, x1), (mlp_in, mlp),
        ],
        in_sem,
    )
    narrow_loads = copies_of([(narrow1.at[t], narrow.at[t]) for t in range(tens)], narrow_sem)
    for copy in loads + narrow_loads:
        copy.start()
    me.greet(corner=True)
    scatter1.begin()
    attend_back_start(kv_ref[...], keys, values, keys_t)
    dkeys[...] = jnp.zeros_like(dkeys)
    dvalues[...] = jnp.zeros_like(dvalues)
    for copy in loads[:4]:
        copy.wait()

    def attention(steps, span):
        def one(t, _):
            attend_back_part(
                place, qt.at[t], dout.at[t], at.at[t], lse.at[t], keys, values, keys_t,
                dkeys, dvalues, gqt.at[t], cos, sin,
                lambda i: timed(steps, (t * (place + 1) + i) * span, span),
            )
            return 0

        lax.fori_loop(0, tens, one, 0)
        return tens * (place + 1) * span

    now = attention(steps1, 24)
    seconds = copies_of([(qt_in[0], qt), (at_in[0], at), (lse_in[0], lse)], in_sem)
    for copy in loads[4:]:
        copy.wait()
    for copy in seconds:
        copy.start()

    normed_t[...] = turn(normed_rows(x1[...], norms1[0:1], norms1[1:2])).astype(BF16)
    attn[...] = jnp.zeros_like(attn)
    for copy in narrow_loads:
        copy.wait()

    def second(t, _):
        timed(steps1, now + t * 20, 20)
        attn[...] += dot_nt(
            turn(gqt[t, :QW]).astype(BF16), joined(narrow.at[t], slice(0, QW))
        )
        put(late1.at[t], 0, dot_nt(normed_t[...], gqt[t]).astype(BF16))
        return 0

    lax.fori_loop(0, tens, second, 0)
    now = now + tens * 20
    narrow_loads = copies_of([(narrow0.at[t], narrow.at[t]) for t in range(tens)], narrow_sem)
    for copy in narrow_loads:
        copy.start()
    scatter_late.begin()
    sums, change = norm_back(x1[...], attn[...], mlp[...], norms1)
    other[...] = sums
    gx[...] += change

    def feed(t, slot):
        return copies_of(
            [(wide0.at[t], wide.at[slot]), (act_in.at[t], act.at[slot]),
             (slope_in.at[t], slope.at[slot])],
            feed_sem.at[slot],
        )

    for copy in feed(0, 0):
        copy.start()
    mix_back_start(gx, x0_ref[...].astype(F32), norms0, low, low_t, normed_t)
    mlp[...] = jnp.zeros_like(mlp)
    for copy in narrow_loads + seconds:
        copy.wait()
    base = now

    def third(t, _):
        slot = lax.rem(t, 2)

        @pl.when(t + 1 < tens)
        def _():
            for copy in feed(t + 1, 1 - slot):
                copy.start()

        for copy in feed(t, slot):
            copy.wait()
        saved = pltpu.make_async_copy(staging, early0.at[t], stage_sem)

        @pl.when(t > 0)
        def _():
            saved.wait()

        def poll(part):
            timed(steps1, base + (t * 4 + part) * 12, 12)

        mlp[...] += mix_back_part(
            low, low_t, normed_t, at.at[t], act.at[slot], slope.at[slot],
            lambda: joined(narrow.at[t], slice(256, 256 + QW)),
            lambda: joined(wide.at[slot], slice(0, hidden)),
            lambda cols: joined(wide.at[slot], slice(hidden + cols.start, hidden + cols.stop)),
            dout.at[t], functools.partial(put, staging), poll,
        )
        saved.start()
        return 0

    lax.fori_loop(0, tens, third, 0)
    now = base + tens * 48
    timed(steps1, now, 10000)
    for peer in (me.to_x, me.to_y, me.to_core):
        pl.semaphore_signal(free_sem, inc=1, device_id=peer, device_id_type=MESH)
    for shift in (1, 2, 3):
        pl.semaphore_signal(
            free_sem, inc=1, device_id=me.at(z=me.along(shift)), device_id_type=MESH
        )
    pltpu.make_async_copy(staging, early0.at[0], stage_sem).wait()
    pl.semaphore_wait(free_sem, 6)
    scatter0.begin()

    now = attention(steps0, 24)
    for part in range(tens):
        span = slice(part * rows, (part + 1) * rows)
        piece = jnp.concatenate([turn(dkeys[span]), turn(dvalues[span])], axis=0)
        merge_low[part] = piece.astype(BF16)

        @pl.when(place == part)
        def _(piece=piece):
            merged[...] = piece

    merges = [
        remote(merge_low.at[peer[1]], merge_land.at[k], merge_send.at[k], merge_recv.at[k], peer)
        for k, peer in enumerate((me.to_core, me.to_y, me.to_corner))
    ]
    for copy in merges:
        copy.start()
    normed_t[...] = turn(
        normed_rows(x0_ref[...].astype(F32), norms0[0:1], norms0[1:2])
    ).astype(BF16)
    longest = 4 * tens * 24
    timed(steps0, now, longest - now)
    now = longest
    for copy in merges:
        copy.wait_recv()
    merged[...] += (
        merge_land[0].astype(F32) + merge_land[1].astype(F32) + merge_land[2].astype(F32)
    )
    shared_rows(merged[...], cos, sin, shared)
    attn[...] = shared_back(
        shared, joined(narrow.at[0], slice(QW, 256)), joined(narrow.at[0], slice(256 + QW, 512))
    )

    def fourth(t, _):
        timed(steps0, now + t * 20, 20)
        grad_t = gqt[t, :QW]
        attn[...] += dot_nt(turn(grad_t).astype(BF16), joined(narrow.at[t], slice(0, QW)))
        left = jnp.concatenate([grad_t, shared[:HD]], axis=0)
        saved = pltpu.make_async_copy(late0, late0_out.at[t, :, :, :, 0:256], late_sem.at[0])

        @pl.when(t > 0)
        def _():
            saved.wait()

        put(late0, 0, dot_nt(normed_t[...], left).astype(BF16))
        saved.start()
        return 0

    lax.fori_loop(0, tens, fourth, 0)
    now = now + tens * 20
    sums, change = norm_back(x0_ref[...].astype(F32), attn[...], mlp[...], norms0)
    gx[...] += change
    put(right_ref, 0, right_columns(shared, normed_t, sums, other[...]))
    saves = [pltpu.make_async_copy(late0, late0_out.at[0, :, :, :, 0:256], late_sem.at[0])]
    for t in range(tens):
        saves.append(
            pltpu.make_async_copy(
                right_ref, late0_out.at[t, :, :, :, 256:384], late_sem.at[1 + t]
            )
        )
        saves[-1].start()
    saves.append(pltpu.make_async_copy(gx, grad_out, late_sem.at[1 + tens]))
    saves[-1].start()
    timed(steps0, now, 10000)
    for copy in saves:
        copy.wait()
    for copy in merges:
        copy.wait_send()


def backward_call(norms, trig, kv, x0, early1, gx, x1, mlp, qts, ats, lses, dout, act, slope, weights):
    rows, width = x0.shape
    tens = qts[0].shape[0]
    length = kv.shape[0]
    hidden = act.shape[2]
    depth = width // 8
    early1 = blocks_of(early1)
    early_cols = early1.shape[4]
    weights = [blocks_of(pack) for pack in weights]
    vmem = pl.BlockSpec(memory_space=pltpu.VMEM)
    anywhere = pl.BlockSpec(memory_space=pl.ANY)
    heads = pltpu.VMEM((tens, 256, rows), BF16)
    state = pltpu.VMEM((rows, width), F32)
    args = [norms, trig, kv, x0, early1, gx, x1, mlp, *qts, *ats, *lses, dout, act, slope, *weights]
    return pl.pallas_call(
        backward_kernel,
        in_specs=[vmem] * 4 + [anywhere] * (len(args) - 4),
        out_specs=[vmem, vmem, vmem] + [anywhere] * 3,
        out_shape=[
            jax.ShapeDtypeStruct((depth, early_cols), F32),
            jax.ShapeDtypeStruct((depth, early_cols), F32),
            jax.ShapeDtypeStruct((depth, 256), F32),
            jax.ShapeDtypeStruct((rows, width), F32),
            jax.ShapeDtypeStruct((tens, 4, 2, depth, 384), BF16),
            jax.ShapeDtypeStruct((tens, 4, 2, depth, early_cols), BF16),
        ],
        scratch_shapes=Scatter.scratch(depth, early_cols)
        + Scatter.scratch(depth, 256)
        + [
            pltpu.SemaphoreType.REGULAR,
            state,
            state,
            state,
            state,
            heads,
            heads,
            pltpu.VMEM((tens, 8, rows), F32),
            heads,
            heads,
            pltpu.VMEM((length, HD), BF16),
            pltpu.VMEM((length, HD), BF16),
            pltpu.VMEM((HD, length), BF16),
            pltpu.VMEM((length, HD), F32),
            pltpu.VMEM((length, HD), F32),
            pltpu.VMEM((rows, width), BF16),
            pltpu.VMEM((width, rows), BF16),
            pltpu.VMEM((width, rows), BF16),
            pltpu.VMEM((tens, 4, 2, depth, 512), BF16),
            pltpu.VMEM((2, 4, 2, depth, 2 * hidden), BF16),
            pltpu.VMEM((2, rows, hidden), BF16),
            pltpu.VMEM((2, rows, hidden), BF16),
            pltpu.VMEM((4, 2, depth, early_cols), BF16),
            pltpu.VMEM((tens, 4, 2, depth, 256), BF16),
            pltpu.VMEM((4, 2, depth, 256), BF16),
            pltpu.VMEM((4, 2, depth, 128), BF16),
            pltpu.VMEM((2 * HD, rows), BF16),
            pltpu.VMEM((4, width), F32),
            pltpu.VMEM((tens, 2 * HD, rows), BF16),
            pltpu.VMEM((3, 2 * HD, rows), BF16),
            pltpu.VMEM((2 * HD, rows), F32),
            pltpu.SemaphoreType.DMA((3,)),
            pltpu.SemaphoreType.DMA((3,)),
            pltpu.SemaphoreType.DMA((7,)),
            pltpu.SemaphoreType.DMA((tens,)),
            pltpu.SemaphoreType.DMA((2, 3)),
            pltpu.SemaphoreType.DMA,
            pltpu.SemaphoreType.DMA((tens + 2,)),
        ],
        compiler_params=comm_params(5),
    )(*args)


def lamb_parts(weight, first, second, grad):
    first_new = BETA_FIRST * first + (1.0 - BETA_FIRST) * grad
    second_new = BETA_SECOND * second + (1.0 - BETA_SECOND) * grad * grad
    update = (
        first_new
        / (1.0 - BETA_FIRST**STEP)
        / (jnp.sqrt(second_new / (1.0 - BETA_SECOND**STEP)) + ADAM_EPSILON)
        + WEIGHT_DECAY * weight
    )
    return (first_new, second_new, update)


def keyval_grad(late):
    lane = lax.broadcasted_iota(jnp.int32, (late.shape[0], 2 * HD), 1)
    left = pltpu.roll(late[:, 128:256], HD, 1)
    right = pltpu.roll(late[:, 256:384], HD, 1)
    return jnp.where(lane < HD, left, right)


def norm_grad(late):
    return turn(late[:, 256:384])[HD : HD + 8]


def square(value):
    total = jnp.sum(value * value, axis=1, keepdims=True)
    return jnp.sum(total, axis=0, keepdims=True)


def lanes(pairs):
    lane = lax.broadcasted_iota(jnp.int32, (1, 128), 1)
    row = jnp.zeros((1, 128), F32)
    for place, value in pairs:
        row = jnp.where(lane == place, value, row)
    return row


class Tensors:
    def __init__(self, refs, early, late):
        self.refs = refs
        self.early, self.late = early, late

    def early_grad(self, layer, which):
        pack = self.early[layer]
        hidden = (pack.shape[1] - 256) // 2
        if which == "up":
            return pack[:, :hidden]
        if which == "down":
            return turn(pack[:, hidden : 2 * hidden])
        return turn(pack[:, 2 * hidden :])[:QW]

    def parts(self, array, index, grad):
        weight, first, second = (ref[...] if index is None else ref[index] for ref in array)
        return (weight,) + lamb_parts(weight, first, second, grad)

    def each(self, late0):
        query, keyval, output, upward, downward, norms = range(6)
        for layer in range(2):
            yield 5 + layer, upward, layer, lambda: self.early_grad(layer, "up")
            yield 7 + layer, downward, layer, lambda: self.early_grad(layer, "down")
            yield 3 + layer, output, layer, lambda: self.early_grad(layer, "output")
        yield 1, query, 1, lambda: self.late[1][:, :QW]
        yield 0, query, 0, lambda: late0()[:, :QW]
        yield 2, keyval, None, lambda: keyval_grad(late0())
        for layer in range(2):
            yield 9 + 4 * layer, norms, layer, lambda: norm_grad(late0())[4 * layer : 4 * layer + 4]


def norms_kernel(*refs):
    refs = Refs(refs)
    parts_ref, early0, early1, late1 = refs.take(4)
    arrays = [refs.take(3) for _ in range(6)]
    late0_ref, sums_ref = refs.take(2)
    scatter_refs = refs.take(10)
    near_land, along_land, send, recv = refs.take(4)
    me = Place()
    scatter = Scatter(me, parts_ref, late0_ref, *scatter_refs)
    steps = scatter.steps()
    me.greet(near=True)
    scatter.begin()
    tensors = Tensors(arrays, (early0, early1), (None, late1))
    leader = (me.tensor == 0).astype(F32)
    old, new = [], []

    def late0():
        return late0_ref[...]

    waiting = list(steps[:-1])
    for place, array, index, grad in tensors.each(late0):
        if place == 0:
            for step in waiting:
                step()
            scatter.end()
        elif place != 2 and place < 9 and place != 1 and waiting:
            waiting.pop(0)()
            waiting.pop(0)()
        weight, _, _, update = tensors.parts(arrays[array], index, grad())
        if place >= 9:
            for row in range(4):
                old.append((place + row, square(weight[row : row + 1]) * leader))
                new.append((place + row, square(update[row : row + 1]) * leader))
        else:
            scale = leader if place == 2 else 1.0
            old.append((place, square(weight) * scale))
            new.append((place, square(update) * scale))

    near_land[0] = jnp.concatenate([lanes(old), lanes(new), jnp.zeros((6, 128), F32)], axis=0)
    copies = []
    for code, peer in me.near():
        copies.append(
            remote(near_land.at[0], near_land.at[code], send.at[code], recv.at[code], peer)
        )
        copies[-1].start()
    for copy in copies:
        copy.wait()
    total = jnp.zeros((8, 128), F32)
    for x in range(2):
        for y in range(2):
            for core in range(2):
                code = lax.rem(x + me.x, 2) * 4 + lax.rem(y + me.y, 2) * 2
                total = total + near_land[code + lax.rem(core + me.core, 2)]
    along_land[0] = total
    copies = []
    for shift in (1, 2, 3):
        copies.append(
            remote(
                along_land.at[0], along_land.at[shift], send.at[7 + shift],
                recv.at[7 + shift], me.at(z=me.along(shift)),
            )
        )
        copies[-1].start()
    for copy in copies:
        copy.wait()
    total = jnp.zeros((8, 128), F32)
    for z in range(4):
        total = total + along_land[me.along(4 - z)]
    sums_ref[...] = total


def norms_call(parts, early, late1, arrays):
    parts = blocks_of(parts)
    rows, cols = parts.shape[3:]
    vmem = pl.BlockSpec(memory_space=pltpu.VMEM)
    flat = [ref for array in arrays for ref in array]
    return pl.pallas_call(
        norms_kernel,
        in_specs=[pl.BlockSpec(memory_space=pl.ANY)] + [vmem] * (3 + len(flat)),
        out_specs=[vmem, vmem],
        out_shape=[
            jax.ShapeDtypeStruct((rows, cols), F32),
            jax.ShapeDtypeStruct((8, 128), F32),
        ],
        scratch_shapes=Scatter.scratch(rows, cols)
        + [
            pltpu.VMEM((8, 8, 128), F32),
            pltpu.VMEM((4, 8, 128), F32),
            pltpu.SemaphoreType.DMA((11,)),
            pltpu.SemaphoreType.DMA((11,)),
        ],
        compiler_params=comm_params(8),
    )(parts, *early, late1, *flat)


def lamb_kernel(*refs):
    refs = Refs(refs)
    sums_ref, early0, early1, late0_ref, late1 = refs.take(5)
    arrays = [refs.take(3) for _ in range(6)]
    outs = [refs.take(4) for _ in range(6)]
    norm_out, ratio_out = refs.take(2)
    weight_norm = jnp.sqrt(sums_ref[0:1])
    update_norms = jnp.sqrt(sums_ref[1:2])
    used = lax.broadcasted_iota(jnp.int32, (1, 128), 1) < 17
    ratios = jnp.where(used, weight_norm / jnp.where(used, update_norms, 1.0), 0.0)
    norm_out[...] = update_norms
    ratio_out[...] = ratios
    tensors = Tensors(arrays, (early0, early1), (None, late1))
    for place, array, index, grad in tensors.each(lambda: late0_ref[...]):
        weight, first, second, update = tensors.parts(arrays[array], index, grad())
        if place >= 9:
            factor = jnp.concatenate(
                [ratios[:, place + row : place + row + 1] for row in range(4)], axis=0
            )
        else:
            factor = ratios[:, place : place + 1]
        after = weight - LEARN_RATE * factor * update
        where = Ellipsis if index is None else index
        for ref, value in zip(outs[array], (first, second, after, after.astype(BF16))):
            ref[where] = value


def lamb_call(sums, early, late, arrays):
    vmem = pl.BlockSpec(memory_space=pltpu.VMEM)
    flat = [ref for array in arrays for ref in array]
    shapes = []
    for array in arrays:
        shape = array[0].shape
        shapes += [jax.ShapeDtypeStruct(shape, F32)] * 3 + [jax.ShapeDtypeStruct(shape, BF16)]
    shapes += [jax.ShapeDtypeStruct((1, 128), F32)] * 2
    return pl.pallas_call(
        lamb_kernel,
        in_specs=[vmem] * (5 + len(flat)),
        out_specs=[vmem] * len(shapes),
        out_shape=shapes,
        compiler_params=comm_params(None),
    )(sums, *early, *late, *flat)


def angles(places):
    steps = jnp.arange(HALF).astype(F32)
    inverse = jnp.exp(steps * (-2.0 * math.log(10000.0) / ROT))
    phase = (0.25 * inverse)[:, None] * places.astype(F32)[None, :]
    return jnp.concatenate([jnp.cos(phase), jnp.sin(phase)], axis=0)


def param_squares(arrays, leader):
    query, keyval, output, upward, downward, norms = arrays
    return jnp.concatenate(
        [
            jnp.sum(query * query, axis=(1, 2)),
            (jnp.sum(keyval * keyval) * leader)[None],
            jnp.sum(output * output, axis=(1, 2)),
            jnp.sum(upward * upward, axis=(1, 2)),
            jnp.sum(downward * downward, axis=(1, 2)),
            jnp.sum(norms * norms, axis=2).reshape(8) * leader,
        ]
    )


def apply_trust(masters, updates, trust):
    factors = (
        trust[0:2][:, None, None],
        trust[2],
        trust[3:5][:, None, None],
        trust[5:7][:, None, None],
        trust[7:9][:, None, None],
        trust[9:17].reshape(2, 4, 1),
    )
    return tuple(
        (
            weight - LEARN_RATE * factor * update
            for weight, factor, update in zip(masters, factors, updates)
        )
    )


def plain_scatter(parts, depth):
    pieces = parts.reshape(-1, depth, parts.shape[-1])
    return lax.psum_scatter(pieces, ("tensor", "dp"), scatter_dimension=0).astype(F32)


def shards(
    fast,
    hidden_in,
    out_grad,
    positions,
    query_weight,
    keyval_weight,
    output_weight,
    up_weight,
    down_weight,
    norm_params,
    query_first,
    query_second,
    keyval_first,
    keyval_second,
    output_first,
    output_second,
    up_first,
    up_second,
    down_first,
    down_second,
    norm_first,
    norm_second,
):
    masters = (query_weight, keyval_weight, output_weight, up_weight, down_weight, norm_params)
    tensor = lax.axis_index("tensor")
    leader = (tensor == 0).astype(F32)
    rows, width = hidden_in.shape
    tens = positions.shape[0] // rows
    depth = keyval_weight.shape[0]

    narrow, wide = [], []
    for layer in range(2):
        if layer == 0:
            keys, values = keyval_weight[:, :HD], keyval_weight[:, HD:]
        else:
            keys = values = jnp.zeros((depth, HD), F32)
        pieces = [query_weight[layer], keys, output_weight[layer].T, values]
        narrow.append(jnp.concatenate(pieces, axis=1).astype(BF16))
        wide.append(
            jnp.concatenate([up_weight[layer], down_weight[layer].T], axis=1).astype(BF16)
        )
    norm_low = norm_params.astype(BF16).reshape(8, depth)

    def joined(pack):
        return pack.reshape(tens, width, pack.shape[-1])

    trig = angles(lax.dynamic_slice_in_dim(positions, tensor * rows, rows, 0))
    if fast:
        small = jnp.pad(norm_low.T, ((0, 0), (0, 120)))
        norm_rows, kv, state, act, slope, *others = forward_call(
            hidden_in, trig, small, [narrow[0], wide[0], narrow[1], wide[1]]
        )
        norm_full = norm_rows.reshape(2, 4, width)
        kv = kv.reshape(-1, 2 * HD)
        qts, ats, lses = others[0:2], others[2:4], others[4:6]
        attn_all = [joined(others[6]), joined(others[8])]
        feed_all = [joined(others[7]), joined(others[9])]
        saved = [(hidden_in, qts[0], ats[0], lses[0], act, slope)]
        current, act, slope = mix_call(state, norm_full[1], ats[1], attn_all[1], feed_all[1])
        saved.append((state, qts[1], ats[1], lses[1], act, slope))
    else:
        attn_all, feed_all = (
            [joined(lax.all_gather(pack, ("tensor", "dp"), axis=0)) for pack in packs]
            for packs in (narrow, wide)
        )
        norm_full = lax.all_gather(norm_low, "dp", axis=0)
        norm_full = jnp.swapaxes(norm_full, 0, 1).reshape(2, 4, width).astype(F32)
        current = hidden_in
        saved = []
        for layer in range(2):
            norms = norm_full[layer]
            if layer == 0:
                qt, kv = qkv_call(True, current, norms, trig, attn_all[layer])
                kv = share_call(kv, tens).reshape(-1, 2 * HD)
            else:
                (qt,) = qkv_call(False, current, norms, trig, attn_all[layer])
            at, lse = attend_call(qt, kv)
            after, act, slope = mix_call(current, norms, at, attn_all[layer], feed_all[layer])
            saved.append((current, qt, at, lse, act, slope))
            current = after

    x, qt, at, lse, act, slope = saved[1]
    norms = norm_full[1]
    early, late = [None, None], [None, None]
    pack, dout, mlp = mix_back_call(
        out_grad, x, norms, at, act, slope, attn_all[1], feed_all[1]
    )
    if fast:
        _, _, _, _, act, slope = saved[0]
        early[0], early[1], late[1], grad, pack, _ = backward_call(
            norm_rows, trig, kv, hidden_in, pack, out_grad, x, mlp, qts, ats, lses, dout,
            act, slope, [attn_all[0], attn_all[1], feed_all[0]],
        )
        pack = pack.reshape(tens, width, pack.shape[-1])
    else:
        gqt, dkv = attend_back_call(qt, dout, at, lse, kv, trig)
        early[1] = plain_scatter(pack, depth)
        grad, pack, sums = norm_back_call(False, out_grad, x, norms, mlp, gqt, attn_all[1])
        late[1] = plain_scatter(pack, depth)
        x, qt, at, lse, act, slope = saved[0]
        norms = norm_full[0]
        pack, dout, mlp = mix_back_call(
            grad, x, norms, at, act, slope, attn_all[0], feed_all[0]
        )
        early[0] = plain_scatter(pack, depth)
        gqt, dkv = attend_back_call(qt, dout, at, lse, kv, trig, dkv)
        dkv = merge_call(dkv)
        grad, pack = norm_back_call(
            True, grad, x, norms, mlp, gqt, attn_all[0], dkv, trig, sums
        )

    arrays = (
        (query_weight, query_first, query_second),
        (keyval_weight, keyval_first, keyval_second),
        (output_weight, output_first, output_second),
        (up_weight, up_first, up_second),
        (down_weight, down_first, down_second),
        (norm_params, norm_first, norm_second),
    )
    if fast:
        late[0], totals = norms_call(pack, early, late[1], arrays)
        *nexts, update_norms, trust_ratios = lamb_call(totals, early, late, arrays)
        return (current, grad, *nexts, update_norms[0, :17], trust_ratios[0, :17])
    late[0] = plain_scatter(pack, depth)
    hidden = up_weight.shape[2]
    query_g = jnp.stack([late[layer][:, :QW] for layer in range(2)])
    keyval_g = late[0][:, QW : QW + 2 * HD]
    output_g = jnp.stack([early[layer][:, 2 * hidden : 2 * hidden + QW].T for layer in range(2)])
    up_g = jnp.stack([early[layer][:, :hidden] for layer in range(2)])
    down_g = jnp.stack([early[layer][:, hidden : 2 * hidden].T for layer in range(2)])
    norm_g = late[0][:, QW + 2 * HD : QW + 2 * HD + 8].T.reshape(2, 4, depth)

    grads = (query_g, keyval_g, output_g, up_g, down_g, norm_g)
    parts = [lamb_parts(*array, grad) for array, grad in zip(arrays, grads)]
    updates = tuple((part[2] for part in parts))
    weight_total, update_total = lax.psum(
        (param_squares(masters, leader), param_squares(updates, leader)), ("dp", "tensor")
    )
    weight_norm = jnp.sqrt(weight_total)
    update_norms = jnp.sqrt(update_total)
    trust_ratios = weight_norm / update_norms
    nexts = apply_trust(masters, updates, trust_ratios)
    outs = [current, grad]
    for index in range(6):
        low = nexts[index].astype(BF16)
        outs += [parts[index][0], parts[index][1], nexts[index], low]
    return tuple(outs) + (update_norms, trust_ratios)


def solution(mesh):
    fast = mesh.shape["dp"] == 8 and mesh.shape["tensor"] == 4
    columns = P(None, "dp", "tensor")
    across = P(None, "tensor", "dp")
    flat = P("dp", None)
    norm = P(None, None, "dp")
    state = P(("dp", "tensor"), None)
    in_specs = (
        (state, state, P("dp"), columns, flat, across, columns, across, norm)
        + (columns, columns, flat, flat, across, across, columns, columns, across, across)
        + (norm, norm)
    )
    out_specs = (
        (state, state)
        + (columns,) * 4
        + (flat,) * 4
        + (across,) * 4
        + (columns,) * 4
        + (across,) * 4
        + (norm,) * 4
        + (P(), P())
    )
    return jax.shard_map(
        functools.partial(shards, fast),
        mesh=mesh,
        in_specs=in_specs,
        out_specs=out_specs,
        check_vma=False,
    )
```

```python
import functools
import math

import jax
import jax.numpy as jnp
from jax import lax
from jax.experimental import pallas as pl
from jax.experimental.pallas import tpu as pltpu
from jax.sharding import PartitionSpec as P

F32 = jnp.float32
BF16 = jnp.bfloat16
MESH = pl.DeviceIdType.MESH

HD = 64
ROT = 16
HALF = ROT // 2
STEP = 5
HEADS_HERE = 3
QW = 192

NORM_EPSILON = 1e-05
BETA_FIRST = 0.5
BETA_SECOND = 0.55
ADAM_EPSILON = 1e-06
WEIGHT_DECAY = 0.01
LEARN_RATE = 0.5
SCALE = HD**-0.5
ROOM = 63 * 2**20


def dot(a, b):
    return jnp.dot(a, b, preferred_element_type=F32)


def dot_nt(a, b):
    return lax.dot_general(a, b, (((1,), (1,)), ((), ())), preferred_element_type=F32)


def turn(a):
    return jnp.transpose(a.astype(F32), (1, 0))


def standard(values):
    center = values - jnp.mean(values, axis=-1, keepdims=True)
    spread = jnp.mean(center * center, axis=-1, keepdims=True)
    inverse = lax.rsqrt(spread + NORM_EPSILON)
    return center * inverse, inverse


def gelu_parts(v):
    x = jnp.abs(v) * (2.0**-0.5)
    bell = jnp.exp(-x * x)
    t = 1.0 / (1.0 + 0.3275911 * x)
    series = t * (
        0.254829592
        + t * (-0.284496736 + t * (1.421413741 + t * (-1.453152027 + t * 1.061405429)))
    )
    tail = 0.5 * series * bell
    cumulative = jnp.where(v < 0.0, tail, 1.0 - tail)
    return cumulative, bell * (1.0 / math.sqrt(2.0 * math.pi))


class Place:
    def __init__(self):
        dp, tensor = lax.axis_index("dp"), lax.axis_index("tensor")
        self.z, self.x = lax.div(dp, 2), lax.rem(dp, 2)
        self.y, self.core = lax.div(tensor, 2), lax.rem(tensor, 2)
        self.tensor = tensor
        self.to_x = self.at(x=1 - self.x)
        self.to_y = self.at(y=1 - self.y)
        self.to_core = self.at(core=1 - self.core)
        self.to_corner = self.at(y=1 - self.y, core=1 - self.core)

    def at(self, z=None, x=None, y=None, core=None):
        z = self.z if z is None else z
        x = self.x if x is None else x
        y = self.y if y is None else y
        core = self.core if core is None else core
        return (z * 2 + x, y * 2 + core)

    def along(self, shift):
        return lax.rem(self.z + shift, 4)

    def near(self):
        return [
            (
                code,
                self.at(
                    x=lax.rem(self.x + code // 4, 2),
                    y=lax.rem(self.y + code // 2 % 2, 2),
                    core=lax.rem(self.core + code % 2, 2),
                ),
            )
            for code in range(1, 8)
        ]

    def peers(self, corner, near):
        peers = [self.at(z=self.along(shift)) for shift in (1, 2, 3)]
        if near:
            peers += [peer for _, peer in self.near()]
        else:
            peers += [self.to_x, self.to_y, self.to_core]
        if corner:
            peers.append(self.to_corner)
        return peers

    def hail(self, corner=False, near=False):
        barrier = pltpu.get_barrier_semaphore()
        for peer in self.peers(corner, near):
            pl.semaphore_signal(barrier, inc=1, device_id=peer, device_id_type=MESH)

    def listen(self, corner=False, near=False):
        pl.semaphore_wait(pltpu.get_barrier_semaphore(), len(self.peers(corner, near)))

    def greet(self, corner=False, near=False):
        self.hail(corner, near)
        self.listen(corner, near)


class Refs:
    def __init__(self, refs):
        self.refs = list(refs)

    def take(self, count):
        taken, self.refs = self.refs[:count], self.refs[count:]
        return taken


def comm_params(ident):
    if ident is None:
        return pltpu.CompilerParams(vmem_limit_bytes=ROOM)
    return pltpu.CompilerParams(
        collective_id=ident, has_side_effects=True, vmem_limit_bytes=ROOM
    )


def remote(src, dst, send, recv, to):
    return pltpu.make_async_remote_copy(
        src_ref=src, dst_ref=dst, send_sem=send, recv_sem=recv, device_id=to, device_id_type=MESH
    )


def timed(steps, now, span):
    if not steps:
        return
    ready = [(now <= due) & (due < now + span) for due, _ in steps]

    @pl.when(functools.reduce(jnp.logical_or, ready))
    def _():
        for now_due, (_, step) in zip(ready, steps):
            pl.when(now_due)(step)


def within(steps, first, last):
    return [entry for entry in steps if first <= entry[0] < last]


class Gather:
    COUNT = 35

    def __init__(self, me, source, out, own_sem, send, recv):
        half = source.shape[0] // 2
        top, low = pl.ds(0, half), pl.ds(half, half)
        other = (1 - me.y) * 2 + me.core
        mine = out.at[me.tensor, me.z, me.x]

        def copy(slot, src, dst, to):
            return remote(src, dst, send.at[slot], recv.at[slot], to)

        parts = {"own": pltpu.make_async_copy(source, mine, own_sem)}
        for d in range(4):
            z = me.along(4 - d)
            block = out.at[me.tensor, z, me.x]
            origin = source if d == 0 else block
            if d > 0:
                parts["z", d] = copy(d - 1, source, mine, me.at(z=me.along(d)))
            parts["x", d] = copy(3 + d, origin, block, me.to_x)
            parts["y", d] = copy(7 + d, origin, block, me.to_y)
            parts["core", d] = copy(11 + d, origin, block, me.to_core)
            from_x, from_y = out.at[me.tensor, z, 1 - me.x], out.at[other, z, me.x]
            parts["xy", d] = copy(15 + d, from_x.at[top], from_x.at[top], me.to_y)
            parts["yx", d] = copy(19 + d, from_y.at[low], from_y.at[low], me.to_x)
            parts["core x", d] = copy(23 + d, from_x, from_x, me.to_core)
            parts["core y", d] = copy(27 + d, from_y, from_y, me.to_core)
            far = out.at[other, z, 1 - me.x]
            parts["core far", d] = copy(31 + d, far, far, me.to_core)
        self.parts = parts

    def along(self, *shifts):
        for d in shifts:
            self.parts["z", d].start()

    def own(self):
        for key in (("x", 0), ("y", 0), ("core", 0), "own"):
            self.parts[key].start()

    def pass_on(self, d):
        self.parts["z", d].wait()
        for way in ("x", "y", "core"):
            self.parts[way, d].start()

    def cross(self, d):
        self.parts["x", d].wait_recv()
        self.parts["xy", d].start()
        self.parts["core x", d].start()
        self.parts["y", d].wait_recv()
        self.parts["yx", d].start()
        self.parts["core y", d].start()

    def far(self, d):
        self.parts["xy", d].wait_recv()
        self.parts["yx", d].wait_recv()
        self.parts["core far", d].start()

    def arrive(self):
        self.parts["own"].wait()
        for key, copy in self.parts.items():
            if key != "own" and key[0].startswith("core"):
                copy.wait_recv()

    def end(self):
        for key, copy in self.parts.items():
            if key != "own" and key[0] != "z":
                copy.wait_send()


def add_rows(total, part):
    def one(i, _):
        rows = pl.ds(pl.multiple_of(i * 16, 16), 16)
        total[rows, :] += part[rows, :]
        return 0

    lax.fori_loop(0, total.shape[0] // 16, one, 0)


class Scatter:
    COUNT = 27

    @staticmethod
    def scratch(rows, cols):
        half = rows // 2
        return [
            pltpu.VMEM((4, 2, 2, rows, cols), BF16),
            pltpu.VMEM((2, 4, 2, rows, cols), BF16),
            pltpu.VMEM((4, 2, half, cols), BF16),
            pltpu.VMEM((4, 2, half, cols), BF16),
            pltpu.VMEM((4, half, cols), BF16),
            pltpu.VMEM((4, half, cols), BF16),
            pltpu.VMEM((3, rows, cols), BF16),
            pltpu.SemaphoreType.DMA((8,)),
            pltpu.SemaphoreType.DMA((Scatter.COUNT,)),
            pltpu.SemaphoreType.DMA((Scatter.COUNT,)),
        ]

    def __init__(
        self, me, source, out, total, from_core, from_x, from_y, turn_x, turn_y, from_z,
        load_sem, send, recv,
    ):
        self.me, self.out, self.total = me, out, total
        self.from_core, self.from_x, self.from_y = from_core, from_x, from_y
        self.turn_x, self.turn_y, self.from_z = turn_x, turn_y, from_z
        half = total.shape[3] // 2
        self.top, self.low = pl.ds(0, half), pl.ds(half, half)
        self.order = [me.along(d) for d in (2, 3, 1, 0)]
        self.parts = parts = {}

        def copy(slot, src, dst, to):
            return remote(src, dst, send.at[slot], recv.at[slot], to)

        for d, z in enumerate(self.order):
            for y in range(2):
                parts["load", d, y] = pltpu.make_async_copy(
                    source.at[2 * y + me.core, z], total.at[z, :, y], load_sem.at[2 * d + y]
                )
                parts["core", d, y] = copy(
                    2 * d + y, source.at[2 * y + 1 - me.core, z], from_core.at[y, z], me.to_core
                )
            parts["x", d] = copy(
                8 + d, total.at[z, 1 - me.x, :, self.top], from_x.at[z], me.to_x
            )
            parts["y", d] = copy(
                12 + d, total.at[z, :, 1 - me.y, self.low], from_y.at[z], me.to_y
            )
            parts["xy", d] = copy(
                16 + d, total.at[z, me.x, 1 - me.y, self.top], turn_y.at[z], me.to_y
            )
            parts["yx", d] = copy(
                20 + d, total.at[z, 1 - me.x, me.y, self.low], turn_x.at[z], me.to_x
            )
            if d < 3:
                parts["z", d] = copy(24 + d, total.at[z, me.x, me.y], from_z.at[d], me.at(z=z))

    def send(self):
        for d in range(4):
            for y in range(2):
                self.parts["core", d, y].start()

    def fetch(self):
        for d in range(4):
            for y in range(2):
                self.parts["load", d, y].start()

    def launch(self, d):
        self.parts["x", d].start()
        self.parts["y", d].start()

    def begin(self):
        self.send()
        self.fetch()

    def core(self, d):
        z = self.order[d]
        for y in range(2):
            self.parts["load", d, y].wait()
            self.parts["core", d, y].wait_recv()
            for x in range(2):
                add_rows(self.total.at[z, x, y], self.from_core.at[y, z, x])
        if d < 2:
            self.launch(d)

    def cross(self, d):
        me, z = self.me, self.order[d]
        self.parts["x", d].wait_recv()
        self.parts["y", d].wait_recv()
        if d < 2:
            self.launch(d + 2)
        for y in range(2):
            add_rows(self.total.at[z, me.x, y, self.top], self.from_x.at[z, y])
        self.parts["xy", d].start()
        for x in range(2):
            add_rows(self.total.at[z, x, me.y, self.low], self.from_y.at[z, x])
        self.parts["yx", d].start()

    def far(self, d):
        me, z = self.me, self.order[d]
        self.parts["xy", d].wait_recv()
        add_rows(self.total.at[z, me.x, me.y, self.top], self.turn_y.at[z])
        self.parts["yx", d].wait_recv()
        add_rows(self.total.at[z, me.x, me.y, self.low], self.turn_x.at[z])
        if d < 3:
            self.parts["z", d].start()

    def end(self):
        me = self.me
        for d in range(3):
            self.parts["z", d].wait_recv()

        def one(i, _):
            rows = pl.ds(pl.multiple_of(i * 16, 16), 16)
            result = self.total[me.z, me.x, me.y, rows, :].astype(F32)
            for d in range(3):
                result = result + self.from_z[d, rows, :].astype(F32)
            self.out[rows, :] = result
            return 0

        lax.fori_loop(0, self.out.shape[0] // 16, one, 0)
        for key, copy in self.parts.items():
            if key[0] != "load":
                copy.wait_send()

    def steps(self):
        order = [
            (self.core, 0), (self.core, 1), (self.core, 2), (self.core, 3), (self.cross, 0),
            (self.cross, 1), (self.far, 0), (self.far, 1), (self.cross, 2), (self.cross, 3),
            (self.far, 2), (self.far, 3),
        ]
        return [functools.partial(step, d) for step, d in order] + [self.end]


def tensor_barrier(count):
    me = lax.axis_index("tensor")
    barrier = pltpu.get_barrier_semaphore()
    for shift in range(1, count):
        pl.semaphore_signal(
            barrier, inc=1, device_id={"tensor": lax.rem(me + shift, count)}, device_id_type=MESH
        )
    pl.semaphore_wait(barrier, count - 1)


def share_kernel(count, mine_ref, out_ref, here_sem, send_sem, recv_sem):
    me = lax.axis_index("tensor")
    tensor_barrier(count)
    copies = []
    for shift in range(1, count):
        copies.append(
            pltpu.make_async_remote_copy(
                src_ref=mine_ref,
                dst_ref=out_ref.at[me],
                send_sem=send_sem.at[shift],
                recv_sem=recv_sem.at[shift],
                device_id={"tensor": lax.rem(me + shift, count)},
                device_id_type=MESH,
            )
        )
        copies[-1].start()
    own = pltpu.make_async_copy(mine_ref, out_ref.at[me], here_sem)
    own.start()
    own.wait()
    for copy in copies:
        copy.wait()


def share_call(mine, count):
    return pl.pallas_call(
        functools.partial(share_kernel, count),
        in_specs=[pl.BlockSpec(memory_space=pltpu.VMEM)],
        out_specs=pl.BlockSpec(memory_space=pltpu.VMEM),
        out_shape=jax.ShapeDtypeStruct((count,) + mine.shape, mine.dtype),
        scratch_shapes=[
            pltpu.SemaphoreType.DMA,
            pltpu.SemaphoreType.DMA((count,)),
            pltpu.SemaphoreType.DMA((count,)),
        ],
        compiler_params=pltpu.CompilerParams(collective_id=9, has_side_effects=True),
    )(mine)


def merge_kernel(count, parts_ref, out_ref, low, landed, send_sem, recv_sem):
    me = lax.axis_index("tensor")
    low[...] = parts_ref[...].astype(BF16)
    tensor_barrier(count)
    copies = []
    for shift in range(1, count):
        to = lax.rem(me + shift, count)
        copies.append(
            pltpu.make_async_remote_copy(
                src_ref=low.at[to],
                dst_ref=landed.at[shift],
                send_sem=send_sem.at[shift],
                recv_sem=recv_sem.at[shift],
                device_id={"tensor": to},
                device_id_type=MESH,
            )
        )
        copies[-1].start()
    total = parts_ref[me]
    for shift, copy in enumerate(copies, 1):
        copy.wait()
        total = total + landed[shift].astype(F32)
    out_ref[...] = total


def merge_call(parts):
    count = parts.shape[0]
    vmem = pl.BlockSpec(memory_space=pltpu.VMEM)
    return pl.pallas_call(
        functools.partial(merge_kernel, count),
        in_specs=[vmem],
        out_specs=vmem,
        out_shape=jax.ShapeDtypeStruct(parts.shape[1:], F32),
        scratch_shapes=[
            pltpu.VMEM(parts.shape, BF16),
            pltpu.VMEM(parts.shape, BF16),
            pltpu.SemaphoreType.DMA((count,)),
            pltpu.SemaphoreType.DMA((count,)),
        ],
        compiler_params=pltpu.CompilerParams(collective_id=10, has_side_effects=True),
    )(parts)


def blocks_of(parts):
    tens, width, cols = parts.shape
    return parts.reshape(tens, 4, 2, width // 8, cols)


def rotated(low, cos, sin):
    first, second = low[:HALF], low[HALF:ROT]
    return jnp.concatenate([first * cos - second * sin, second * cos + first * sin], axis=0)


def put_query(lin, cos, sin, qt_ref):
    for head in range(HEADS_HERE):
        base = head * HD
        low = rotated(lin[base : base + ROT], cos, sin)
        qt_ref[base : base + ROT] = (low.astype(BF16).astype(F32) * SCALE).astype(BF16)
        qt_ref[base + ROT : base + HD] = (
            lin[base + ROT : base + HD].astype(BF16).astype(F32) * SCALE
        ).astype(BF16)
    qt_ref[QW:] = jnp.zeros_like(qt_ref[QW:])


def keyval_rows(lin, value, cos, sin):
    key = jnp.concatenate([rotated(lin[QW : QW + ROT], cos, sin), lin[QW + ROT :]], axis=0)
    return turn(jnp.concatenate([key, value], axis=0)).astype(BF16)


def normed_rows(x, gain, bias):
    return (standard(x)[0] * gain + bias).astype(BF16)


def qkv_kernel(first, x_ref, norm_ref, trig_ref, qk_ref, *rest):
    if first:
        ov_ref, qt_ref, kv_ref, normed = rest
    else:
        qt_ref, normed = rest
    t = pl.program_id(0)

    @pl.when(t == 0)
    def _():
        normed[...] = normed_rows(x_ref[...].astype(F32), norm_ref[0:1], norm_ref[1:2])

    cos, sin = trig_ref[0:HALF], trig_ref[HALF:ROT]
    lin = turn(dot(normed[...], qk_ref[0]))
    put_query(lin, cos, sin, qt_ref.at[0])
    if first:

        @pl.when(t == 0)
        def _():
            value = turn(dot(normed[...], ov_ref[0]))[QW:]
            kv_ref[...] = keyval_rows(lin, value, cos, sin)


def qkv_call(first, x, norms, trig, weights):
    rows, width = x.shape
    tens = weights.shape[0]
    whole = pl.BlockSpec(memory_space=pltpu.VMEM)
    in_specs = [whole, whole, whole, pl.BlockSpec((1, width, 256), lambda t: (t, 0, 0))]
    out_shape = [jax.ShapeDtypeStruct((tens, 256, rows), BF16)]
    out_specs = [pl.BlockSpec((1, 256, rows), lambda t: (t, 0, 0))]
    args = [x, norms, trig, weights]
    if first:
        in_specs.append(pl.BlockSpec((1, width, 256), lambda t: (0, 0, 1)))
        args.append(weights)
        out_shape.append(jax.ShapeDtypeStruct((rows, 2 * HD), BF16))
        out_specs.append(whole)
    return pl.pallas_call(
        functools.partial(qkv_kernel, first),
        grid=(tens,),
        in_specs=in_specs,
        out_specs=out_specs,
        out_shape=out_shape,
        scratch_shapes=[pltpu.VMEM((rows, width), BF16)],
        compiler_params=pltpu.CompilerParams(vmem_limit_bytes=ROOM),
    )(*args)


def attend_part(place, qt_ref, keys, values_t, at_ref, lse_ref, poll=None, between=None):
    rows = qt_ref.shape[1]

    def block(index, carry, diagonal):
        here = pl.ds(pl.multiple_of(index * rows, rows), rows)
        key = keys[here, :]
        value_t = values_t[:, here]
        out = []
        for head in range(HEADS_HERE):
            scores = dot(key, qt_ref[head * HD : (head + 1) * HD])
            if diagonal:
                below = lax.broadcasted_iota(jnp.int32, scores.shape, 0)
                across = lax.broadcasted_iota(jnp.int32, scores.shape, 1)
                scores = jnp.where(below <= across, scores, -1e30)
            peak = jnp.max(scores, axis=0, keepdims=True)
            if carry is not None:
                peak = jnp.maximum(peak, carry[head][0])
            weights = jnp.exp(scores - peak)
            total = jnp.sum(weights, axis=0, keepdims=True)
            mixed = dot(value_t, weights.astype(BF16))
            if carry is not None:
                fade = jnp.exp(carry[head][0] - peak)
                total = total + carry[head][1] * fade
                mixed = mixed + carry[head][2] * fade
            out.append((peak, total, mixed))
        return tuple(out)

    if poll:
        poll(0)
    carry = block(place, None, True)
    if between:
        between()

    def later(i, carry):
        if poll:
            poll(1 + i)
        return block(i, carry, False)

    carry = lax.fori_loop(0, place, later, carry)
    lse_ref[...] = jnp.zeros_like(lse_ref)
    for head in range(HEADS_HERE):
        peak, total, mixed = carry[head]
        at_ref[head * HD : (head + 1) * HD] = (mixed / total).astype(BF16)
        lse_ref[head : head + 1] = peak + jnp.log(total)
    at_ref[QW:] = jnp.zeros_like(at_ref[QW:])


def attend_kernel(qt_ref, kv_ref, at_ref, lse_ref, keys, values_t):
    @pl.when(pl.program_id(0) == 0)
    def _():
        keys[...] = kv_ref[:, :HD]
        values_t[...] = turn(kv_ref[...])[HD:].astype(BF16)

    attend_part(
        lax.axis_index("tensor"), qt_ref.at[0], keys, values_t, at_ref.at[0], lse_ref.at[0]
    )


def attend_call(qt, kv):
    tens, _, rows = qt.shape
    length = kv.shape[0]
    whole = pl.BlockSpec(memory_space=pltpu.VMEM)
    part = pl.BlockSpec((1, 256, rows), lambda t: (t, 0, 0))
    return pl.pallas_call(
        attend_kernel,
        grid=(tens,),
        in_specs=[part, whole],
        out_specs=[part, pl.BlockSpec((1, 8, rows), lambda t: (t, 0, 0))],
        out_shape=[
            jax.ShapeDtypeStruct((tens, 256, rows), BF16),
            jax.ShapeDtypeStruct((tens, 8, rows), F32),
        ],
        scratch_shapes=[pltpu.VMEM((length, HD), BF16), pltpu.VMEM((HD, length), BF16)],
        compiler_params=comm_params(None),
    )(qt, kv)


def mix_part(normed, at_ref, outward, upward, down, act_ref, slope_ref, poll=None):
    attended = turn(at_ref[:QW]).astype(BF16)
    step = 256
    parts = act_ref.shape[1] // step
    for part in range(parts):
        if poll:
            poll(part)
        cols = slice(part * step, (part + 1) * step)
        pre = dot(normed[...], upward(cols))
        cumulative, bell = gelu_parts(pre)
        act_ref[:, cols] = (pre * cumulative).astype(BF16)
        slope_ref[:, cols] = (cumulative + pre * bell).astype(BF16)
    if poll:
        poll(parts)
    return dot_nt(attended, outward()) + dot_nt(act_ref[...], down())


def mix_kernel(
    x_ref, norm_ref, at_ref, o_ref, up_ref, down_ref, out_ref, act_ref, slope_ref, normed, total
):
    t = pl.program_id(0)

    @pl.when(t == 0)
    def _():
        x = x_ref[...].astype(F32)
        normed[...] = normed_rows(x, norm_ref[2:3], norm_ref[3:4])
        total[...] = x

    total[...] += mix_part(
        normed, at_ref.at[0], lambda: o_ref[0, :, :QW], lambda cols: up_ref[0, :, cols],
        lambda: down_ref[0], act_ref.at[0], slope_ref.at[0],
    )

    @pl.when(t == pl.num_programs(0) - 1)
    def _():
        out_ref[...] = total[...]


def mix_call(x, norms, at, outward, feed):
    rows, width = x.shape
    tens = feed.shape[0]
    hidden = feed.shape[2] // 2
    whole = pl.BlockSpec(memory_space=pltpu.VMEM)
    wide = pl.BlockSpec((1, rows, hidden), lambda t: (t, 0, 0))
    return pl.pallas_call(
        mix_kernel,
        grid=(tens,),
        in_specs=[
            whole,
            whole,
            pl.BlockSpec((1, 256, rows), lambda t: (t, 0, 0)),
            pl.BlockSpec((1, width, 256), lambda t: (t, 0, 1)),
            pl.BlockSpec((1, width, hidden), lambda t: (t, 0, 0)),
            pl.BlockSpec((1, width, hidden), lambda t: (t, 0, 1)),
        ],
        out_specs=[whole, wide, wide],
        out_shape=[
            jax.ShapeDtypeStruct((rows, width), F32),
            jax.ShapeDtypeStruct((tens, rows, hidden), BF16),
            jax.ShapeDtypeStruct((tens, rows, hidden), BF16),
        ],
        scratch_shapes=[pltpu.VMEM((rows, width), BF16), pltpu.VMEM((rows, width), F32)],
        compiler_params=comm_params(None),
    )(x, norms, at, outward, feed, feed)


def mix_back_part(
    low, low_t, normed_t, at_ref, act_ref, slope_ref, outward, upward, down, dot_ref, pack_put,
    poll=None,
):
    hidden = act_ref.shape[1]
    if poll:
        poll(0)
    grad_attended = dot(low[...], outward())
    dot_ref[:QW] = turn(grad_attended).astype(BF16)
    dot_ref[QW:] = jnp.zeros_like(dot_ref[QW:])
    pack_put(2 * hidden, dot_nt(low_t[...], at_ref[...]).astype(BF16))
    if poll:
        poll(1)
    for start in range(0, hidden, 256):
        cols = slice(start, start + 256)
        pack_put(hidden + start, dot(low_t[...], act_ref[:, cols]).astype(BF16))
    if poll:
        poll(2)
    grad_pre = []
    for start in range(0, hidden, 256):
        cols = slice(start, start + 256)
        grad = (dot(low[...], down(cols)) * slope_ref[:, cols].astype(F32)).astype(BF16)
        pack_put(start, dot(normed_t[...], grad).astype(BF16))
        grad_pre.append(grad)
    if poll:
        poll(3)
    return dot_nt(jnp.concatenate(grad_pre, axis=1), upward())


def mix_back_start(gx_ref, x, norm_ref, low, low_t, normed_t):
    grad = gx_ref[...].astype(BF16)
    low[...] = grad
    low_t[...] = turn(grad).astype(BF16)
    normed_t[...] = turn(normed_rows(x, norm_ref[2:3], norm_ref[3:4])).astype(BF16)


def mix_back_kernel(
    gx_ref, x_ref, norm_ref, at_ref, act_ref, slope_ref, o_ref, up_ref, down_ref,
    pack_ref, dot_ref, mlp_ref, low, low_t, normed_t,
):
    @pl.when(pl.program_id(0) == 0)
    def _():
        mix_back_start(gx_ref, x_ref[...].astype(F32), norm_ref, low, low_t, normed_t)
        mlp_ref[...] = jnp.zeros_like(mlp_ref)

    def pack_put(start, value):
        pack_ref[0, :, start : start + value.shape[1]] = value

    mlp_ref[...] += mix_back_part(
        low, low_t, normed_t, at_ref.at[0], act_ref.at[0], slope_ref.at[0],
        lambda: o_ref[0, :, :QW], lambda: up_ref[0], lambda cols: down_ref[0, :, cols],
        dot_ref.at[0], pack_put,
    )


def mix_back_call(gx, x, norms, at, act, slope, outward, feed):
    rows, width = x.shape
    tens = feed.shape[0]
    hidden = act.shape[2]
    whole = pl.BlockSpec(memory_space=pltpu.VMEM)
    wide = pl.BlockSpec((1, rows, hidden), lambda t: (t, 0, 0))
    part = pl.BlockSpec((1, 256, rows), lambda t: (t, 0, 0))
    return pl.pallas_call(
        mix_back_kernel,
        grid=(tens,),
        in_specs=[
            whole,
            whole,
            whole,
            part,
            wide,
            wide,
            pl.BlockSpec((1, width, 256), lambda t: (t, 0, 1)),
            pl.BlockSpec((1, width, hidden), lambda t: (t, 0, 0)),
            pl.BlockSpec((1, width, hidden), lambda t: (t, 0, 1)),
        ],
        out_specs=[pl.BlockSpec((1, width, 2 * hidden + 256), lambda t: (t, 0, 0)), part, whole],
        out_shape=[
            jax.ShapeDtypeStruct((tens, width, 2 * hidden + 256), BF16),
            jax.ShapeDtypeStruct((tens, 256, rows), BF16),
            jax.ShapeDtypeStruct((rows, width), F32),
        ],
        scratch_shapes=[
            pltpu.VMEM((rows, width), BF16),
            pltpu.VMEM((width, rows), BF16),
            pltpu.VMEM((width, rows), BF16),
        ],
        compiler_params=comm_params(None),
    )(gx, x, norms, at, act, slope, outward, feed, feed)


def attend_back_start(kv, keys, values, keys_t):
    both_t = turn(kv)
    keys[...] = kv[:, :HD]
    keys_t[...] = both_t[:HD].astype(BF16)
    values[...] = turn(both_t[HD:]).astype(BF16)


def attend_back_part(
    place, qt_ref, dot_ref, at_ref, lse_ref, keys, values, keys_t, dkeys, dvalues, gqt_ref,
    cos, sin, poll=None,
):
    rows = qt_ref.shape[1]
    inner = []
    for head in range(HEADS_HERE):
        span = slice(head * HD, (head + 1) * HD)
        inner.append(
            jnp.sum(
                dot_ref[span].astype(F32) * at_ref[span].astype(F32), axis=0, keepdims=True
            )
        )

    def block(index, carry, diagonal):
        here = pl.ds(pl.multiple_of(index * rows, rows), rows)
        key = keys[here, :]
        value = values[here, :]
        key_t = keys_t[:, here]
        out = []
        dkey = dvalue = None
        for head in range(HEADS_HERE):
            span = slice(head * HD, (head + 1) * HD)
            query_t = qt_ref[span]
            grad_t = dot_ref[span]
            scores = dot(key, query_t)
            probs = jnp.exp(scores - lse_ref[head : head + 1])
            if diagonal:
                below = lax.broadcasted_iota(jnp.int32, scores.shape, 0)
                across = lax.broadcasted_iota(jnp.int32, scores.shape, 1)
                probs = jnp.where(below <= across, probs, 0.0)
            grad_probs = dot(value, grad_t)
            grad_scores = (probs * (grad_probs - inner[head])).astype(BF16)
            part_v = dot_nt(probs.astype(BF16), grad_t)
            part_k = dot_nt(grad_scores, query_t)
            dkey = part_k if head == 0 else dkey + part_k
            dvalue = part_v if head == 0 else dvalue + part_v
            part_q = dot(key_t, grad_scores)
            out.append(part_q if carry is None else carry[head] + part_q)
        dkeys[here, :] += dkey
        dvalues[here, :] += dvalue
        return tuple(out)

    def later(i, carry):
        if poll:
            poll(1 + i)
        return block(i, carry, False)

    if poll:
        poll(0)
    carry = block(place, None, True)
    carry = lax.fori_loop(0, place, later, carry)
    for head in range(HEADS_HERE):
        base = head * HD
        grad = carry[head] * SCALE
        gqt_ref[base : base + ROT] = rotated(grad[:ROT], cos, -sin).astype(BF16)
        gqt_ref[base + ROT : base + HD] = grad[ROT:].astype(BF16)
    gqt_ref[QW:] = jnp.zeros_like(gqt_ref[QW:])


def attend_back_kernel(start_given, *refs):
    refs = Refs(refs)
    qt_ref, dot_ref, at_ref, lse_ref, kv_ref, trig_ref = refs.take(6)
    before_ref = refs.take(1)[0] if start_given else None
    gqt_ref, dkv_ref, keys, values, keys_t, dkeys, dvalues = refs.take(7)
    t = pl.program_id(0)
    rows = qt_ref.shape[2]

    @pl.when(t == 0)
    def _():
        attend_back_start(kv_ref[...], keys, values, keys_t)
        dkeys[...] = jnp.zeros_like(dkeys)
        dvalues[...] = jnp.zeros_like(dvalues)

    attend_back_part(
        lax.axis_index("tensor"), qt_ref.at[0], dot_ref.at[0], at_ref.at[0], lse_ref.at[0],
        keys, values, keys_t, dkeys, dvalues, gqt_ref.at[0],
        trig_ref[0:HALF], trig_ref[HALF:ROT],
    )

    @pl.when(t == pl.num_programs(0) - 1)
    def _():
        both = jnp.concatenate([turn(dkeys[...]), turn(dvalues[...])], axis=0)
        for part in range(dkv_ref.shape[0]):
            piece = both[:, part * rows : (part + 1) * rows]
            if start_given:
                piece = piece + before_ref[part]
            dkv_ref[part] = piece


def attend_back_call(qt, dout, at, lse, kv, trig, before=None):
    tens, _, rows = qt.shape
    length = kv.shape[0]
    whole = pl.BlockSpec(memory_space=pltpu.VMEM)
    part = pl.BlockSpec((1, 256, rows), lambda t: (t, 0, 0))
    args = [qt, dout, at, lse, kv, trig]
    in_specs = [part, part, part, pl.BlockSpec((1, 8, rows), lambda t: (t, 0, 0)), whole, whole]
    if before is not None:
        args.append(before)
        in_specs.append(whole)
    return pl.pallas_call(
        functools.partial(attend_back_kernel, before is not None),
        grid=(tens,),
        in_specs=in_specs,
        out_specs=[part, whole],
        out_shape=[
            jax.ShapeDtypeStruct((tens, 256, rows), BF16),
            jax.ShapeDtypeStruct((length // rows, 2 * HD, rows), F32),
        ],
        scratch_shapes=[
            pltpu.VMEM((length, HD), BF16),
            pltpu.VMEM((length, HD), BF16),
            pltpu.VMEM((HD, length), BF16),
            pltpu.VMEM((length, HD), F32),
            pltpu.VMEM((length, HD), F32),
        ],
        compiler_params=comm_params(None),
    )(*args)


def shared_rows(grad, cos, sin, shared):
    shared[:ROT] = rotated(grad[:ROT], cos, -sin).astype(BF16)
    shared[ROT:] = grad[ROT:].astype(BF16)


def shared_back(shared, key_weight, value_weight):
    return dot_nt(turn(shared[:HD]).astype(BF16), key_weight) + dot_nt(
        turn(shared[HD:]).astype(BF16), value_weight
    )


def right_columns(shared, normed_t, sums, other):
    pad = jnp.zeros((HD, sums.shape[1]), F32)
    lower = turn(jnp.concatenate([pad, sums, other, pad[8:]], axis=0))
    upper = jnp.concatenate([shared[HD:], jnp.zeros_like(shared[HD:])], axis=0)
    return (dot_nt(normed_t[...], upper) + lower).astype(BF16)


def norm_back(x, attn_grad, mlp_grad, norm_ref):
    unit, inverse = standard(x)
    sums = jnp.concatenate(
        [
            jnp.sum(attn_grad * unit, axis=0, keepdims=True),
            jnp.sum(attn_grad, axis=0, keepdims=True),
            jnp.sum(mlp_grad * unit, axis=0, keepdims=True),
            jnp.sum(mlp_grad, axis=0, keepdims=True),
        ],
        axis=0,
    )
    grad = attn_grad * norm_ref[0:1] + mlp_grad * norm_ref[2:3]
    mean = jnp.mean(grad, axis=-1, keepdims=True)
    slant = jnp.mean(grad * unit, axis=-1, keepdims=True)
    return sums, inverse * (grad - mean - unit * slant)


def norm_back_kernel(first, gx_ref, x_ref, norm_ref, mlp_ref, gqt_ref, qk_ref, *rest):
    if first:
        ov_ref, dkv_ref, trig_ref, other_ref, out_ref, pack_ref, normed_t, attn, shared = rest
    else:
        out_ref, pack_ref, sums_ref, normed_t, attn = rest
    t = pl.program_id(0)

    @pl.when(t == 0)
    def _():
        x = x_ref[...].astype(F32)
        normed = (standard(x)[0] * norm_ref[0:1] + norm_ref[1:2]).astype(BF16)
        normed_t[...] = turn(normed).astype(BF16)
        if first:
            cos, sin = trig_ref[0:HALF], trig_ref[HALF:ROT]
            shared_rows(dkv_ref[...], cos, sin, shared)
            attn[...] = shared_back(shared, qk_ref[0, :, QW:], ov_ref[0, :, QW:])
        else:
            attn[...] = jnp.zeros_like(attn)

    grad_t = gqt_ref[0, :QW]
    attn[...] += dot_nt(turn(grad_t).astype(BF16), qk_ref[0, :, :QW])
    if first:
        left = jnp.concatenate([grad_t, shared[:HD]], axis=0)
        pack_ref[t, :, :256] = dot_nt(normed_t[...], left).astype(BF16)
    else:
        pack_ref[0] = dot_nt(normed_t[...], gqt_ref[0]).astype(BF16)

    @pl.when(t == pl.num_programs(0) - 1)
    def _():
        sums, change = norm_back(x_ref[...].astype(F32), attn[...], mlp_ref[...], norm_ref)
        if first:
            right = right_columns(shared, normed_t, sums, other_ref[...])
            for part in range(pack_ref.shape[0]):
                pack_ref[part, :, 256:] = right
        else:
            sums_ref[...] = sums
        out_ref[...] = gx_ref[...] + change


def norm_back_call(first, gx, x, norms, mlp, gqt, weights, dkv=None, trig=None, other=None):
    rows, width = x.shape
    tens = weights.shape[0]
    whole = pl.BlockSpec(memory_space=pltpu.VMEM)
    part = pl.BlockSpec((1, 256, rows), lambda t: (t, 0, 0))
    args = [gx, x, norms, mlp, gqt, weights]
    in_specs = [whole] * 4 + [part, pl.BlockSpec((1, width, 256), lambda t: (t, 0, 0))]
    scratch = [pltpu.VMEM((width, rows), BF16), pltpu.VMEM((rows, width), F32)]
    out_shape = [jax.ShapeDtypeStruct((rows, width), F32)]
    if first:
        args += [weights, dkv, trig, other]
        in_specs += [pl.BlockSpec((1, width, 256), lambda t: (0, 0, 1)), whole, whole, whole]
        scratch.append(pltpu.VMEM((2 * HD, rows), BF16))
        out_shape.append(jax.ShapeDtypeStruct((tens, width, 384), BF16))
        out_specs = [whole, whole]
    else:
        out_shape.append(jax.ShapeDtypeStruct((tens, width, 256), BF16))
        out_shape.append(jax.ShapeDtypeStruct((4, width), F32))
        out_specs = [whole, pl.BlockSpec((1, width, 256), lambda t: (t, 0, 0)), whole]
    return pl.pallas_call(
        functools.partial(norm_back_kernel, first),
        grid=(tens,),
        in_specs=in_specs,
        out_specs=out_specs,
        out_shape=out_shape,
        scratch_shapes=scratch,
        compiler_params=comm_params(None),
    )(*args)


QUERY_START = (240, 741)
ATTEND_START = (275, 781)
ATTEND_SPAN = 17
MIX_START, MIX_SPAN = 581, 10
GATHER_TIMES = (
    (1, "cross", 0, 250),
    (2, "along", 1, 255),
    (2, "along", 2, 257),
    (2, "along", 3, 266),
    (1, "pass_on", 3, 290),
    (1, "cross", 1, 330),
    (1, "far", 0, 335),
    (1, "pass_on", 2, 365),
    (3, "along", 1, 370),
    (3, "along", 3, 371),
    (1, "cross", 3, 430),
    (1, "far", 1, 435),
    (2, "own", None, 480),
    (2, "pass_on", 1, 481),
    (2, "pass_on", 3, 482),
    (2, "pass_on", 2, 483),
    (1, "cross", 2, 490),
    (1, "far", 3, 505),
    (1, "far", 2, 550),
    (3, "along", 2, 582),
    (2, "cross", 0, 590),
    (2, "cross", 1, 600),
    (2, "far", 0, 605),
    (3, "own", None, 606),
    (3, "pass_on", 1, 607),
    (2, "cross", 3, 620),
    (2, "far", 1, 625),
    (2, "cross", 2, 640),
    (3, "pass_on", 3, 645),
    (2, "far", 3, 650),
    (2, "far", 2, 665),
    (3, "cross", 0, 732),
    (3, "pass_on", 2, 770),
    (3, "cross", 1, 800),
    (3, "far", 0, 805),
    (3, "cross", 3, 860),
    (3, "far", 1, 865),
    (3, "cross", 2, 920),
    (3, "far", 3, 925),
    (3, "far", 2, 970),
)


def pack_narrow(pack, wide, query, output, keyval):
    wide[...] = jnp.zeros_like(wide)
    wide[:, 0:QW] = query
    wide[:, 256 : 256 + QW] = turn(output)
    if keyval is not None:
        upper = lax.broadcasted_iota(jnp.int32, keyval.shape, 1) >= HD
        wide[:, 128:256] += jnp.where(upper, pltpu.roll(keyval, HD, 1), 0.0)
        wide[:, 384:512] += jnp.where(upper, keyval, 0.0)
    pack[...] = wide[...].astype(BF16)


def forward_kernel(*refs):
    refs = Refs(refs)
    x_ref, trig_ref = refs.take(2)
    masters = refs.take(6)
    norm_ref, kv_out, state_out, act_out, slope_out = refs.take(5)
    qt_outs, at_outs, lse_outs = refs.take(2), refs.take(2), refs.take(2)
    packs = refs.take(4)
    own_sem, send, recv = refs.take(3)
    sources, (spread_ref, small_ref) = refs.take(4), refs.take(2)
    small_land, small_own, small_send, small_recv = refs.take(4)
    kv_here, landed, kv_send, kv_recv = refs.take(4)
    narrow, wide, load_sem = refs.take(3)
    normed, total, qt, at, lse, act, slope, keys, values_t, save_sem = refs.take(10)

    me = Place()
    place = me.tensor
    tens, rows = qt.shape[1], qt.shape[3]
    width = total.shape[1]
    hidden = act.shape[2]
    gathers = [
        Gather(me, sources[k], packs[k], own_sem.at[k], send.at[k], recv.at[k]) for k in range(4)
    ]
    steps = []
    for k, what, which, due in GATHER_TIMES:
        action = getattr(gathers[k], what)
        steps.append((due, action if which is None else functools.partial(action, which)))
    mine = small_land.at[me.z, me.x]
    small_mine = pltpu.make_async_copy(small_ref, mine, small_own)
    small_along = [
        remote(small_ref, mine, small_send.at[d], small_recv.at[d], me.at(z=me.along(d)))
        for d in (1, 2, 3)
    ]
    column = small_land.at[:, me.x]
    small_across = remote(column, column, small_send.at[0], small_recv.at[0], me.to_x)
    kv_copies = [
        remote(kv_here, landed.at[place], kv_send.at[k], kv_recv.at[k], peer)
        for k, peer in enumerate((me.to_core, me.to_y, me.to_corner))
    ]
    saves = []

    def save(src, dst):
        copy = pltpu.make_async_copy(src, dst, save_sem.at[len(saves)])
        copy.start()
        saves.append(copy)

    def load(k, buffer, slot):
        return [
            pltpu.make_async_copy(packs[k].at[t], buffer.at[t], load_sem.at[slot, t])
            for t in range(tens)
        ]

    def joined(buffer, t, cols):
        value = buffer[t, :, :, :, cols]
        return value.reshape(width, value.shape[-1])

    me.hail(corner=True)
    query_ref, keyval_ref, output_ref, up_ref, down_ref, param_ref = masters
    small_ref[...] = turn(
        jnp.concatenate(
            [param_ref[0], param_ref[1], jnp.zeros((120, param_ref.shape[2]), F32)], axis=0
        )
    ).astype(BF16)
    pack_narrow(sources[0], spread_ref, query_ref[0], output_ref[0], keyval_ref[...])
    me.listen(corner=True)
    small_mine.start()
    for copy in small_along:
        copy.start()
    first, second = gathers[:2]
    first.along(1, 3, 2)
    first.own()
    sources[1][:, :hidden] = up_ref[0].astype(BF16)
    sources[1][:, hidden:] = down_ref[0].astype(BF16)
    x = x_ref[...].astype(F32)
    total[...] = standard(x)[0]
    first.pass_on(1)
    small_mine.wait()
    for copy in small_along:
        copy.wait_recv()
    small_across.start()
    first.cross(0)
    second.along(1, 3)
    first.pass_on(3)
    first.cross(1)
    first.far(0)
    first.pass_on(2)
    second.along(2)
    second.own()
    pack_narrow(sources[2], spread_ref, query_ref[1], output_ref[1], None)
    sources[3][:, :hidden] = up_ref[1].astype(BF16)
    sources[3][:, hidden:] = down_ref[1].astype(BF16)
    small_across.wait_recv()
    norm_ref[...] = turn(small_land[...].reshape(width, 128))[:8]
    normed[...] = (total[...] * norm_ref[0:1] + norm_ref[1:2]).astype(BF16)
    first.cross(3)
    first.far(1)
    first.cross(2)
    second.pass_on(1)
    first.far(3)
    first.far(2)
    first.arrive()
    loads = load(0, narrow.at[0], 0)
    for copy in loads:
        copy.start()
    for copy in small_along + [small_across]:
        copy.wait_send()
    gathers[0].end()

    cos, sin = trig_ref[0:HALF], trig_ref[HALF:ROT]

    def qkv(layer, loads):
        due = within(steps, QUERY_START[layer], ATTEND_START[layer])
        span = (ATTEND_START[layer] - QUERY_START[layer] + tens - 1) // tens

        def one(t, _):
            timed(due, QUERY_START[layer] + t * span, span)
            for part, copy in enumerate(loads):
                pl.when(t == part)(copy.wait)
            lin = turn(dot(normed[...], joined(narrow.at[layer], t, slice(0, 256))))
            put_query(lin, cos, sin, qt.at[layer, t])
            if layer == 0:

                @pl.when(t == 0)
                def _():
                    value = turn(dot(normed[...], joined(narrow.at[0], 0, slice(384, 512))))
                    kv_here[...] = keyval_rows(lin, value[HD:], cos, sin)
                    for copy in kv_copies:
                        copy.start()

            return 0

        lax.fori_loop(0, tens, one, 0)

    def attention(layer, last, between=None):
        start = ATTEND_START[layer]
        due = within(steps, start, last)

        def one(t, _):
            def first():
                if between:
                    pl.when(t == 0)(between)

            attend_part(
                place, qt.at[layer, t], keys, values_t, at.at[layer, t], lse.at[layer, t],
                lambda i: timed(due, start + (t * (place + 1) + i) * ATTEND_SPAN, ATTEND_SPAN),
                first,
            )
            return 0

        lax.fori_loop(0, tens, one, 0)
        now = start + tens * (place + 1) * ATTEND_SPAN
        timed(due, now, last - now)
        save(qt.at[layer], qt_outs[layer])
        save(at.at[layer], at_outs[layer])
        save(lse.at[layer], lse_outs[layer])

    qkv(0, loads)
    here = pl.ds(pl.multiple_of(place * rows, rows), rows)
    landed[place] = kv_here[...]
    keys[here, :] = kv_here[:, :HD]
    values_t[:, here] = turn(kv_here[...])[HD:].astype(BF16)

    def meet():
        for copy in kv_copies:
            copy.wait()
        for part in range(tens):
            span = pl.ds(part * rows, rows)
            keys[span, :] = landed[part, :, :HD]
            values_t[:, span] = turn(landed[part])[HD:].astype(BF16)

    attention(0, MIX_START, meet)
    save(landed, kv_out)
    gathers[1].arrive()
    loads = load(1, wide, 1)
    for copy in loads:
        copy.start()
    gathers[1].end()
    x = x_ref[...].astype(F32)
    normed[...] = normed_rows(x, norm_ref[2:3], norm_ref[3:4])
    total[...] = x
    wide_loads = loads

    due = within(steps, MIX_START, QUERY_START[1])

    def mix(t, _):
        for part, copy in enumerate(wide_loads):
            pl.when(t == part)(copy.wait)
        total[...] += mix_part(
            normed, at.at[0, t], lambda: joined(narrow.at[0], t, slice(256, 256 + QW)),
            lambda cols: joined(wide, t, cols),
            lambda: joined(wide, t, slice(hidden, 2 * hidden)), act.at[t], slope.at[t],
            lambda i: timed(due, MIX_START + (t * 4 + i) * MIX_SPAN, MIX_SPAN),
        )
        return 0

    lax.fori_loop(0, tens, mix, 0)
    save(total, state_out)
    save(act, act_out)
    save(slope, slope_out)
    gathers[2].arrive()
    loads = load(2, narrow.at[1], 2)
    for copy in loads:
        copy.start()
    gathers[2].end()
    normed[...] = normed_rows(total[...], norm_ref[4:5], norm_ref[5:6])
    qkv(1, loads)
    attention(1, 10000)
    gathers[3].arrive()
    gathers[3].end()
    for copy in saves:
        copy.wait()


def forward_call(x, trig, masters):
    rows, width = x.shape
    tens = 4
    _, depth, hidden = masters[3].shape
    packs = [(depth, 512), (depth, 2 * hidden)] * 2
    vmem = pl.BlockSpec(memory_space=pltpu.VMEM)
    anywhere = pl.BlockSpec(memory_space=pl.ANY)
    heads = jax.ShapeDtypeStruct((tens, 256, rows), BF16)
    sums = jax.ShapeDtypeStruct((tens, 8, rows), F32)
    feed = jax.ShapeDtypeStruct((tens, rows, hidden), BF16)
    out_shape = [
        jax.ShapeDtypeStruct((8, width), F32),
        jax.ShapeDtypeStruct((tens, rows, 2 * HD), BF16),
        jax.ShapeDtypeStruct((rows, width), F32),
        feed,
        feed,
        heads,
        heads,
        heads,
        heads,
        sums,
        sums,
    ] + [jax.ShapeDtypeStruct((4, 4, 2) + pack, BF16) for pack in packs]
    return pl.pallas_call(
        forward_kernel,
        in_specs=[vmem] * 8,
        out_specs=[vmem] + [anywhere] * (len(out_shape) - 1),
        out_shape=out_shape,
        scratch_shapes=[
            pltpu.SemaphoreType.DMA((4,)),
            pltpu.SemaphoreType.DMA((4, Gather.COUNT)),
            pltpu.SemaphoreType.DMA((4, Gather.COUNT)),
            *[pltpu.VMEM(pack, BF16) for pack in packs],
            pltpu.VMEM((depth, 512), F32),
            pltpu.VMEM((depth, 128), BF16),
            pltpu.VMEM((4, 2, depth, 128), BF16),
            pltpu.SemaphoreType.DMA,
            pltpu.SemaphoreType.DMA((4,)),
            pltpu.SemaphoreType.DMA((4,)),
            pltpu.VMEM((rows, 2 * HD), BF16),
            pltpu.VMEM((tens, rows, 2 * HD), BF16),
            pltpu.SemaphoreType.DMA((3,)),
            pltpu.SemaphoreType.DMA((3,)),
            pltpu.VMEM((2, tens, 4, 2, depth, 512), BF16),
            pltpu.VMEM((tens, 4, 2, depth, 2 * hidden), BF16),
            pltpu.SemaphoreType.DMA((3, tens)),
            pltpu.VMEM((rows, width), BF16),
            pltpu.VMEM((rows, width), F32),
            pltpu.VMEM((2, tens, 256, rows), BF16),
            pltpu.VMEM((2, tens, 256, rows), BF16),
            pltpu.VMEM((2, tens, 8, rows), F32),
            pltpu.VMEM((tens, rows, hidden), BF16),
            pltpu.VMEM((tens, rows, hidden), BF16),
            pltpu.VMEM((tens * rows, HD), BF16),
            pltpu.VMEM((HD, tens * rows), BF16),
            pltpu.SemaphoreType.DMA((10,)),
        ],
        compiler_params=comm_params(1),
    )(x, trig, *masters)


EARLY_TIMES = (5, 10, 30, 55, 150, 180, 275, 300, 315, 400, 425, 470, 545)
LATE_TIMES = (500, 510, 515, 520, 530, 540, 550, 555, 560, 570, 580, 590, 640)
LAST_TIMES = (475, 476, 477, 478, 500, 505, 520, 525, 530, 535, 548, 555, 600)


def narrowed(scratch, cols):
    lanes = pl.ds(0, cols)
    views = [ref.at[(slice(None),) * (len(ref.shape) - 1) + (lanes,)] for ref in scratch[:7]]
    return views + list(scratch[7:])


def backward_kernel(*refs):
    refs = Refs(refs)
    norm_ref, trig_ref, kv_ref, x0_ref = refs.take(4)
    gx_in, x1_in = refs.take(2)
    qt_in, at_in, lse_in = refs.take(2), refs.take(2), refs.take(2)
    act_in, slope_in, narrow_in, wide_in = [refs.take(2) for _ in range(4)]
    early_out, late_outs = refs.take(2), refs.take(2)
    grad_out, late0_out, late1 = refs.take(3)
    early_in = refs.take(2)
    early_scratch, late_scratch = refs.take(10), refs.take(10)
    free_sem, again_sem = refs.take(2)
    gx, x1, mlp, attn = refs.take(4)
    qt, at, lse, dout, gqt = refs.take(5)
    keys, values, keys_t, dkeys, dvalues = refs.take(5)
    low, low_t, normed_t = refs.take(3)
    narrow, wide, act, slope = refs.take(4)
    staging, late0, right_ref, shared, other = refs.take(5)
    merge_low, merge_land, merged, merge_send, merge_recv = refs.take(5)
    in_sem, narrow_sem, feed_sem, stage_sem, late_sem = refs.take(5)

    me = Place()
    place = me.tensor
    tens, rows = qt.shape[0], qt.shape[2]
    width = gx.shape[1]
    hidden = act.shape[2]
    cos, sin = trig_ref[0:HALF], trig_ref[HALF:ROT]
    norms0, norms1 = norm_ref.at[0:4], norm_ref.at[4:8]

    def joined(ref, cols):
        value = ref[:, :, :, cols]
        return value.reshape(width, value.shape[-1])

    def put(ref, start, value):
        cols = value.shape[1]
        ref[:, :, :, start : start + cols] = value.reshape(ref.shape[:3] + (cols,))

    def copies_of(pairs, sem):
        return [
            pltpu.make_async_copy(src, dst, sem.at[k]) for k, (src, dst) in enumerate(pairs)
        ]

    scatter0, scatter1 = (
        Scatter(me, early_in[k], early_out[k], *early_scratch) for k in range(2)
    )
    scatter_late = Scatter(me, late1, late_outs[1], *narrowed(late_scratch, 256))
    scatter_last = Scatter(me, late0_out, late_outs[0], *late_scratch)
    steps1 = list(zip(EARLY_TIMES, scatter1.steps())) + list(zip(LATE_TIMES, scatter_late.steps()))
    steps1.sort(key=lambda entry: entry[0])
    steps0 = list(zip(EARLY_TIMES, scatter0.steps())) + list(zip(LAST_TIMES, scatter_last.steps()))
    steps0.sort(key=lambda entry: entry[0])

    def release(sem):
        for peer in me.peers(False, False):
            pl.semaphore_signal(sem, inc=1, device_id=peer, device_id_type=MESH)

    def narrow_copies(layer):
        return copies_of([(narrow_in[layer].at[t], narrow.at[t]) for t in range(tens)], narrow_sem)

    def feed_back(layer, x, norms, poll, middle):
        def block_of(i):
            core = jnp.where(i < 2, 1 - me.core, me.core)
            return lax.rem(i, 2) * 2 + core

        def feed(t, slot):
            return copies_of(
                [(wide_in[layer].at[t], wide.at[slot]), (act_in[layer].at[t], act.at[slot]),
                 (slope_in[layer].at[t], slope.at[slot])],
                feed_sem.at[slot],
            )

        for copy in feed(block_of(0), 0):
            copy.start()
        mix_back_start(gx, x, norms, low, low_t, normed_t)
        mlp[...] = jnp.zeros_like(mlp)

        def one(i, _):
            t, slot = block_of(i), lax.rem(i, 2)

            @pl.when(i + 1 < tens)
            def _():
                for copy in feed(block_of(i + 1), 1 - slot):
                    copy.start()

            for copy in feed(t, slot):
                copy.wait()
            saved = pltpu.make_async_copy(staging, early_in[layer].at[t], stage_sem)

            @pl.when(i > 0)
            def _():
                saved.wait()

            pl.when(i == 2)(middle)
            mlp[...] += mix_back_part(
                low, low_t, normed_t, at.at[t], act.at[slot], slope.at[slot],
                lambda: joined(narrow.at[t], slice(256, 256 + QW)),
                lambda: joined(wide.at[slot], slice(0, hidden)),
                lambda cols: joined(wide.at[slot], slice(hidden + cols.start, hidden + cols.stop)),
                dout.at[t], functools.partial(put, staging),
                functools.partial(poll, i) if poll else None,
            )
            saved.start()
            return 0

        lax.fori_loop(0, tens, one, 0)
        pltpu.make_async_copy(staging, early_in[layer].at[0], stage_sem).wait()

    loads = copies_of(
        [(gx_in, gx), (x1_in, x1), (at_in[1], at), (qt_in[1], qt), (lse_in[1], lse)], in_sem
    )
    narrow_loads = narrow_copies(1)
    for copy in loads + narrow_loads:
        copy.start()
    me.greet(corner=True)
    attend_back_start(kv_ref[...], keys, values, keys_t)
    dkeys[...] = jnp.zeros_like(dkeys)
    dvalues[...] = jnp.zeros_like(dvalues)
    for copy in loads + narrow_loads:
        copy.wait()

    feed_back(1, x1[...], norms1, None, scatter1.send)
    scatter1.fetch()

    def attention(steps, span):
        due = within(steps, 0, 4 * tens * span)

        def one(t, _):
            attend_back_part(
                place, qt.at[t], dout.at[t], at.at[t], lse.at[t], keys, values, keys_t,
                dkeys, dvalues, gqt.at[t], cos, sin,
                lambda i: timed(due, (t * (place + 1) + i) * span, span),
            )
            return 0

        lax.fori_loop(0, tens, one, 0)
        return tens * (place + 1) * span

    now = attention(steps1, 24)
    seconds = copies_of([(at_in[0], at), (qt_in[0], qt), (lse_in[0], lse)], in_sem)
    for copy in seconds:
        copy.start()

    normed_t[...] = turn(normed_rows(x1[...], norms1[0:1], norms1[1:2])).astype(BF16)
    attn[...] = jnp.zeros_like(attn)

    def second(t, _):
        timed(within(steps1, 90, 470), now + t * 20, 20)
        attn[...] += dot_nt(
            turn(gqt[t, :QW]).astype(BF16), joined(narrow.at[t], slice(0, QW))
        )
        saved = pltpu.make_async_copy(late0, late1.at[t], late_sem.at[0])

        @pl.when(t > 0)
        def _():
            saved.wait()

        put(late0, 0, dot_nt(normed_t[...], gqt[t]).astype(BF16))
        saved.start()
        return 0

    lax.fori_loop(0, tens, second, 0)
    now = now + tens * 20
    narrow_loads = narrow_copies(0)
    for copy in narrow_loads:
        copy.start()
    pltpu.make_async_copy(late0, late1.at[0], late_sem.at[0]).wait()
    scatter_late.begin()
    sums, change = norm_back(x1[...], attn[...], mlp[...], norms1)
    other[...] = sums
    gx[...] += change

    for copy in narrow_loads + seconds:
        copy.wait()
    longest = 4 * tens * 24 + tens * 20
    base = now

    def moment(i, part):
        return jnp.where(i < 2, base, longest) + (i * 4 + part) * 12

    def middle():
        half = longest + 96
        timed(within(steps1, 0, half), base + 96, half - base - 96)
        release(free_sem)
        pl.semaphore_wait(free_sem, 6)
        scatter0.send()

    feed_back(
        0, x0_ref[...].astype(F32), norms0,
        lambda i, part: timed(within(steps1, 170, 660), moment(i, part), 12), middle,
    )
    release(again_sem)
    scatter0.fetch()

    now = attention(steps0, 24)
    for part in range(tens):
        span = slice(part * rows, (part + 1) * rows)
        piece = jnp.concatenate([turn(dkeys[span]), turn(dvalues[span])], axis=0)
        merge_low[part] = piece.astype(BF16)

        @pl.when(place == part)
        def _(piece=piece):
            merged[...] = piece

    merges = [
        remote(merge_low.at[peer[1]], merge_land.at[k], merge_send.at[k], merge_recv.at[k], peer)
        for k, peer in enumerate((me.to_core, me.to_y, me.to_corner))
    ]
    for copy in merges:
        copy.start()
    normed_t[...] = turn(
        normed_rows(x0_ref[...].astype(F32), norms0[0:1], norms0[1:2])
    ).astype(BF16)
    longest = 4 * tens * 24
    timed(steps0, now, longest - now)
    now = longest
    for copy in merges:
        copy.wait_recv()
    merged[...] += (
        merge_land[0].astype(F32) + merge_land[1].astype(F32) + merge_land[2].astype(F32)
    )
    shared_rows(merged[...], cos, sin, shared)
    attn[...] = shared_back(
        shared, joined(narrow.at[0], slice(QW, 256)), joined(narrow.at[0], slice(256 + QW, 512))
    )

    def fourth(t, _):
        timed(within(steps0, 384, 464), now + t * 20, 20)
        grad_t = gqt[t, :QW]
        attn[...] += dot_nt(turn(grad_t).astype(BF16), joined(narrow.at[t], slice(0, QW)))
        left = jnp.concatenate([grad_t, shared[:HD]], axis=0)
        saved = pltpu.make_async_copy(late0, late0_out.at[t, :, :, :, 0:256], late_sem.at[0])

        @pl.when(t > 0)
        def _():
            saved.wait()

        put(late0, 0, dot_nt(normed_t[...], left).astype(BF16))
        saved.start()
        return 0

    lax.fori_loop(0, tens, fourth, 0)
    now = now + tens * 20
    sums, change = norm_back(x0_ref[...].astype(F32), attn[...], mlp[...], norms0)
    gx[...] += change
    put(right_ref, 0, right_columns(shared, normed_t, sums, other[...]))
    saves = [pltpu.make_async_copy(late0, late0_out.at[0, :, :, :, 0:256], late_sem.at[0])]
    for t in range(tens):
        saves.append(
            pltpu.make_async_copy(
                right_ref, late0_out.at[t, :, :, :, 256:384], late_sem.at[1 + t]
            )
        )
        saves[-1].start()
    for copy in saves:
        copy.wait()
    pl.semaphore_wait(again_sem, 6)
    scatter_last.begin()
    saved = pltpu.make_async_copy(gx, grad_out, late_sem.at[1 + tens])
    saved.start()
    timed(steps0, now, 10000)
    saved.wait()
    for copy in merges:
        copy.wait_send()


def backward_call(norms, trig, kv, x0, gx, x1, qts, ats, lses, acts, slopes, narrows, wides):
    rows, width = x0.shape
    tens = qts[0].shape[0]
    length = kv.shape[0]
    hidden = acts[0].shape[2]
    early_cols = 2 * hidden + 256
    depth = width // 8
    weights = [blocks_of(pack) for pack in narrows + wides]
    vmem = pl.BlockSpec(memory_space=pltpu.VMEM)
    anywhere = pl.BlockSpec(memory_space=pl.ANY)
    heads = pltpu.VMEM((tens, 256, rows), BF16)
    state = pltpu.VMEM((rows, width), F32)
    args = [norms, trig, kv, x0, gx, x1, *qts, *ats, *lses, *acts, *slopes, *weights]
    return pl.pallas_call(
        backward_kernel,
        in_specs=[vmem] * 4 + [anywhere] * (len(args) - 4),
        out_specs=[vmem] * 4 + [anywhere] * 5,
        out_shape=[
            jax.ShapeDtypeStruct((depth, early_cols), F32),
            jax.ShapeDtypeStruct((depth, early_cols), F32),
            jax.ShapeDtypeStruct((depth, 384), F32),
            jax.ShapeDtypeStruct((depth, 256), F32),
            jax.ShapeDtypeStruct((rows, width), F32),
            jax.ShapeDtypeStruct((tens, 4, 2, depth, 384), BF16),
            jax.ShapeDtypeStruct((tens, 4, 2, depth, 256), BF16),
            jax.ShapeDtypeStruct((tens, 4, 2, depth, early_cols), BF16),
            jax.ShapeDtypeStruct((tens, 4, 2, depth, early_cols), BF16),
        ],
        scratch_shapes=Scatter.scratch(depth, early_cols)
        + Scatter.scratch(depth, 384)
        + [
            pltpu.SemaphoreType.REGULAR,
            pltpu.SemaphoreType.REGULAR,
            state,
            state,
            state,
            state,
            heads,
            heads,
            pltpu.VMEM((tens, 8, rows), F32),
            heads,
            heads,
            pltpu.VMEM((length, HD), BF16),
            pltpu.VMEM((length, HD), BF16),
            pltpu.VMEM((HD, length), BF16),
            pltpu.VMEM((length, HD), F32),
            pltpu.VMEM((length, HD), F32),
            pltpu.VMEM((rows, width), BF16),
            pltpu.VMEM((width, rows), BF16),
            pltpu.VMEM((width, rows), BF16),
            pltpu.VMEM((tens, 4, 2, depth, 512), BF16),
            pltpu.VMEM((2, 4, 2, depth, 2 * hidden), BF16),
            pltpu.VMEM((2, rows, hidden), BF16),
            pltpu.VMEM((2, rows, hidden), BF16),
            pltpu.VMEM((4, 2, depth, early_cols), BF16),
            pltpu.VMEM((4, 2, depth, 256), BF16),
            pltpu.VMEM((4, 2, depth, 128), BF16),
            pltpu.VMEM((2 * HD, rows), BF16),
            pltpu.VMEM((4, width), F32),
            pltpu.VMEM((tens, 2 * HD, rows), BF16),
            pltpu.VMEM((3, 2 * HD, rows), BF16),
            pltpu.VMEM((2 * HD, rows), F32),
            pltpu.SemaphoreType.DMA((3,)),
            pltpu.SemaphoreType.DMA((3,)),
            pltpu.SemaphoreType.DMA((5,)),
            pltpu.SemaphoreType.DMA((tens,)),
            pltpu.SemaphoreType.DMA((2, 3)),
            pltpu.SemaphoreType.DMA,
            pltpu.SemaphoreType.DMA((tens + 2,)),
        ],
        compiler_params=comm_params(5),
    )(*args)


def lamb_parts(weight, first, second, grad):
    first_new = BETA_FIRST * first + (1.0 - BETA_FIRST) * grad
    second_new = BETA_SECOND * second + (1.0 - BETA_SECOND) * grad * grad
    update = (
        first_new
        / (1.0 - BETA_FIRST**STEP)
        / (jnp.sqrt(second_new / (1.0 - BETA_SECOND**STEP)) + ADAM_EPSILON)
        + WEIGHT_DECAY * weight
    )
    return (first_new, second_new, update)


def keyval_grad(late):
    lane = lax.broadcasted_iota(jnp.int32, (late.shape[0], 2 * HD), 1)
    left = pltpu.roll(late[:, 128:256], HD, 1)
    right = pltpu.roll(late[:, 256:384], HD, 1)
    return jnp.where(lane < HD, left, right)


def norm_grad(late):
    return turn(late[:, 256:384])[HD : HD + 8]


def square(value):
    total = jnp.sum(value * value, axis=1, keepdims=True)
    return jnp.sum(total, axis=0, keepdims=True)


def lanes(pairs):
    lane = lax.broadcasted_iota(jnp.int32, (1, 128), 1)
    row = jnp.zeros((1, 128), F32)
    for place, value in pairs:
        row = jnp.where(lane == place, value, row)
    return row


class Tensors:
    def __init__(self, refs, early, late):
        self.refs = refs
        self.early, self.late = early, late

    def early_grad(self, layer, which):
        pack = self.early[layer]
        hidden = (pack.shape[1] - 256) // 2
        if which == "up":
            return pack[:, :hidden]
        if which == "down":
            return pack[:, hidden : 2 * hidden]
        return turn(pack[:, 2 * hidden :])[:QW]

    def parts(self, array, index, grad):
        weight, first, second = (ref[...] if index is None else ref[index] for ref in array)
        return (weight,) + lamb_parts(weight, first, second, grad)

    def each(self):
        query, keyval, output, upward, downward, norms = range(6)
        for layer in range(2):
            yield 5 + layer, upward, layer, lambda: self.early_grad(layer, "up")
            yield 7 + layer, downward, layer, lambda: self.early_grad(layer, "down")
            yield 3 + layer, output, layer, lambda: self.early_grad(layer, "output")
            yield layer, query, layer, lambda: self.late[layer][:, :QW]
        yield 2, keyval, None, lambda: keyval_grad(self.late[0][...])
        for layer in range(2):
            rows = slice(4 * layer, 4 * layer + 4)
            yield 9 + 4 * layer, norms, layer, lambda: norm_grad(self.late[0][...])[rows]


def norms_kernel(*refs):
    refs = Refs(refs)
    early0, early1, late0, late1 = refs.take(4)
    arrays = [refs.take(3) for _ in range(6)]
    sums_ref = refs.take(1)[0]
    near_land, along_land, send, recv = refs.take(4)
    me = Place()
    me.hail(near=True)
    tensors = Tensors(arrays, (early0, early1), (late0, late1))
    leader = (me.tensor == 0).astype(F32)
    old, new = [], []
    for place, array, index, grad in tensors.each():
        weight, _, _, update = tensors.parts(arrays[array], index, grad())
        if place >= 9:
            for row in range(4):
                old.append((place + row, square(weight[row : row + 1]) * leader))
                new.append((place + row, square(update[row : row + 1]) * leader))
        else:
            scale = leader if place == 2 else 1.0
            old.append((place, square(weight) * scale))
            new.append((place, square(update) * scale))

    me.listen(near=True)
    near_land[0] = jnp.concatenate([lanes(old), lanes(new), jnp.zeros((6, 128), F32)], axis=0)
    copies = []
    for code, peer in me.near():
        copies.append(
            remote(near_land.at[0], near_land.at[code], send.at[code], recv.at[code], peer)
        )
        copies[-1].start()
    for copy in copies:
        copy.wait()
    total = jnp.zeros((8, 128), F32)
    for x in range(2):
        for y in range(2):
            for core in range(2):
                code = lax.rem(x + me.x, 2) * 4 + lax.rem(y + me.y, 2) * 2
                total = total + near_land[code + lax.rem(core + me.core, 2)]
    along_land[0] = total
    copies = []
    for shift in (1, 2, 3):
        copies.append(
            remote(
                along_land.at[0], along_land.at[shift], send.at[7 + shift],
                recv.at[7 + shift], me.at(z=me.along(shift)),
            )
        )
        copies[-1].start()
    for copy in copies:
        copy.wait()
    total = jnp.zeros((8, 128), F32)
    for z in range(4):
        total = total + along_land[me.along(4 - z)]
    sums_ref[...] = total


def norms_call(early, late, arrays):
    vmem = pl.BlockSpec(memory_space=pltpu.VMEM)
    flat = [ref for array in arrays for ref in array]
    return pl.pallas_call(
        norms_kernel,
        in_specs=[vmem] * (4 + len(flat)),
        out_specs=vmem,
        out_shape=jax.ShapeDtypeStruct((8, 128), F32),
        scratch_shapes=[
            pltpu.VMEM((8, 8, 128), F32),
            pltpu.VMEM((4, 8, 128), F32),
            pltpu.SemaphoreType.DMA((11,)),
            pltpu.SemaphoreType.DMA((11,)),
        ],
        compiler_params=comm_params(8),
    )(*early, *late, *flat)


def lamb_kernel(*refs):
    refs = Refs(refs)
    sums_ref, early0, early1, late0, late1 = refs.take(5)
    arrays = [refs.take(3) for _ in range(6)]
    outs = [refs.take(4) for _ in range(6)]
    norm_out, ratio_out = refs.take(2)
    weight_norm = jnp.sqrt(sums_ref[0:1])
    update_norms = jnp.sqrt(sums_ref[1:2])
    used = lax.broadcasted_iota(jnp.int32, (1, 128), 1) < 17
    ratios = jnp.where(used, weight_norm / jnp.where(used, update_norms, 1.0), 0.0)
    norm_out[...] = update_norms
    ratio_out[...] = ratios
    tensors = Tensors(arrays, (early0, early1), (late0, late1))
    for place, array, index, grad in tensors.each():
        weight, first, second, update = tensors.parts(arrays[array], index, grad())
        if place >= 9:
            factor = jnp.concatenate(
                [ratios[:, place + row : place + row + 1] for row in range(4)], axis=0
            )
        else:
            factor = ratios[:, place : place + 1]
        after = weight - LEARN_RATE * factor * update
        where = Ellipsis if index is None else index
        for ref, value in zip(outs[array], (first, second, after, after.astype(BF16))):
            ref[where] = value


def lamb_call(sums, early, late, arrays):
    vmem = pl.BlockSpec(memory_space=pltpu.VMEM)
    flat = [ref for array in arrays for ref in array]
    shapes = []
    for array in arrays:
        shape = array[0].shape
        shapes += [jax.ShapeDtypeStruct(shape, F32)] * 3 + [jax.ShapeDtypeStruct(shape, BF16)]
    shapes += [jax.ShapeDtypeStruct((1, 128), F32)] * 2
    return pl.pallas_call(
        lamb_kernel,
        in_specs=[vmem] * (5 + len(flat)),
        out_specs=[vmem] * len(shapes),
        out_shape=shapes,
        compiler_params=comm_params(None),
    )(sums, *early, *late, *flat)


def angles(places):
    steps = jnp.arange(HALF).astype(F32)
    inverse = jnp.exp(steps * (-2.0 * math.log(10000.0) / ROT))
    phase = (0.25 * inverse)[:, None] * places.astype(F32)[None, :]
    return jnp.concatenate([jnp.cos(phase), jnp.sin(phase)], axis=0)


def param_squares(arrays, leader):
    query, keyval, output, upward, downward, norms = arrays
    return jnp.concatenate(
        [
            jnp.sum(query * query, axis=(1, 2)),
            (jnp.sum(keyval * keyval) * leader)[None],
            jnp.sum(output * output, axis=(1, 2)),
            jnp.sum(upward * upward, axis=(1, 2)),
            jnp.sum(downward * downward, axis=(1, 2)),
            jnp.sum(norms * norms, axis=2).reshape(8) * leader,
        ]
    )


def apply_trust(masters, updates, trust):
    factors = (
        trust[0:2][:, None, None],
        trust[2],
        trust[3:5][:, None, None],
        trust[5:7][:, None, None],
        trust[7:9][:, None, None],
        trust[9:17].reshape(2, 4, 1),
    )
    return tuple(
        (
            weight - LEARN_RATE * factor * update
            for weight, factor, update in zip(masters, factors, updates)
        )
    )


def plain_scatter(parts, depth):
    pieces = parts.reshape(-1, depth, parts.shape[-1])
    return lax.psum_scatter(pieces, ("tensor", "dp"), scatter_dimension=0).astype(F32)


def shards(
    fast,
    hidden_in,
    out_grad,
    positions,
    query_weight,
    keyval_weight,
    output_weight,
    up_weight,
    down_weight,
    norm_params,
    query_first,
    query_second,
    keyval_first,
    keyval_second,
    output_first,
    output_second,
    up_first,
    up_second,
    down_first,
    down_second,
    norm_first,
    norm_second,
):
    masters = (query_weight, keyval_weight, output_weight, up_weight, down_weight, norm_params)
    tensor = lax.axis_index("tensor")
    leader = (tensor == 0).astype(F32)
    rows, width = hidden_in.shape
    tens = positions.shape[0] // rows
    depth = keyval_weight.shape[0]

    def joined(pack):
        return pack.reshape(tens, width, pack.shape[-1])

    trig = angles(lax.dynamic_slice_in_dim(positions, tensor * rows, rows, 0))
    if fast:
        norm_rows, kv, state, act, slope, *others = forward_call(
            hidden_in, trig, masters[:4] + (jnp.swapaxes(down_weight, 1, 2), norm_params)
        )
        norm_full = norm_rows.reshape(2, 4, width)
        kv = kv.reshape(-1, 2 * HD)
        qts, ats, lses = others[0:2], others[2:4], others[4:6]
        attn_all = [joined(others[6]), joined(others[8])]
        feed_all = [joined(others[7]), joined(others[9])]
        saved = [(hidden_in, qts[0], ats[0], lses[0], act, slope)]
        current, act, slope = mix_call(state, norm_full[1], ats[1], attn_all[1], feed_all[1])
        saved.append((state, qts[1], ats[1], lses[1], act, slope))
    else:
        narrow, wide = [], []
        for layer in range(2):
            if layer == 0:
                keys, values = keyval_weight[:, :HD], keyval_weight[:, HD:]
            else:
                keys = values = jnp.zeros((depth, HD), F32)
            pieces = [query_weight[layer], keys, output_weight[layer].T, values]
            narrow.append(jnp.concatenate(pieces, axis=1).astype(BF16))
            wide.append(
                jnp.concatenate([up_weight[layer], down_weight[layer].T], axis=1).astype(BF16)
            )
        norm_low = norm_params.astype(BF16).reshape(8, depth)
        attn_all, feed_all = (
            [joined(lax.all_gather(pack, ("tensor", "dp"), axis=0)) for pack in packs]
            for packs in (narrow, wide)
        )
        norm_full = lax.all_gather(norm_low, "dp", axis=0)
        norm_full = jnp.swapaxes(norm_full, 0, 1).reshape(2, 4, width).astype(F32)
        current = hidden_in
        saved = []
        for layer in range(2):
            norms = norm_full[layer]
            if layer == 0:
                qt, kv = qkv_call(True, current, norms, trig, attn_all[layer])
                kv = share_call(kv, tens).reshape(-1, 2 * HD)
            else:
                (qt,) = qkv_call(False, current, norms, trig, attn_all[layer])
            at, lse = attend_call(qt, kv)
            after, act, slope = mix_call(current, norms, at, attn_all[layer], feed_all[layer])
            saved.append((current, qt, at, lse, act, slope))
            current = after

    x, qt, at, lse, act, slope = saved[1]
    norms = norm_full[1]
    early, late = [None, None], [None, None]
    if fast:
        early[0], early[1], late[0], late[1], grad, *_ = backward_call(
            norm_rows, trig, kv, hidden_in, out_grad, x, qts, ats, lses,
            [saved[0][4], act], [saved[0][5], slope], attn_all, feed_all,
        )
    else:
        pack, dout, mlp = mix_back_call(
            out_grad, x, norms, at, act, slope, attn_all[1], feed_all[1]
        )
        gqt, dkv = attend_back_call(qt, dout, at, lse, kv, trig)
        early[1] = plain_scatter(pack, depth)
        grad, pack, sums = norm_back_call(False, out_grad, x, norms, mlp, gqt, attn_all[1])
        late[1] = plain_scatter(pack, depth)
        x, qt, at, lse, act, slope = saved[0]
        norms = norm_full[0]
        pack, dout, mlp = mix_back_call(
            grad, x, norms, at, act, slope, attn_all[0], feed_all[0]
        )
        early[0] = plain_scatter(pack, depth)
        gqt, dkv = attend_back_call(qt, dout, at, lse, kv, trig, dkv)
        dkv = merge_call(dkv)
        grad, pack = norm_back_call(
            True, grad, x, norms, mlp, gqt, attn_all[0], dkv, trig, sums
        )

    arrays = (
        (query_weight, query_first, query_second),
        (keyval_weight, keyval_first, keyval_second),
        (output_weight, output_first, output_second),
        (up_weight, up_first, up_second),
        (down_weight, down_first, down_second),
        (norm_params, norm_first, norm_second),
    )
    if fast:
        arrays = arrays[:4] + (tuple(jnp.swapaxes(a, 1, 2) for a in arrays[4]),) + arrays[5:]
        totals = norms_call(early, late, arrays)
        *nexts, update_norms, trust_ratios = lamb_call(totals, early, late, arrays)
        nexts[16:20] = [jnp.swapaxes(a, 1, 2) for a in nexts[16:20]]
        return (current, grad, *nexts, update_norms[0, :17], trust_ratios[0, :17])
    late[0] = plain_scatter(pack, depth)
    hidden = up_weight.shape[2]
    query_g = jnp.stack([late[layer][:, :QW] for layer in range(2)])
    keyval_g = late[0][:, QW : QW + 2 * HD]
    output_g = jnp.stack([early[layer][:, 2 * hidden : 2 * hidden + QW].T for layer in range(2)])
    up_g = jnp.stack([early[layer][:, :hidden] for layer in range(2)])
    down_g = jnp.stack([early[layer][:, hidden : 2 * hidden].T for layer in range(2)])
    norm_g = late[0][:, QW + 2 * HD : QW + 2 * HD + 8].T.reshape(2, 4, depth)

    grads = (query_g, keyval_g, output_g, up_g, down_g, norm_g)
    parts = [lamb_parts(*array, grad) for array, grad in zip(arrays, grads)]
    updates = tuple((part[2] for part in parts))
    weight_total, update_total = lax.psum(
        (param_squares(masters, leader), param_squares(updates, leader)), ("dp", "tensor")
    )
    weight_norm = jnp.sqrt(weight_total)
    update_norms = jnp.sqrt(update_total)
    trust_ratios = weight_norm / update_norms
    nexts = apply_trust(masters, updates, trust_ratios)
    outs = [current, grad]
    for index in range(6):
        low = nexts[index].astype(BF16)
        outs += [parts[index][0], parts[index][1], nexts[index], low]
    return tuple(outs) + (update_norms, trust_ratios)


def solution(mesh):
    fast = mesh.shape["dp"] == 8 and mesh.shape["tensor"] == 4
    columns = P(None, "dp", "tensor")
    across = P(None, "tensor", "dp")
    flat = P("dp", None)
    norm = P(None, None, "dp")
    state = P(("dp", "tensor"), None)
    in_specs = (
        (state, state, P("dp"), columns, flat, across, columns, across, norm)
        + (columns, columns, flat, flat, across, across, columns, columns, across, across)
        + (norm, norm)
    )
    out_specs = (
        (state, state)
        + (columns,) * 4
        + (flat,) * 4
        + (across,) * 4
        + (columns,) * 4
        + (across,) * 4
        + (norm,) * 4
        + (P(), P())
    )
    return jax.shard_map(
        functools.partial(shards, fast),
        mesh=mesh,
        in_specs=in_specs,
        out_specs=out_specs,
        check_vma=False,
    )
```

```python
import functools
import math

import jax
import jax.numpy as jnp
from jax import lax
from jax.experimental import pallas as pl
from jax.experimental.pallas import tpu as pltpu
from jax.sharding import PartitionSpec as P

F32 = jnp.float32
BF16 = jnp.bfloat16
MESH = pl.DeviceIdType.MESH

HD = 64
ROT = 16
HALF = ROT // 2
STEP = 5
HEADS_HERE = 3
QW = 192

NORM_EPSILON = 1e-05
BETA_FIRST = 0.5
BETA_SECOND = 0.55
ADAM_EPSILON = 1e-06
WEIGHT_DECAY = 0.01
LEARN_RATE = 0.5
SCALE = HD**-0.5
ROOM = 63 * 2**20


def dot(a, b):
    return jnp.dot(a, b, preferred_element_type=F32)


def dot_nt(a, b):
    return lax.dot_general(a, b, (((1,), (1,)), ((), ())), preferred_element_type=F32)


def turn(a):
    return jnp.transpose(a.astype(F32), (1, 0))


def standard(values):
    center = values - jnp.mean(values, axis=-1, keepdims=True)
    spread = jnp.mean(center * center, axis=-1, keepdims=True)
    inverse = lax.rsqrt(spread + NORM_EPSILON)
    return center * inverse, inverse


def gelu_parts(v):
    x = jnp.abs(v) * (2.0**-0.5)
    bell = jnp.exp(-x * x)
    t = 1.0 / (1.0 + 0.3275911 * x)
    series = t * (
        0.254829592
        + t * (-0.284496736 + t * (1.421413741 + t * (-1.453152027 + t * 1.061405429)))
    )
    tail = 0.5 * series * bell
    cumulative = jnp.where(v < 0.0, tail, 1.0 - tail)
    return cumulative, bell * (1.0 / math.sqrt(2.0 * math.pi))


class Place:
    def __init__(self):
        dp, tensor = lax.axis_index("dp"), lax.axis_index("tensor")
        self.z, self.x = lax.div(dp, 2), lax.rem(dp, 2)
        self.y, self.core = lax.div(tensor, 2), lax.rem(tensor, 2)
        self.tensor = tensor
        self.to_x = self.at(x=1 - self.x)
        self.to_y = self.at(y=1 - self.y)
        self.to_core = self.at(core=1 - self.core)
        self.to_corner = self.at(y=1 - self.y, core=1 - self.core)

    def at(self, z=None, x=None, y=None, core=None):
        z = self.z if z is None else z
        x = self.x if x is None else x
        y = self.y if y is None else y
        core = self.core if core is None else core
        return (z * 2 + x, y * 2 + core)

    def along(self, shift):
        return lax.rem(self.z + shift, 4)

    def near(self):
        return [
            (
                code,
                self.at(
                    x=lax.rem(self.x + code // 4, 2),
                    y=lax.rem(self.y + code // 2 % 2, 2),
                    core=lax.rem(self.core + code % 2, 2),
                ),
            )
            for code in range(1, 8)
        ]

    def peers(self, corner, near):
        peers = [self.at(z=self.along(shift)) for shift in (1, 2, 3)]
        if near:
            peers += [peer for _, peer in self.near()]
        else:
            peers += [self.to_x, self.to_y, self.to_core]
        if corner:
            peers.append(self.to_corner)
        return peers

    def hail(self, corner=False, near=False):
        barrier = pltpu.get_barrier_semaphore()
        for peer in self.peers(corner, near):
            pl.semaphore_signal(barrier, inc=1, device_id=peer, device_id_type=MESH)

    def listen(self, corner=False, near=False):
        pl.semaphore_wait(pltpu.get_barrier_semaphore(), len(self.peers(corner, near)))

    def greet(self, corner=False, near=False):
        self.hail(corner, near)
        self.listen(corner, near)


class Refs:
    def __init__(self, refs):
        self.refs = list(refs)

    def take(self, count):
        taken, self.refs = self.refs[:count], self.refs[count:]
        return taken


def comm_params(ident):
    if ident is None:
        return pltpu.CompilerParams(vmem_limit_bytes=ROOM)
    return pltpu.CompilerParams(
        collective_id=ident, has_side_effects=True, vmem_limit_bytes=ROOM
    )


def remote(src, dst, send, recv, to):
    return pltpu.make_async_remote_copy(
        src_ref=src, dst_ref=dst, send_sem=send, recv_sem=recv, device_id=to, device_id_type=MESH
    )


def timed(steps, now, span):
    if not steps:
        return
    ready = [(now <= due) & (due < now + span) for due, _ in steps]

    @pl.when(functools.reduce(jnp.logical_or, ready))
    def _():
        for now_due, (_, step) in zip(ready, steps):
            pl.when(now_due)(step)


def within(steps, first, last):
    return [entry for entry in steps if first <= entry[0] < last]


class Gather:
    COUNT = 35

    def __init__(self, me, source, out, own_sem, send, recv):
        half = source.shape[0] // 2
        top, low = pl.ds(0, half), pl.ds(half, half)
        other = (1 - me.y) * 2 + me.core
        mine = out.at[me.tensor, me.z, me.x]

        def copy(slot, src, dst, to):
            return remote(src, dst, send.at[slot], recv.at[slot], to)

        parts = {"own": pltpu.make_async_copy(source, mine, own_sem)}
        for d in range(4):
            z = me.along(4 - d)
            block = out.at[me.tensor, z, me.x]
            origin = source if d == 0 else block
            if d > 0:
                parts["z", d] = copy(d - 1, source, mine, me.at(z=me.along(d)))
            parts["x", d] = copy(3 + d, origin, block, me.to_x)
            parts["y", d] = copy(7 + d, origin, block, me.to_y)
            parts["core", d] = copy(11 + d, origin, block, me.to_core)
            from_x, from_y = out.at[me.tensor, z, 1 - me.x], out.at[other, z, me.x]
            parts["xy", d] = copy(15 + d, from_x.at[top], from_x.at[top], me.to_y)
            parts["yx", d] = copy(19 + d, from_y.at[low], from_y.at[low], me.to_x)
            parts["core x", d] = copy(23 + d, from_x, from_x, me.to_core)
            parts["core y", d] = copy(27 + d, from_y, from_y, me.to_core)
            far = out.at[other, z, 1 - me.x]
            parts["core far", d] = copy(31 + d, far, far, me.to_core)
        self.parts = parts

    def along(self, *shifts):
        for d in shifts:
            self.parts["z", d].start()

    def own(self):
        for key in (("x", 0), ("y", 0), ("core", 0), "own"):
            self.parts[key].start()

    def pass_on(self, d):
        self.parts["z", d].wait()
        for way in ("x", "y", "core"):
            self.parts[way, d].start()

    def cross(self, d):
        self.parts["x", d].wait_recv()
        self.parts["xy", d].start()
        self.parts["core x", d].start()
        self.parts["y", d].wait_recv()
        self.parts["yx", d].start()
        self.parts["core y", d].start()

    def far(self, d):
        self.parts["xy", d].wait_recv()
        self.parts["yx", d].wait_recv()
        self.parts["core far", d].start()

    def arrive(self):
        self.parts["own"].wait()
        for key, copy in self.parts.items():
            if key != "own" and key[0].startswith("core"):
                copy.wait_recv()

    def end(self):
        for key, copy in self.parts.items():
            if key != "own" and key[0] != "z":
                copy.wait_send()


def add_rows(total, part):
    def one(i, _):
        rows = pl.ds(pl.multiple_of(i * 16, 16), 16)
        total[rows, :] += part[rows, :]
        return 0

    lax.fori_loop(0, total.shape[0] // 16, one, 0)


class Scatter:
    COUNT = 27

    @staticmethod
    def scratch(rows, cols):
        half = rows // 2
        return [
            pltpu.VMEM((4, 2, 2, rows, cols), BF16),
            pltpu.VMEM((2, 4, 2, rows, cols), BF16),
            pltpu.VMEM((4, 2, half, cols), BF16),
            pltpu.VMEM((4, 2, half, cols), BF16),
            pltpu.VMEM((4, half, cols), BF16),
            pltpu.VMEM((4, half, cols), BF16),
            pltpu.VMEM((3, rows, cols), BF16),
            pltpu.SemaphoreType.DMA((8,)),
            pltpu.SemaphoreType.DMA((Scatter.COUNT,)),
            pltpu.SemaphoreType.DMA((Scatter.COUNT,)),
        ]

    def __init__(
        self, me, source, out, total, from_core, from_x, from_y, turn_x, turn_y, from_z,
        load_sem, send, recv,
    ):
        self.me, self.out, self.total = me, out, total
        self.from_core, self.from_x, self.from_y = from_core, from_x, from_y
        self.turn_x, self.turn_y, self.from_z = turn_x, turn_y, from_z
        half = total.shape[3] // 2
        self.top, self.low = pl.ds(0, half), pl.ds(half, half)
        self.order = [me.along(d) for d in (2, 3, 1, 0)]
        self.parts = parts = {}

        def copy(slot, src, dst, to):
            return remote(src, dst, send.at[slot], recv.at[slot], to)

        for d, z in enumerate(self.order):
            for y in range(2):
                parts["load", d, y] = pltpu.make_async_copy(
                    source.at[2 * y + me.core, z], total.at[z, :, y], load_sem.at[2 * d + y]
                )
                parts["core", d, y] = copy(
                    2 * d + y, source.at[2 * y + 1 - me.core, z], from_core.at[y, z], me.to_core
                )
            parts["x", d] = copy(
                8 + d, total.at[z, 1 - me.x, :, self.top], from_x.at[z], me.to_x
            )
            parts["y", d] = copy(
                12 + d, total.at[z, :, 1 - me.y, self.low], from_y.at[z], me.to_y
            )
            parts["xy", d] = copy(
                16 + d, total.at[z, me.x, 1 - me.y, self.top], turn_y.at[z], me.to_y
            )
            parts["yx", d] = copy(
                20 + d, total.at[z, 1 - me.x, me.y, self.low], turn_x.at[z], me.to_x
            )
            if d < 3:
                parts["z", d] = copy(24 + d, total.at[z, me.x, me.y], from_z.at[d], me.at(z=z))

    def send(self):
        for d in range(4):
            for y in range(2):
                self.parts["core", d, y].start()

    def fetch(self):
        for d in range(4):
            for y in range(2):
                self.parts["load", d, y].start()

    def launch(self, d):
        self.parts["x", d].start()
        self.parts["y", d].start()

    def begin(self):
        self.send()
        self.fetch()

    def core(self, d):
        z = self.order[d]
        for y in range(2):
            self.parts["load", d, y].wait()
            self.parts["core", d, y].wait_recv()
            for x in range(2):
                add_rows(self.total.at[z, x, y], self.from_core.at[y, z, x])
        if d < 2:
            self.launch(d)

    def cross(self, d):
        me, z = self.me, self.order[d]
        self.parts["x", d].wait_recv()
        self.parts["y", d].wait_recv()
        if d < 2:
            self.launch(d + 2)
        for y in range(2):
            add_rows(self.total.at[z, me.x, y, self.top], self.from_x.at[z, y])
        self.parts["xy", d].start()
        for x in range(2):
            add_rows(self.total.at[z, x, me.y, self.low], self.from_y.at[z, x])
        self.parts["yx", d].start()

    def far(self, d):
        me, z = self.me, self.order[d]
        self.parts["xy", d].wait_recv()
        add_rows(self.total.at[z, me.x, me.y, self.top], self.turn_y.at[z])
        self.parts["yx", d].wait_recv()
        add_rows(self.total.at[z, me.x, me.y, self.low], self.turn_x.at[z])
        if d < 3:
            self.parts["z", d].start()

    def end(self):
        me = self.me
        for d in range(3):
            self.parts["z", d].wait_recv()

        def one(i, _):
            rows = pl.ds(pl.multiple_of(i * 16, 16), 16)
            result = self.total[me.z, me.x, me.y, rows, :].astype(F32)
            for d in range(3):
                result = result + self.from_z[d, rows, :].astype(F32)
            self.out[rows, :] = result
            return 0

        lax.fori_loop(0, self.out.shape[0] // 16, one, 0)
        for key, copy in self.parts.items():
            if key[0] != "load":
                copy.wait_send()

    def steps(self):
        order = [
            (self.core, 0), (self.core, 1), (self.core, 2), (self.core, 3), (self.cross, 0),
            (self.cross, 1), (self.far, 0), (self.far, 1), (self.cross, 2), (self.cross, 3),
            (self.far, 2), (self.far, 3),
        ]
        return [functools.partial(step, d) for step, d in order] + [self.end]


def tensor_barrier(count):
    me = lax.axis_index("tensor")
    barrier = pltpu.get_barrier_semaphore()
    for shift in range(1, count):
        pl.semaphore_signal(
            barrier, inc=1, device_id={"tensor": lax.rem(me + shift, count)}, device_id_type=MESH
        )
    pl.semaphore_wait(barrier, count - 1)


def share_kernel(count, mine_ref, out_ref, here_sem, send_sem, recv_sem):
    me = lax.axis_index("tensor")
    tensor_barrier(count)
    copies = []
    for shift in range(1, count):
        copies.append(
            pltpu.make_async_remote_copy(
                src_ref=mine_ref,
                dst_ref=out_ref.at[me],
                send_sem=send_sem.at[shift],
                recv_sem=recv_sem.at[shift],
                device_id={"tensor": lax.rem(me + shift, count)},
                device_id_type=MESH,
            )
        )
        copies[-1].start()
    own = pltpu.make_async_copy(mine_ref, out_ref.at[me], here_sem)
    own.start()
    own.wait()
    for copy in copies:
        copy.wait()


def share_call(mine, count):
    return pl.pallas_call(
        functools.partial(share_kernel, count),
        in_specs=[pl.BlockSpec(memory_space=pltpu.VMEM)],
        out_specs=pl.BlockSpec(memory_space=pltpu.VMEM),
        out_shape=jax.ShapeDtypeStruct((count,) + mine.shape, mine.dtype),
        scratch_shapes=[
            pltpu.SemaphoreType.DMA,
            pltpu.SemaphoreType.DMA((count,)),
            pltpu.SemaphoreType.DMA((count,)),
        ],
        compiler_params=pltpu.CompilerParams(collective_id=9, has_side_effects=True),
    )(mine)


def merge_kernel(count, parts_ref, out_ref, low, landed, send_sem, recv_sem):
    me = lax.axis_index("tensor")
    low[...] = parts_ref[...].astype(BF16)
    tensor_barrier(count)
    copies = []
    for shift in range(1, count):
        to = lax.rem(me + shift, count)
        copies.append(
            pltpu.make_async_remote_copy(
                src_ref=low.at[to],
                dst_ref=landed.at[shift],
                send_sem=send_sem.at[shift],
                recv_sem=recv_sem.at[shift],
                device_id={"tensor": to},
                device_id_type=MESH,
            )
        )
        copies[-1].start()
    total = parts_ref[me]
    for shift, copy in enumerate(copies, 1):
        copy.wait()
        total = total + landed[shift].astype(F32)
    out_ref[...] = total


def merge_call(parts):
    count = parts.shape[0]
    vmem = pl.BlockSpec(memory_space=pltpu.VMEM)
    return pl.pallas_call(
        functools.partial(merge_kernel, count),
        in_specs=[vmem],
        out_specs=vmem,
        out_shape=jax.ShapeDtypeStruct(parts.shape[1:], F32),
        scratch_shapes=[
            pltpu.VMEM(parts.shape, BF16),
            pltpu.VMEM(parts.shape, BF16),
            pltpu.SemaphoreType.DMA((count,)),
            pltpu.SemaphoreType.DMA((count,)),
        ],
        compiler_params=pltpu.CompilerParams(collective_id=10, has_side_effects=True),
    )(parts)


def blocks_of(parts):
    tens, width, cols = parts.shape
    return parts.reshape(tens, 4, 2, width // 8, cols)


def rotated(low, cos, sin):
    first, second = low[:HALF], low[HALF:ROT]
    return jnp.concatenate([first * cos - second * sin, second * cos + first * sin], axis=0)


def put_query(lin, cos, sin, qt_ref):
    for head in range(HEADS_HERE):
        base = head * HD
        low = rotated(lin[base : base + ROT], cos, sin)
        qt_ref[base : base + ROT] = (low.astype(BF16).astype(F32) * SCALE).astype(BF16)
        qt_ref[base + ROT : base + HD] = (
            lin[base + ROT : base + HD].astype(BF16).astype(F32) * SCALE
        ).astype(BF16)
    qt_ref[QW:] = jnp.zeros_like(qt_ref[QW:])


def keyval_rows(lin, value, cos, sin):
    key = jnp.concatenate([rotated(lin[QW : QW + ROT], cos, sin), lin[QW + ROT :]], axis=0)
    return turn(jnp.concatenate([key, value], axis=0)).astype(BF16)


def normed_rows(x, gain, bias):
    return (standard(x)[0] * gain + bias).astype(BF16)


def qkv_kernel(first, x_ref, norm_ref, trig_ref, qk_ref, *rest):
    if first:
        ov_ref, qt_ref, kv_ref, normed = rest
    else:
        qt_ref, normed = rest
    t = pl.program_id(0)

    @pl.when(t == 0)
    def _():
        normed[...] = normed_rows(x_ref[...].astype(F32), norm_ref[0:1], norm_ref[1:2])

    cos, sin = trig_ref[0:HALF], trig_ref[HALF:ROT]
    lin = turn(dot(normed[...], qk_ref[0]))
    put_query(lin, cos, sin, qt_ref.at[0])
    if first:

        @pl.when(t == 0)
        def _():
            value = turn(dot(normed[...], ov_ref[0]))[QW:]
            kv_ref[...] = keyval_rows(lin, value, cos, sin)


def qkv_call(first, x, norms, trig, weights):
    rows, width = x.shape
    tens = weights.shape[0]
    whole = pl.BlockSpec(memory_space=pltpu.VMEM)
    in_specs = [whole, whole, whole, pl.BlockSpec((1, width, 256), lambda t: (t, 0, 0))]
    out_shape = [jax.ShapeDtypeStruct((tens, 256, rows), BF16)]
    out_specs = [pl.BlockSpec((1, 256, rows), lambda t: (t, 0, 0))]
    args = [x, norms, trig, weights]
    if first:
        in_specs.append(pl.BlockSpec((1, width, 256), lambda t: (0, 0, 1)))
        args.append(weights)
        out_shape.append(jax.ShapeDtypeStruct((rows, 2 * HD), BF16))
        out_specs.append(whole)
    return pl.pallas_call(
        functools.partial(qkv_kernel, first),
        grid=(tens,),
        in_specs=in_specs,
        out_specs=out_specs,
        out_shape=out_shape,
        scratch_shapes=[pltpu.VMEM((rows, width), BF16)],
        compiler_params=pltpu.CompilerParams(vmem_limit_bytes=ROOM),
    )(*args)


def attend_part(place, qt_ref, keys, values_t, at_ref, lse_ref, poll=None, between=None):
    rows = qt_ref.shape[1]

    def block(index, carry, diagonal):
        here = pl.ds(pl.multiple_of(index * rows, rows), rows)
        key = keys[here, :]
        value_t = values_t[:, here]
        out = []
        for head in range(HEADS_HERE):
            scores = dot(key, qt_ref[head * HD : (head + 1) * HD])
            if diagonal:
                below = lax.broadcasted_iota(jnp.int32, scores.shape, 0)
                across = lax.broadcasted_iota(jnp.int32, scores.shape, 1)
                scores = jnp.where(below <= across, scores, -1e30)
            peak = jnp.max(scores, axis=0, keepdims=True)
            if carry is not None:
                peak = jnp.maximum(peak, carry[head][0])
            weights = jnp.exp(scores - peak)
            total = jnp.sum(weights, axis=0, keepdims=True)
            mixed = dot(value_t, weights.astype(BF16))
            if carry is not None:
                fade = jnp.exp(carry[head][0] - peak)
                total = total + carry[head][1] * fade
                mixed = mixed + carry[head][2] * fade
            out.append((peak, total, mixed))
        return tuple(out)

    if poll:
        poll(0)
    carry = block(place, None, True)
    if between:
        between()

    def later(i, carry):
        if poll:
            poll(1 + i)
        return block(i, carry, False)

    carry = lax.fori_loop(0, place, later, carry)
    lse_ref[...] = jnp.zeros_like(lse_ref)
    for head in range(HEADS_HERE):
        peak, total, mixed = carry[head]
        at_ref[head * HD : (head + 1) * HD] = (mixed / total).astype(BF16)
        lse_ref[head : head + 1] = peak + jnp.log(total)
    at_ref[QW:] = jnp.zeros_like(at_ref[QW:])


def attend_kernel(qt_ref, kv_ref, at_ref, lse_ref, keys, values_t):
    @pl.when(pl.program_id(0) == 0)
    def _():
        keys[...] = kv_ref[:, :HD]
        values_t[...] = turn(kv_ref[...])[HD:].astype(BF16)

    attend_part(
        lax.axis_index("tensor"), qt_ref.at[0], keys, values_t, at_ref.at[0], lse_ref.at[0]
    )


def attend_call(qt, kv):
    tens, _, rows = qt.shape
    length = kv.shape[0]
    whole = pl.BlockSpec(memory_space=pltpu.VMEM)
    part = pl.BlockSpec((1, 256, rows), lambda t: (t, 0, 0))
    return pl.pallas_call(
        attend_kernel,
        grid=(tens,),
        in_specs=[part, whole],
        out_specs=[part, pl.BlockSpec((1, 8, rows), lambda t: (t, 0, 0))],
        out_shape=[
            jax.ShapeDtypeStruct((tens, 256, rows), BF16),
            jax.ShapeDtypeStruct((tens, 8, rows), F32),
        ],
        scratch_shapes=[pltpu.VMEM((length, HD), BF16), pltpu.VMEM((HD, length), BF16)],
        compiler_params=comm_params(None),
    )(qt, kv)


def mix_part(normed, at_ref, outward, upward, down, act_ref, slope_ref, poll=None):
    attended = turn(at_ref[:QW]).astype(BF16)
    step = 256
    parts = act_ref.shape[1] // step
    for part in range(parts):
        if poll:
            poll(part)
        cols = slice(part * step, (part + 1) * step)
        pre = dot(normed[...], upward(cols))
        cumulative, bell = gelu_parts(pre)
        act_ref[:, cols] = (pre * cumulative).astype(BF16)
        slope_ref[:, cols] = (cumulative + pre * bell).astype(BF16)
    if poll:
        poll(parts)
    return dot_nt(attended, outward()) + dot_nt(act_ref[...], down())


def mix_kernel(
    x_ref, norm_ref, at_ref, o_ref, up_ref, down_ref, out_ref, act_ref, slope_ref, normed, total
):
    t = pl.program_id(0)

    @pl.when(t == 0)
    def _():
        x = x_ref[...].astype(F32)
        normed[...] = normed_rows(x, norm_ref[2:3], norm_ref[3:4])
        total[...] = x

    total[...] += mix_part(
        normed, at_ref.at[0], lambda: o_ref[0, :, :QW], lambda cols: up_ref[0, :, cols],
        lambda: down_ref[0], act_ref.at[0], slope_ref.at[0],
    )

    @pl.when(t == pl.num_programs(0) - 1)
    def _():
        out_ref[...] = total[...]


def mix_call(x, norms, at, outward, feed):
    rows, width = x.shape
    tens = feed.shape[0]
    hidden = feed.shape[2] // 2
    whole = pl.BlockSpec(memory_space=pltpu.VMEM)
    wide = pl.BlockSpec((1, rows, hidden), lambda t: (t, 0, 0))
    return pl.pallas_call(
        mix_kernel,
        grid=(tens,),
        in_specs=[
            whole,
            whole,
            pl.BlockSpec((1, 256, rows), lambda t: (t, 0, 0)),
            pl.BlockSpec((1, width, 256), lambda t: (t, 0, 1)),
            pl.BlockSpec((1, width, hidden), lambda t: (t, 0, 0)),
            pl.BlockSpec((1, width, hidden), lambda t: (t, 0, 1)),
        ],
        out_specs=[whole, wide, wide],
        out_shape=[
            jax.ShapeDtypeStruct((rows, width), F32),
            jax.ShapeDtypeStruct((tens, rows, hidden), BF16),
            jax.ShapeDtypeStruct((tens, rows, hidden), BF16),
        ],
        scratch_shapes=[pltpu.VMEM((rows, width), BF16), pltpu.VMEM((rows, width), F32)],
        compiler_params=comm_params(None),
    )(x, norms, at, outward, feed, feed)


def mix_back_part(
    low, low_t, normed_t, at_ref, act_ref, slope_ref, outward, upward, down, dot_ref, pack_put,
    poll=None,
):
    hidden = act_ref.shape[1]
    if poll:
        poll(0)
    grad_attended = dot(low[...], outward())
    dot_ref[:QW] = turn(grad_attended).astype(BF16)
    dot_ref[QW:] = jnp.zeros_like(dot_ref[QW:])
    pack_put(2 * hidden, dot_nt(low_t[...], at_ref[...]).astype(BF16))
    if poll:
        poll(1)
    for start in range(0, hidden, 256):
        cols = slice(start, start + 256)
        pack_put(hidden + start, dot(low_t[...], act_ref[:, cols]).astype(BF16))
    if poll:
        poll(2)
    grad_pre = []
    for start in range(0, hidden, 256):
        cols = slice(start, start + 256)
        grad = (dot(low[...], down(cols)) * slope_ref[:, cols].astype(F32)).astype(BF16)
        pack_put(start, dot(normed_t[...], grad).astype(BF16))
        grad_pre.append(grad)
    if poll:
        poll(3)
    return dot_nt(jnp.concatenate(grad_pre, axis=1), upward())


def mix_back_start(gx_ref, x, norm_ref, low, low_t, normed_t):
    grad = gx_ref[...].astype(BF16)
    low[...] = grad
    low_t[...] = turn(grad).astype(BF16)
    normed_t[...] = turn(normed_rows(x, norm_ref[2:3], norm_ref[3:4])).astype(BF16)


def mix_back_kernel(
    gx_ref, x_ref, norm_ref, at_ref, act_ref, slope_ref, o_ref, up_ref, down_ref,
    pack_ref, dot_ref, mlp_ref, low, low_t, normed_t,
):
    @pl.when(pl.program_id(0) == 0)
    def _():
        mix_back_start(gx_ref, x_ref[...].astype(F32), norm_ref, low, low_t, normed_t)
        mlp_ref[...] = jnp.zeros_like(mlp_ref)

    def pack_put(start, value):
        pack_ref[0, :, start : start + value.shape[1]] = value

    mlp_ref[...] += mix_back_part(
        low, low_t, normed_t, at_ref.at[0], act_ref.at[0], slope_ref.at[0],
        lambda: o_ref[0, :, :QW], lambda: up_ref[0], lambda cols: down_ref[0, :, cols],
        dot_ref.at[0], pack_put,
    )


def mix_back_call(gx, x, norms, at, act, slope, outward, feed):
    rows, width = x.shape
    tens = feed.shape[0]
    hidden = act.shape[2]
    whole = pl.BlockSpec(memory_space=pltpu.VMEM)
    wide = pl.BlockSpec((1, rows, hidden), lambda t: (t, 0, 0))
    part = pl.BlockSpec((1, 256, rows), lambda t: (t, 0, 0))
    return pl.pallas_call(
        mix_back_kernel,
        grid=(tens,),
        in_specs=[
            whole,
            whole,
            whole,
            part,
            wide,
            wide,
            pl.BlockSpec((1, width, 256), lambda t: (t, 0, 1)),
            pl.BlockSpec((1, width, hidden), lambda t: (t, 0, 0)),
            pl.BlockSpec((1, width, hidden), lambda t: (t, 0, 1)),
        ],
        out_specs=[pl.BlockSpec((1, width, 2 * hidden + 256), lambda t: (t, 0, 0)), part, whole],
        out_shape=[
            jax.ShapeDtypeStruct((tens, width, 2 * hidden + 256), BF16),
            jax.ShapeDtypeStruct((tens, 256, rows), BF16),
            jax.ShapeDtypeStruct((rows, width), F32),
        ],
        scratch_shapes=[
            pltpu.VMEM((rows, width), BF16),
            pltpu.VMEM((width, rows), BF16),
            pltpu.VMEM((width, rows), BF16),
        ],
        compiler_params=comm_params(None),
    )(gx, x, norms, at, act, slope, outward, feed, feed)


def attend_back_start(kv, keys, values, keys_t):
    both_t = turn(kv)
    keys[...] = kv[:, :HD]
    keys_t[...] = both_t[:HD].astype(BF16)
    values[...] = turn(both_t[HD:]).astype(BF16)


def attend_back_part(
    place, qt_ref, dot_ref, at_ref, lse_ref, keys, values, keys_t, dkeys, dvalues, gqt_ref,
    cos, sin, poll=None,
):
    rows = qt_ref.shape[1]
    inner = []
    for head in range(HEADS_HERE):
        span = slice(head * HD, (head + 1) * HD)
        inner.append(
            jnp.sum(
                dot_ref[span].astype(F32) * at_ref[span].astype(F32), axis=0, keepdims=True
            )
        )

    def block(index, carry, diagonal):
        here = pl.ds(pl.multiple_of(index * rows, rows), rows)
        key = keys[here, :]
        value = values[here, :]
        key_t = keys_t[:, here]
        out = []
        dkey = dvalue = None
        for head in range(HEADS_HERE):
            span = slice(head * HD, (head + 1) * HD)
            query_t = qt_ref[span]
            grad_t = dot_ref[span]
            scores = dot(key, query_t)
            probs = jnp.exp(scores - lse_ref[head : head + 1])
            if diagonal:
                below = lax.broadcasted_iota(jnp.int32, scores.shape, 0)
                across = lax.broadcasted_iota(jnp.int32, scores.shape, 1)
                probs = jnp.where(below <= across, probs, 0.0)
            grad_probs = dot(value, grad_t)
            grad_scores = (probs * (grad_probs - inner[head])).astype(BF16)
            part_v = dot_nt(probs.astype(BF16), grad_t)
            part_k = dot_nt(grad_scores, query_t)
            dkey = part_k if head == 0 else dkey + part_k
            dvalue = part_v if head == 0 else dvalue + part_v
            part_q = dot(key_t, grad_scores)
            out.append(part_q if carry is None else carry[head] + part_q)
        dkeys[here, :] += dkey
        dvalues[here, :] += dvalue
        return tuple(out)

    def later(i, carry):
        if poll:
            poll(1 + i)
        return block(i, carry, False)

    if poll:
        poll(0)
    carry = block(place, None, True)
    carry = lax.fori_loop(0, place, later, carry)
    for head in range(HEADS_HERE):
        base = head * HD
        grad = carry[head] * SCALE
        gqt_ref[base : base + ROT] = rotated(grad[:ROT], cos, -sin).astype(BF16)
        gqt_ref[base + ROT : base + HD] = grad[ROT:].astype(BF16)
    gqt_ref[QW:] = jnp.zeros_like(gqt_ref[QW:])


def attend_back_kernel(start_given, *refs):
    refs = Refs(refs)
    qt_ref, dot_ref, at_ref, lse_ref, kv_ref, trig_ref = refs.take(6)
    before_ref = refs.take(1)[0] if start_given else None
    gqt_ref, dkv_ref, keys, values, keys_t, dkeys, dvalues = refs.take(7)
    t = pl.program_id(0)
    rows = qt_ref.shape[2]

    @pl.when(t == 0)
    def _():
        attend_back_start(kv_ref[...], keys, values, keys_t)
        dkeys[...] = jnp.zeros_like(dkeys)
        dvalues[...] = jnp.zeros_like(dvalues)

    attend_back_part(
        lax.axis_index("tensor"), qt_ref.at[0], dot_ref.at[0], at_ref.at[0], lse_ref.at[0],
        keys, values, keys_t, dkeys, dvalues, gqt_ref.at[0],
        trig_ref[0:HALF], trig_ref[HALF:ROT],
    )

    @pl.when(t == pl.num_programs(0) - 1)
    def _():
        both = jnp.concatenate([turn(dkeys[...]), turn(dvalues[...])], axis=0)
        for part in range(dkv_ref.shape[0]):
            piece = both[:, part * rows : (part + 1) * rows]
            if start_given:
                piece = piece + before_ref[part]
            dkv_ref[part] = piece


def attend_back_call(qt, dout, at, lse, kv, trig, before=None):
    tens, _, rows = qt.shape
    length = kv.shape[0]
    whole = pl.BlockSpec(memory_space=pltpu.VMEM)
    part = pl.BlockSpec((1, 256, rows), lambda t: (t, 0, 0))
    args = [qt, dout, at, lse, kv, trig]
    in_specs = [part, part, part, pl.BlockSpec((1, 8, rows), lambda t: (t, 0, 0)), whole, whole]
    if before is not None:
        args.append(before)
        in_specs.append(whole)
    return pl.pallas_call(
        functools.partial(attend_back_kernel, before is not None),
        grid=(tens,),
        in_specs=in_specs,
        out_specs=[part, whole],
        out_shape=[
            jax.ShapeDtypeStruct((tens, 256, rows), BF16),
            jax.ShapeDtypeStruct((length // rows, 2 * HD, rows), F32),
        ],
        scratch_shapes=[
            pltpu.VMEM((length, HD), BF16),
            pltpu.VMEM((length, HD), BF16),
            pltpu.VMEM((HD, length), BF16),
            pltpu.VMEM((length, HD), F32),
            pltpu.VMEM((length, HD), F32),
        ],
        compiler_params=comm_params(None),
    )(*args)


def shared_rows(grad, cos, sin, shared):
    shared[:ROT] = rotated(grad[:ROT], cos, -sin).astype(BF16)
    shared[ROT:] = grad[ROT:].astype(BF16)


def shared_back(shared, key_weight, value_weight):
    return dot_nt(turn(shared[:HD]).astype(BF16), key_weight) + dot_nt(
        turn(shared[HD:]).astype(BF16), value_weight
    )


def right_columns(shared, normed_t, sums, other):
    pad = jnp.zeros((HD, sums.shape[1]), F32)
    lower = turn(jnp.concatenate([pad, sums, other, pad[8:]], axis=0))
    upper = jnp.concatenate([shared[HD:], jnp.zeros_like(shared[HD:])], axis=0)
    return (dot_nt(normed_t[...], upper) + lower).astype(BF16)


def norm_back(x, attn_grad, mlp_grad, norm_ref):
    unit, inverse = standard(x)
    sums = jnp.concatenate(
        [
            jnp.sum(attn_grad * unit, axis=0, keepdims=True),
            jnp.sum(attn_grad, axis=0, keepdims=True),
            jnp.sum(mlp_grad * unit, axis=0, keepdims=True),
            jnp.sum(mlp_grad, axis=0, keepdims=True),
        ],
        axis=0,
    )
    grad = attn_grad * norm_ref[0:1] + mlp_grad * norm_ref[2:3]
    mean = jnp.mean(grad, axis=-1, keepdims=True)
    slant = jnp.mean(grad * unit, axis=-1, keepdims=True)
    return sums, inverse * (grad - mean - unit * slant)


def norm_back_kernel(first, gx_ref, x_ref, norm_ref, mlp_ref, gqt_ref, qk_ref, *rest):
    if first:
        ov_ref, dkv_ref, trig_ref, other_ref, out_ref, pack_ref, normed_t, attn, shared = rest
    else:
        out_ref, pack_ref, sums_ref, normed_t, attn = rest
    t = pl.program_id(0)

    @pl.when(t == 0)
    def _():
        x = x_ref[...].astype(F32)
        normed = (standard(x)[0] * norm_ref[0:1] + norm_ref[1:2]).astype(BF16)
        normed_t[...] = turn(normed).astype(BF16)
        if first:
            cos, sin = trig_ref[0:HALF], trig_ref[HALF:ROT]
            shared_rows(dkv_ref[...], cos, sin, shared)
            attn[...] = shared_back(shared, qk_ref[0, :, QW:], ov_ref[0, :, QW:])
        else:
            attn[...] = jnp.zeros_like(attn)

    grad_t = gqt_ref[0, :QW]
    attn[...] += dot_nt(turn(grad_t).astype(BF16), qk_ref[0, :, :QW])
    if first:
        left = jnp.concatenate([grad_t, shared[:HD]], axis=0)
        pack_ref[t, :, :256] = dot_nt(normed_t[...], left).astype(BF16)
    else:
        pack_ref[0] = dot_nt(normed_t[...], gqt_ref[0]).astype(BF16)

    @pl.when(t == pl.num_programs(0) - 1)
    def _():
        sums, change = norm_back(x_ref[...].astype(F32), attn[...], mlp_ref[...], norm_ref)
        if first:
            right = right_columns(shared, normed_t, sums, other_ref[...])
            for part in range(pack_ref.shape[0]):
                pack_ref[part, :, 256:] = right
        else:
            sums_ref[...] = sums
        out_ref[...] = gx_ref[...] + change


def norm_back_call(first, gx, x, norms, mlp, gqt, weights, dkv=None, trig=None, other=None):
    rows, width = x.shape
    tens = weights.shape[0]
    whole = pl.BlockSpec(memory_space=pltpu.VMEM)
    part = pl.BlockSpec((1, 256, rows), lambda t: (t, 0, 0))
    args = [gx, x, norms, mlp, gqt, weights]
    in_specs = [whole] * 4 + [part, pl.BlockSpec((1, width, 256), lambda t: (t, 0, 0))]
    scratch = [pltpu.VMEM((width, rows), BF16), pltpu.VMEM((rows, width), F32)]
    out_shape = [jax.ShapeDtypeStruct((rows, width), F32)]
    if first:
        args += [weights, dkv, trig, other]
        in_specs += [pl.BlockSpec((1, width, 256), lambda t: (0, 0, 1)), whole, whole, whole]
        scratch.append(pltpu.VMEM((2 * HD, rows), BF16))
        out_shape.append(jax.ShapeDtypeStruct((tens, width, 384), BF16))
        out_specs = [whole, whole]
    else:
        out_shape.append(jax.ShapeDtypeStruct((tens, width, 256), BF16))
        out_shape.append(jax.ShapeDtypeStruct((4, width), F32))
        out_specs = [whole, pl.BlockSpec((1, width, 256), lambda t: (t, 0, 0)), whole]
    return pl.pallas_call(
        functools.partial(norm_back_kernel, first),
        grid=(tens,),
        in_specs=in_specs,
        out_specs=out_specs,
        out_shape=out_shape,
        scratch_shapes=scratch,
        compiler_params=comm_params(None),
    )(*args)


QUERY_START = (240, 741)
ATTEND_START = (275, 781)
ATTEND_SPAN = 17
MIX_START, MIX_SPAN = 581, 10
GATHER_TIMES = (
    (1, "cross", 0, 250),
    (2, "along", 1, 255),
    (2, "along", 2, 257),
    (2, "along", 3, 266),
    (1, "pass_on", 3, 290),
    (1, "cross", 1, 330),
    (1, "far", 0, 335),
    (1, "pass_on", 2, 365),
    (3, "along", 1, 370),
    (3, "along", 3, 371),
    (1, "cross", 3, 430),
    (1, "far", 1, 435),
    (2, "own", None, 480),
    (2, "pass_on", 1, 481),
    (2, "pass_on", 3, 482),
    (2, "pass_on", 2, 483),
    (1, "cross", 2, 490),
    (1, "far", 3, 505),
    (1, "far", 2, 550),
    (3, "along", 2, 582),
    (2, "cross", 0, 590),
    (2, "cross", 1, 600),
    (2, "far", 0, 605),
    (3, "own", None, 606),
    (3, "pass_on", 1, 607),
    (2, "cross", 3, 620),
    (2, "far", 1, 625),
    (2, "cross", 2, 640),
    (3, "pass_on", 3, 645),
    (2, "far", 3, 650),
    (2, "far", 2, 665),
    (3, "cross", 0, 732),
    (3, "pass_on", 2, 770),
    (3, "cross", 1, 800),
    (3, "far", 0, 805),
    (3, "cross", 3, 860),
    (3, "far", 1, 865),
    (3, "cross", 2, 920),
    (3, "far", 3, 925),
    (3, "far", 2, 970),
)


def pack_narrow(pack, wide, query, output, keyval):
    wide[...] = jnp.zeros_like(wide)
    wide[:, 0:QW] = query
    wide[:, 256 : 256 + QW] = turn(output)
    if keyval is not None:
        upper = lax.broadcasted_iota(jnp.int32, keyval.shape, 1) >= HD
        wide[:, 128:256] += jnp.where(upper, pltpu.roll(keyval, HD, 1), 0.0)
        wide[:, 384:512] += jnp.where(upper, keyval, 0.0)
    pack[...] = wide[...].astype(BF16)


def forward_kernel(*refs):
    refs = Refs(refs)
    x_ref, trig_ref = refs.take(2)
    masters = refs.take(6)
    norm_ref, norm1_ref, kv_out, state_out, act_out, slope_out = refs.take(6)
    qt_outs, at_outs, lse_outs = refs.take(2), refs.take(2), refs.take(2)
    packs = refs.take(4)
    own_sem, send, recv = refs.take(3)
    sources, (spread_ref, small_ref) = refs.take(4), refs.take(2)
    small_land, small_own, small_send, small_recv = refs.take(4)
    kv_here, landed, kv_send, kv_recv = refs.take(4)
    narrow, wide, load_sem = refs.take(3)
    normed, total, qt, at, lse, act, slope, keys, values_t, save_sem = refs.take(10)

    me = Place()
    place = me.tensor
    tens, rows = qt.shape[1], qt.shape[3]
    width = total.shape[1]
    hidden = act.shape[2]
    gathers = [
        Gather(me, sources[k], packs[k], own_sem.at[k], send.at[k], recv.at[k]) for k in range(4)
    ]
    steps = []
    for k, what, which, due in GATHER_TIMES:
        action = getattr(gathers[k], what)
        steps.append((due, action if which is None else functools.partial(action, which)))
    mine = small_land.at[me.z, me.x]
    small_mine = pltpu.make_async_copy(small_ref, mine, small_own)
    small_along = [
        remote(small_ref, mine, small_send.at[d], small_recv.at[d], me.at(z=me.along(d)))
        for d in (1, 2, 3)
    ]
    column = small_land.at[:, me.x]
    small_across = remote(column, column, small_send.at[0], small_recv.at[0], me.to_x)
    kv_copies = [
        remote(kv_here, landed.at[place], kv_send.at[k], kv_recv.at[k], peer)
        for k, peer in enumerate((me.to_core, me.to_y, me.to_corner))
    ]
    saves = []

    def save(src, dst):
        copy = pltpu.make_async_copy(src, dst, save_sem.at[len(saves)])
        copy.start()
        saves.append(copy)

    def load(k, buffer, slot):
        return [
            pltpu.make_async_copy(packs[k].at[t], buffer.at[t], load_sem.at[slot, t])
            for t in range(tens)
        ]

    def joined(buffer, t, cols):
        value = buffer[t, :, :, :, cols]
        return value.reshape(width, value.shape[-1])

    me.hail(corner=True)
    query_ref, keyval_ref, output_ref, up_ref, down_ref, param_ref = masters
    small_ref[...] = turn(
        jnp.concatenate(
            [param_ref[0], param_ref[1], jnp.zeros((120, param_ref.shape[2]), F32)], axis=0
        )
    ).astype(BF16)
    pack_narrow(sources[0], spread_ref, query_ref[0], output_ref[0], keyval_ref[...])
    me.listen(corner=True)
    small_mine.start()
    for copy in small_along:
        copy.start()
    first, second = gathers[:2]
    first.along(1, 3, 2)
    first.own()
    sources[1][:, :hidden] = up_ref[0].astype(BF16)
    sources[1][:, hidden:] = down_ref[0].astype(BF16)
    second.own()
    x = x_ref[...].astype(F32)
    total[...] = standard(x)[0]
    first.pass_on(1)
    small_mine.wait()
    for copy in small_along:
        copy.wait_recv()
    small_across.start()
    first.cross(0)
    second.along(1, 3)
    first.pass_on(3)
    first.cross(1)
    first.far(0)
    first.pass_on(2)
    second.along(2)
    pack_narrow(sources[2], spread_ref, query_ref[1], output_ref[1], None)
    sources[3][:, :hidden] = up_ref[1].astype(BF16)
    sources[3][:, hidden:] = down_ref[1].astype(BF16)
    small_across.wait_recv()
    norm_ref[...] = turn(small_land[...].reshape(width, 128))[:8]
    norm1_ref[...] = norm_ref[4:8]
    normed[...] = (total[...] * norm_ref[0:1] + norm_ref[1:2]).astype(BF16)
    first.cross(3)
    first.far(1)
    first.cross(2)
    second.pass_on(1)
    first.far(3)
    first.far(2)
    first.arrive()
    loads = load(0, narrow.at[0], 0)
    for copy in loads:
        copy.start()
    for copy in small_along + [small_across]:
        copy.wait_send()
    gathers[0].end()

    cos, sin = trig_ref[0:HALF], trig_ref[HALF:ROT]

    def qkv(layer, loads):
        due = within(steps, QUERY_START[layer], ATTEND_START[layer])
        span = (ATTEND_START[layer] - QUERY_START[layer] + tens - 1) // tens

        def one(t, _):
            timed(due, QUERY_START[layer] + t * span, span)
            for part, copy in enumerate(loads):
                pl.when(t == part)(copy.wait)
            lin = turn(dot(normed[...], joined(narrow.at[layer], t, slice(0, 256))))
            put_query(lin, cos, sin, qt.at[layer, t])
            if layer == 0:

                @pl.when(t == 0)
                def _():
                    value = turn(dot(normed[...], joined(narrow.at[0], 0, slice(384, 512))))
                    kv_here[...] = keyval_rows(lin, value[HD:], cos, sin)
                    for copy in kv_copies:
                        copy.start()

            return 0

        lax.fori_loop(0, tens, one, 0)

    def attention(layer, last, between=None):
        start = ATTEND_START[layer]
        due = within(steps, start, last)

        def one(t, _):
            def first():
                if between:
                    pl.when(t == 0)(between)

            attend_part(
                place, qt.at[layer, t], keys, values_t, at.at[layer, t], lse.at[layer, t],
                lambda i: timed(due, start + (t * (place + 1) + i) * ATTEND_SPAN, ATTEND_SPAN),
                first,
            )
            return 0

        lax.fori_loop(0, tens, one, 0)
        now = start + tens * (place + 1) * ATTEND_SPAN
        timed(due, now, last - now)
        save(qt.at[layer], qt_outs[layer])
        save(at.at[layer], at_outs[layer])
        save(lse.at[layer], lse_outs[layer])

    qkv(0, loads)
    here = pl.ds(pl.multiple_of(place * rows, rows), rows)
    landed[place] = kv_here[...]
    keys[here, :] = kv_here[:, :HD]
    values_t[:, here] = turn(kv_here[...])[HD:].astype(BF16)

    def meet():
        for copy in kv_copies:
            copy.wait()
        for part in range(tens):
            span = pl.ds(part * rows, rows)
            keys[span, :] = landed[part, :, :HD]
            values_t[:, span] = turn(landed[part])[HD:].astype(BF16)

    attention(0, MIX_START, meet)
    save(landed, kv_out)
    gathers[1].arrive()
    loads = load(1, wide, 1)
    for copy in loads:
        copy.start()
    gathers[1].end()
    x = x_ref[...].astype(F32)
    normed[...] = normed_rows(x, norm_ref[2:3], norm_ref[3:4])
    total[...] = x
    wide_loads = loads

    due = within(steps, MIX_START, QUERY_START[1])

    def mix(t, _):
        for part, copy in enumerate(wide_loads):
            pl.when(t == part)(copy.wait)
        total[...] += mix_part(
            normed, at.at[0, t], lambda: joined(narrow.at[0], t, slice(256, 256 + QW)),
            lambda cols: joined(wide, t, cols),
            lambda: joined(wide, t, slice(hidden, 2 * hidden)), act.at[t], slope.at[t],
            lambda i: timed(due, MIX_START + (t * 4 + i) * MIX_SPAN, MIX_SPAN),
        )
        return 0

    lax.fori_loop(0, tens, mix, 0)
    save(total, state_out)
    save(act, act_out)
    save(slope, slope_out)
    gathers[2].arrive()
    loads = load(2, narrow.at[1], 2)
    for copy in loads:
        copy.start()
    gathers[2].end()
    normed[...] = normed_rows(total[...], norm_ref[4:5], norm_ref[5:6])
    qkv(1, loads)
    attention(1, 10000)
    gathers[3].arrive()
    gathers[3].end()
    for copy in saves:
        copy.wait()


def forward_call(x, trig, masters):
    rows, width = x.shape
    tens = 4
    _, depth, hidden = masters[3].shape
    packs = [(depth, 512), (depth, 2 * hidden)] * 2
    vmem = pl.BlockSpec(memory_space=pltpu.VMEM)
    anywhere = pl.BlockSpec(memory_space=pl.ANY)
    heads = jax.ShapeDtypeStruct((tens, 256, rows), BF16)
    sums = jax.ShapeDtypeStruct((tens, 8, rows), F32)
    feed = jax.ShapeDtypeStruct((tens, rows, hidden), BF16)
    out_shape = [
        jax.ShapeDtypeStruct((8, width), F32),
        jax.ShapeDtypeStruct((4, width), F32),
        jax.ShapeDtypeStruct((tens, rows, 2 * HD), BF16),
        jax.ShapeDtypeStruct((rows, width), F32),
        feed,
        feed,
        heads,
        heads,
        heads,
        heads,
        sums,
        sums,
    ] + [jax.ShapeDtypeStruct((4, 4, 2) + pack, BF16) for pack in packs]
    return pl.pallas_call(
        forward_kernel,
        in_specs=[vmem] * 8,
        out_specs=[vmem, vmem] + [anywhere] * (len(out_shape) - 2),
        out_shape=out_shape,
        scratch_shapes=[
            pltpu.SemaphoreType.DMA((4,)),
            pltpu.SemaphoreType.DMA((4, Gather.COUNT)),
            pltpu.SemaphoreType.DMA((4, Gather.COUNT)),
            *[pltpu.VMEM(pack, BF16) for pack in packs],
            pltpu.VMEM((depth, 512), F32),
            pltpu.VMEM((depth, 128), BF16),
            pltpu.VMEM((4, 2, depth, 128), BF16),
            pltpu.SemaphoreType.DMA,
            pltpu.SemaphoreType.DMA((4,)),
            pltpu.SemaphoreType.DMA((4,)),
            pltpu.VMEM((rows, 2 * HD), BF16),
            pltpu.VMEM((tens, rows, 2 * HD), BF16),
            pltpu.SemaphoreType.DMA((3,)),
            pltpu.SemaphoreType.DMA((3,)),
            pltpu.VMEM((2, tens, 4, 2, depth, 512), BF16),
            pltpu.VMEM((tens, 4, 2, depth, 2 * hidden), BF16),
            pltpu.SemaphoreType.DMA((3, tens)),
            pltpu.VMEM((rows, width), BF16),
            pltpu.VMEM((rows, width), F32),
            pltpu.VMEM((2, tens, 256, rows), BF16),
            pltpu.VMEM((2, tens, 256, rows), BF16),
            pltpu.VMEM((2, tens, 8, rows), F32),
            pltpu.VMEM((tens, rows, hidden), BF16),
            pltpu.VMEM((tens, rows, hidden), BF16),
            pltpu.VMEM((tens * rows, HD), BF16),
            pltpu.VMEM((HD, tens * rows), BF16),
            pltpu.SemaphoreType.DMA((10,)),
        ],
        compiler_params=comm_params(1),
    )(x, trig, *masters)


EARLY_TIMES = (5, 10, 30, 55, 150, 180, 275, 300, 315, 400, 425, 470, 545)
LATE_TIMES = (500, 510, 515, 520, 530, 540, 550, 555, 560, 570, 580, 590, 640)
LAST_TIMES = (475, 476, 477, 478, 500, 505, 520, 525, 530, 535, 548, 555, 600)


def narrowed(scratch, cols):
    lanes = pl.ds(0, cols)
    views = [ref.at[(slice(None),) * (len(ref.shape) - 1) + (lanes,)] for ref in scratch[:7]]
    return views + list(scratch[7:])


def backward_kernel(*refs):
    refs = Refs(refs)
    norm_ref, trig_ref, kv_ref, x0_ref = refs.take(4)
    gx_in, x1_in = refs.take(2)
    qt_in, at_in, lse_in = refs.take(2), refs.take(2), refs.take(2)
    act_in, slope_in, narrow_in, wide_in = [refs.take(2) for _ in range(4)]
    early_out, late_outs = refs.take(2), refs.take(2)
    grad_out, late0_out, late1 = refs.take(3)
    early_in = refs.take(2)
    early_scratch, late_scratch = refs.take(10), refs.take(10)
    free_sem, again_sem = refs.take(2)
    gx, x1, mlp, attn = refs.take(4)
    qt, at, lse, dout, gqt = refs.take(5)
    keys, values, keys_t, dkeys, dvalues = refs.take(5)
    low, low_t, normed_t = refs.take(3)
    narrow, wide, act, slope = refs.take(4)
    staging, late0, right_ref, shared, other = refs.take(5)
    merge_low, merge_land, merged, merge_send, merge_recv = refs.take(5)
    in_sem, narrow_sem, feed_sem, stage_sem, late_sem = refs.take(5)

    me = Place()
    place = me.tensor
    tens, rows = qt.shape[0], qt.shape[2]
    width = gx.shape[1]
    hidden = act.shape[2]
    cos, sin = trig_ref[0:HALF], trig_ref[HALF:ROT]
    norms0, norms1 = norm_ref.at[0:4], norm_ref.at[4:8]

    def joined(ref, cols):
        value = ref[:, :, :, cols]
        return value.reshape(width, value.shape[-1])

    def put(ref, start, value):
        cols = value.shape[1]
        ref[:, :, :, start : start + cols] = value.reshape(ref.shape[:3] + (cols,))

    def copies_of(pairs, sem):
        return [
            pltpu.make_async_copy(src, dst, sem.at[k]) for k, (src, dst) in enumerate(pairs)
        ]

    scatter0, scatter1 = (
        Scatter(me, early_in[k], early_out[k], *early_scratch) for k in range(2)
    )
    scatter_late = Scatter(me, late1, late_outs[1], *narrowed(late_scratch, 256))
    scatter_last = Scatter(me, late0_out, late_outs[0], *late_scratch)
    steps1 = list(zip(EARLY_TIMES, scatter1.steps())) + list(zip(LATE_TIMES, scatter_late.steps()))
    steps1.sort(key=lambda entry: entry[0])
    steps0 = list(zip(EARLY_TIMES, scatter0.steps())) + list(zip(LAST_TIMES, scatter_last.steps()))
    steps0.sort(key=lambda entry: entry[0])

    def release(sem):
        for peer in me.peers(False, False):
            pl.semaphore_signal(sem, inc=1, device_id=peer, device_id_type=MESH)

    def narrow_copies(layer):
        return copies_of([(narrow_in[layer].at[t], narrow.at[t]) for t in range(tens)], narrow_sem)

    def feed_back(layer, x, norms, poll, middle):
        def block_of(i):
            core = jnp.where(i < 2, 1 - me.core, me.core)
            return lax.rem(i, 2) * 2 + core

        def feed(t, slot):
            return copies_of(
                [(wide_in[layer].at[t], wide.at[slot]), (act_in[layer].at[t], act.at[slot]),
                 (slope_in[layer].at[t], slope.at[slot])],
                feed_sem.at[slot],
            )

        for copy in feed(block_of(0), 0):
            copy.start()
        mix_back_start(gx, x, norms, low, low_t, normed_t)
        mlp[...] = jnp.zeros_like(mlp)

        def one(i, _):
            t, slot = block_of(i), lax.rem(i, 2)

            @pl.when(i + 1 < tens)
            def _():
                for copy in feed(block_of(i + 1), 1 - slot):
                    copy.start()

            for copy in feed(t, slot):
                copy.wait()
            saved = pltpu.make_async_copy(staging, early_in[layer].at[t], stage_sem)

            @pl.when(i > 0)
            def _():
                saved.wait()

            pl.when(i == 2)(middle)
            mlp[...] += mix_back_part(
                low, low_t, normed_t, at.at[t], act.at[slot], slope.at[slot],
                lambda: joined(narrow.at[t], slice(256, 256 + QW)),
                lambda: joined(wide.at[slot], slice(0, hidden)),
                lambda cols: joined(wide.at[slot], slice(hidden + cols.start, hidden + cols.stop)),
                dout.at[t], functools.partial(put, staging),
                functools.partial(poll, i) if poll else None,
            )
            saved.start()
            return 0

        lax.fori_loop(0, tens, one, 0)
        pltpu.make_async_copy(staging, early_in[layer].at[0], stage_sem).wait()

    loads = copies_of(
        [(gx_in, gx), (x1_in, x1), (at_in[1], at), (qt_in[1], qt), (lse_in[1], lse)], in_sem
    )
    narrow_loads = narrow_copies(1)
    for copy in loads + narrow_loads:
        copy.start()
    me.greet(corner=True)
    attend_back_start(kv_ref[...], keys, values, keys_t)
    dkeys[...] = jnp.zeros_like(dkeys)
    dvalues[...] = jnp.zeros_like(dvalues)
    for copy in loads + narrow_loads:
        copy.wait()

    feed_back(1, x1[...], norms1, None, scatter1.send)
    scatter1.fetch()

    def attention(steps, span):
        due = within(steps, 0, 4 * tens * span)

        def one(t, _):
            attend_back_part(
                place, qt.at[t], dout.at[t], at.at[t], lse.at[t], keys, values, keys_t,
                dkeys, dvalues, gqt.at[t], cos, sin,
                lambda i: timed(due, (t * (place + 1) + i) * span, span),
            )
            return 0

        lax.fori_loop(0, tens, one, 0)
        return tens * (place + 1) * span

    now = attention(steps1, 24)
    seconds = copies_of([(at_in[0], at), (qt_in[0], qt), (lse_in[0], lse)], in_sem)
    for copy in seconds:
        copy.start()

    normed_t[...] = turn(normed_rows(x1[...], norms1[0:1], norms1[1:2])).astype(BF16)
    attn[...] = jnp.zeros_like(attn)

    def second(t, _):
        timed(within(steps1, 90, 470), now + t * 20, 20)
        attn[...] += dot_nt(
            turn(gqt[t, :QW]).astype(BF16), joined(narrow.at[t], slice(0, QW))
        )
        saved = pltpu.make_async_copy(late0, late1.at[t], late_sem.at[0])

        @pl.when(t > 0)
        def _():
            saved.wait()

        put(late0, 0, dot_nt(normed_t[...], gqt[t]).astype(BF16))
        saved.start()
        return 0

    lax.fori_loop(0, tens, second, 0)
    now = now + tens * 20
    narrow_loads = narrow_copies(0)
    for copy in narrow_loads:
        copy.start()
    pltpu.make_async_copy(late0, late1.at[0], late_sem.at[0]).wait()
    scatter_late.begin()
    sums, change = norm_back(x1[...], attn[...], mlp[...], norms1)
    other[...] = sums
    gx[...] += change

    for copy in narrow_loads + seconds:
        copy.wait()
    longest = 4 * tens * 24 + tens * 20
    base = now

    def moment(i, part):
        return jnp.where(i < 2, base, longest) + (i * 4 + part) * 12

    def middle():
        half = longest + 96
        timed(within(steps1, 0, half), base + 96, half - base - 96)
        release(free_sem)
        pl.semaphore_wait(free_sem, 6)
        scatter0.send()

    feed_back(
        0, x0_ref[...].astype(F32), norms0,
        lambda i, part: timed(within(steps1, 170, 660), moment(i, part), 12), middle,
    )
    release(again_sem)
    scatter0.fetch()

    now = attention(steps0, 24)
    for part in range(tens):
        span = slice(part * rows, (part + 1) * rows)
        piece = jnp.concatenate([turn(dkeys[span]), turn(dvalues[span])], axis=0)
        merge_low[part] = piece.astype(BF16)

        @pl.when(place == part)
        def _(piece=piece):
            merged[...] = piece

    merges = [
        remote(merge_low.at[peer[1]], merge_land.at[k], merge_send.at[k], merge_recv.at[k], peer)
        for k, peer in enumerate((me.to_core, me.to_y, me.to_corner))
    ]
    for copy in merges:
        copy.start()
    normed_t[...] = turn(
        normed_rows(x0_ref[...].astype(F32), norms0[0:1], norms0[1:2])
    ).astype(BF16)
    longest = 4 * tens * 24
    timed(steps0, now, longest - now)
    now = longest
    for copy in merges:
        copy.wait_recv()
    merged[...] += (
        merge_land[0].astype(F32) + merge_land[1].astype(F32) + merge_land[2].astype(F32)
    )
    shared_rows(merged[...], cos, sin, shared)
    attn[...] = shared_back(
        shared, joined(narrow.at[0], slice(QW, 256)), joined(narrow.at[0], slice(256 + QW, 512))
    )

    def fourth(t, _):
        timed(within(steps0, 384, 464), now + t * 20, 20)
        grad_t = gqt[t, :QW]
        attn[...] += dot_nt(turn(grad_t).astype(BF16), joined(narrow.at[t], slice(0, QW)))
        left = jnp.concatenate([grad_t, shared[:HD]], axis=0)
        saved = pltpu.make_async_copy(late0, late0_out.at[t, :, :, :, 0:256], late_sem.at[0])

        @pl.when(t > 0)
        def _():
            saved.wait()

        put(late0, 0, dot_nt(normed_t[...], left).astype(BF16))
        saved.start()
        return 0

    lax.fori_loop(0, tens, fourth, 0)
    now = now + tens * 20
    sums, change = norm_back(x0_ref[...].astype(F32), attn[...], mlp[...], norms0)
    gx[...] += change
    put(right_ref, 0, right_columns(shared, normed_t, sums, other[...]))
    saves = [pltpu.make_async_copy(late0, late0_out.at[0, :, :, :, 0:256], late_sem.at[0])]
    for t in range(tens):
        saves.append(
            pltpu.make_async_copy(
                right_ref, late0_out.at[t, :, :, :, 256:384], late_sem.at[1 + t]
            )
        )
        saves[-1].start()
    for copy in saves:
        copy.wait()
    pl.semaphore_wait(again_sem, 6)
    scatter_last.begin()
    saved = pltpu.make_async_copy(gx, grad_out, late_sem.at[1 + tens])
    saved.start()
    timed(steps0, now, 10000)
    saved.wait()
    for copy in merges:
        copy.wait_send()


def backward_call(norms, trig, kv, x0, gx, x1, qts, ats, lses, acts, slopes, narrows, wides):
    rows, width = x0.shape
    tens = qts[0].shape[0]
    length = kv.shape[0]
    hidden = acts[0].shape[2]
    early_cols = 2 * hidden + 256
    depth = width // 8
    weights = [blocks_of(pack) for pack in narrows + wides]
    vmem = pl.BlockSpec(memory_space=pltpu.VMEM)
    anywhere = pl.BlockSpec(memory_space=pl.ANY)
    heads = pltpu.VMEM((tens, 256, rows), BF16)
    state = pltpu.VMEM((rows, width), F32)
    args = [norms, trig, kv, x0, gx, x1, *qts, *ats, *lses, *acts, *slopes, *weights]
    return pl.pallas_call(
        backward_kernel,
        in_specs=[vmem] * 4 + [anywhere] * (len(args) - 4),
        out_specs=[vmem] * 4 + [anywhere] * 5,
        out_shape=[
            jax.ShapeDtypeStruct((depth, early_cols), F32),
            jax.ShapeDtypeStruct((depth, early_cols), F32),
            jax.ShapeDtypeStruct((depth, 384), F32),
            jax.ShapeDtypeStruct((depth, 256), F32),
            jax.ShapeDtypeStruct((rows, width), F32),
            jax.ShapeDtypeStruct((tens, 4, 2, depth, 384), BF16),
            jax.ShapeDtypeStruct((tens, 4, 2, depth, 256), BF16),
            jax.ShapeDtypeStruct((tens, 4, 2, depth, early_cols), BF16),
            jax.ShapeDtypeStruct((tens, 4, 2, depth, early_cols), BF16),
        ],
        scratch_shapes=Scatter.scratch(depth, early_cols)
        + Scatter.scratch(depth, 384)
        + [
            pltpu.SemaphoreType.REGULAR,
            pltpu.SemaphoreType.REGULAR,
            state,
            state,
            state,
            state,
            heads,
            heads,
            pltpu.VMEM((tens, 8, rows), F32),
            heads,
            heads,
            pltpu.VMEM((length, HD), BF16),
            pltpu.VMEM((length, HD), BF16),
            pltpu.VMEM((HD, length), BF16),
            pltpu.VMEM((length, HD), F32),
            pltpu.VMEM((length, HD), F32),
            pltpu.VMEM((rows, width), BF16),
            pltpu.VMEM((width, rows), BF16),
            pltpu.VMEM((width, rows), BF16),
            pltpu.VMEM((tens, 4, 2, depth, 512), BF16),
            pltpu.VMEM((2, 4, 2, depth, 2 * hidden), BF16),
            pltpu.VMEM((2, rows, hidden), BF16),
            pltpu.VMEM((2, rows, hidden), BF16),
            pltpu.VMEM((4, 2, depth, early_cols), BF16),
            pltpu.VMEM((4, 2, depth, 256), BF16),
            pltpu.VMEM((4, 2, depth, 128), BF16),
            pltpu.VMEM((2 * HD, rows), BF16),
            pltpu.VMEM((4, width), F32),
            pltpu.VMEM((tens, 2 * HD, rows), BF16),
            pltpu.VMEM((3, 2 * HD, rows), BF16),
            pltpu.VMEM((2 * HD, rows), F32),
            pltpu.SemaphoreType.DMA((3,)),
            pltpu.SemaphoreType.DMA((3,)),
            pltpu.SemaphoreType.DMA((5,)),
            pltpu.SemaphoreType.DMA((tens,)),
            pltpu.SemaphoreType.DMA((2, 3)),
            pltpu.SemaphoreType.DMA,
            pltpu.SemaphoreType.DMA((tens + 2,)),
        ],
        compiler_params=comm_params(5),
    )(*args)


def lamb_parts(weight, first, second, grad):
    first_new = BETA_FIRST * first + (1.0 - BETA_FIRST) * grad
    second_new = BETA_SECOND * second + (1.0 - BETA_SECOND) * grad * grad
    update = (
        first_new
        / (1.0 - BETA_FIRST**STEP)
        / (jnp.sqrt(second_new / (1.0 - BETA_SECOND**STEP)) + ADAM_EPSILON)
        + WEIGHT_DECAY * weight
    )
    return (first_new, second_new, update)


def keyval_grad(late):
    lane = lax.broadcasted_iota(jnp.int32, (late.shape[0], 2 * HD), 1)
    left = pltpu.roll(late[:, 128:256], HD, 1)
    right = pltpu.roll(late[:, 256:384], HD, 1)
    return jnp.where(lane < HD, left, right)


def norm_grad(late):
    return turn(late[:, 256:384])[HD : HD + 8]


def square(value):
    total = jnp.sum(value * value, axis=1, keepdims=True)
    return jnp.sum(total, axis=0, keepdims=True)


def lanes(pairs):
    lane = lax.broadcasted_iota(jnp.int32, (1, 128), 1)
    row = jnp.zeros((1, 128), F32)
    for place, value in pairs:
        row = jnp.where(lane == place, value, row)
    return row


class Tensors:
    def __init__(self, refs, early, late):
        self.refs = refs
        self.early, self.late = early, late

    def early_grad(self, layer, which):
        pack = self.early[layer]
        hidden = (pack.shape[1] - 256) // 2
        if which == "up":
            return pack[:, :hidden]
        if which == "down":
            return pack[:, hidden : 2 * hidden]
        return turn(pack[:, 2 * hidden :])[:QW]

    def parts(self, array, index, grad):
        weight, first, second = (ref[...] if index is None else ref[index] for ref in array)
        return (weight,) + lamb_parts(weight, first, second, grad)

    def each(self):
        query, keyval, output, upward, downward, norms = range(6)
        for layer in range(2):
            yield 5 + layer, upward, layer, lambda: self.early_grad(layer, "up")
            yield 7 + layer, downward, layer, lambda: self.early_grad(layer, "down")
            yield 3 + layer, output, layer, lambda: self.early_grad(layer, "output")
            yield layer, query, layer, lambda: self.late[layer][:, :QW]
        yield 2, keyval, None, lambda: keyval_grad(self.late[0][...])
        for layer in range(2):
            rows = slice(4 * layer, 4 * layer + 4)
            yield 9 + 4 * layer, norms, layer, lambda: norm_grad(self.late[0][...])[rows]


def norms_kernel(*refs):
    refs = Refs(refs)
    early0, early1, late0, late1 = refs.take(4)
    arrays = [refs.take(3) for _ in range(6)]
    sums_ref = refs.take(1)[0]
    near_land, along_land, send, recv = refs.take(4)
    me = Place()
    me.hail(near=True)
    tensors = Tensors(arrays, (early0, early1), (late0, late1))
    leader = (me.tensor == 0).astype(F32)
    old, new = [], []
    for place, array, index, grad in tensors.each():
        weight, _, _, update = tensors.parts(arrays[array], index, grad())
        if place >= 9:
            for row in range(4):
                old.append((place + row, square(weight[row : row + 1]) * leader))
                new.append((place + row, square(update[row : row + 1]) * leader))
        else:
            scale = leader if place == 2 else 1.0
            old.append((place, square(weight) * scale))
            new.append((place, square(update) * scale))

    me.listen(near=True)
    near_land[0] = jnp.concatenate([lanes(old), lanes(new), jnp.zeros((6, 128), F32)], axis=0)
    copies = []
    for code, peer in me.near():
        copies.append(
            remote(near_land.at[0], near_land.at[code], send.at[code], recv.at[code], peer)
        )
        copies[-1].start()
    for copy in copies:
        copy.wait()
    total = jnp.zeros((8, 128), F32)
    for x in range(2):
        for y in range(2):
            for core in range(2):
                code = lax.rem(x + me.x, 2) * 4 + lax.rem(y + me.y, 2) * 2
                total = total + near_land[code + lax.rem(core + me.core, 2)]
    along_land[0] = total
    copies = []
    for shift in (1, 2, 3):
        copies.append(
            remote(
                along_land.at[0], along_land.at[shift], send.at[7 + shift],
                recv.at[7 + shift], me.at(z=me.along(shift)),
            )
        )
        copies[-1].start()
    for copy in copies:
        copy.wait()
    total = jnp.zeros((8, 128), F32)
    for z in range(4):
        total = total + along_land[me.along(4 - z)]
    sums_ref[...] = total


def norms_call(early, late, arrays):
    vmem = pl.BlockSpec(memory_space=pltpu.VMEM)
    flat = [ref for array in arrays for ref in array]
    return pl.pallas_call(
        norms_kernel,
        in_specs=[vmem] * (4 + len(flat)),
        out_specs=vmem,
        out_shape=jax.ShapeDtypeStruct((8, 128), F32),
        scratch_shapes=[
            pltpu.VMEM((8, 8, 128), F32),
            pltpu.VMEM((4, 8, 128), F32),
            pltpu.SemaphoreType.DMA((11,)),
            pltpu.SemaphoreType.DMA((11,)),
        ],
        compiler_params=comm_params(8),
    )(*early, *late, *flat)


def lamb_kernel(*refs):
    refs = Refs(refs)
    sums_ref, grad_ref, early0, early1, late0, late1 = refs.take(6)
    arrays = [refs.take(3) for _ in range(6)]
    outs = [refs.take(4) for _ in range(6)]
    norm_out, ratio_out, grad_out = refs.take(3)
    grad_out[...] = grad_ref[...]
    weight_norm = jnp.sqrt(sums_ref[0:1])
    update_norms = jnp.sqrt(sums_ref[1:2])
    used = lax.broadcasted_iota(jnp.int32, (1, 128), 1) < 17
    ratios = jnp.where(used, weight_norm / jnp.where(used, update_norms, 1.0), 0.0)
    norm_out[...] = update_norms
    ratio_out[...] = ratios
    tensors = Tensors(arrays, (early0, early1), (late0, late1))
    for place, array, index, grad in tensors.each():
        weight, first, second, update = tensors.parts(arrays[array], index, grad())
        if place >= 9:
            factor = jnp.concatenate(
                [ratios[:, place + row : place + row + 1] for row in range(4)], axis=0
            )
        else:
            factor = ratios[:, place : place + 1]
        after = weight - LEARN_RATE * factor * update
        where = Ellipsis if index is None else index
        for ref, value in zip(outs[array], (first, second, after, after.astype(BF16))):
            ref[where] = value


def lamb_call(sums, grad, early, late, arrays):
    vmem = pl.BlockSpec(memory_space=pltpu.VMEM)
    flat = [ref for array in arrays for ref in array]
    shapes = []
    for array in arrays:
        shape = array[0].shape
        shapes += [jax.ShapeDtypeStruct(shape, F32)] * 3 + [jax.ShapeDtypeStruct(shape, BF16)]
    shapes += [jax.ShapeDtypeStruct((1, 128), F32)] * 2
    shapes.append(jax.ShapeDtypeStruct(grad.shape, F32))
    return pl.pallas_call(
        lamb_kernel,
        in_specs=[vmem] * (6 + len(flat)),
        out_specs=[vmem] * len(shapes),
        out_shape=shapes,
        compiler_params=comm_params(None),
    )(sums, grad, *early, *late, *flat)


def angles(places):
    steps = jnp.arange(HALF).astype(F32)
    inverse = jnp.exp(steps * (-2.0 * math.log(10000.0) / ROT))
    phase = (0.25 * inverse)[:, None] * places.astype(F32)[None, :]
    return jnp.concatenate([jnp.cos(phase), jnp.sin(phase)], axis=0)


def param_squares(arrays, leader):
    query, keyval, output, upward, downward, norms = arrays
    return jnp.concatenate(
        [
            jnp.sum(query * query, axis=(1, 2)),
            (jnp.sum(keyval * keyval) * leader)[None],
            jnp.sum(output * output, axis=(1, 2)),
            jnp.sum(upward * upward, axis=(1, 2)),
            jnp.sum(downward * downward, axis=(1, 2)),
            jnp.sum(norms * norms, axis=2).reshape(8) * leader,
        ]
    )


def apply_trust(masters, updates, trust):
    factors = (
        trust[0:2][:, None, None],
        trust[2],
        trust[3:5][:, None, None],
        trust[5:7][:, None, None],
        trust[7:9][:, None, None],
        trust[9:17].reshape(2, 4, 1),
    )
    return tuple(
        (
            weight - LEARN_RATE * factor * update
            for weight, factor, update in zip(masters, factors, updates)
        )
    )


def plain_scatter(parts, depth):
    pieces = parts.reshape(-1, depth, parts.shape[-1])
    return lax.psum_scatter(pieces, ("tensor", "dp"), scatter_dimension=0).astype(F32)


def shards(
    fast,
    hidden_in,
    out_grad,
    positions,
    query_weight,
    keyval_weight,
    output_weight,
    up_weight,
    down_weight,
    norm_params,
    query_first,
    query_second,
    keyval_first,
    keyval_second,
    output_first,
    output_second,
    up_first,
    up_second,
    down_first,
    down_second,
    norm_first,
    norm_second,
):
    masters = (query_weight, keyval_weight, output_weight, up_weight, down_weight, norm_params)
    tensor = lax.axis_index("tensor")
    leader = (tensor == 0).astype(F32)
    rows, width = hidden_in.shape
    tens = positions.shape[0] // rows
    depth = keyval_weight.shape[0]

    def joined(pack):
        return pack.reshape(tens, width, pack.shape[-1])

    trig = angles(lax.dynamic_slice_in_dim(positions, tensor * rows, rows, 0))
    if fast:
        norm_rows, norm_later, kv, state, act, slope, *others = forward_call(
            hidden_in, trig, masters[:4] + (jnp.swapaxes(down_weight, 1, 2), norm_params)
        )
        kv = kv.reshape(-1, 2 * HD)
        qts, ats, lses = others[0:2], others[2:4], others[4:6]
        attn_all = [joined(others[6]), joined(others[8])]
        feed_all = [joined(others[7]), joined(others[9])]
        saved = [(hidden_in, qts[0], ats[0], lses[0], act, slope)]
        current, act, slope = mix_call(state, norm_later, ats[1], attn_all[1], feed_all[1])
        saved.append((state, qts[1], ats[1], lses[1], act, slope))
    else:
        narrow, wide = [], []
        for layer in range(2):
            if layer == 0:
                keys, values = keyval_weight[:, :HD], keyval_weight[:, HD:]
            else:
                keys = values = jnp.zeros((depth, HD), F32)
            pieces = [query_weight[layer], keys, output_weight[layer].T, values]
            narrow.append(jnp.concatenate(pieces, axis=1).astype(BF16))
            wide.append(
                jnp.concatenate([up_weight[layer], down_weight[layer].T], axis=1).astype(BF16)
            )
        norm_low = norm_params.astype(BF16).reshape(8, depth)
        attn_all, feed_all = (
            [joined(lax.all_gather(pack, ("tensor", "dp"), axis=0)) for pack in packs]
            for packs in (narrow, wide)
        )
        norm_full = lax.all_gather(norm_low, "dp", axis=0)
        norm_full = jnp.swapaxes(norm_full, 0, 1).reshape(2, 4, width).astype(F32)
        current = hidden_in
        saved = []
        for layer in range(2):
            norms = norm_full[layer]
            if layer == 0:
                qt, kv = qkv_call(True, current, norms, trig, attn_all[layer])
                kv = share_call(kv, tens).reshape(-1, 2 * HD)
            else:
                (qt,) = qkv_call(False, current, norms, trig, attn_all[layer])
            at, lse = attend_call(qt, kv)
            after, act, slope = mix_call(current, norms, at, attn_all[layer], feed_all[layer])
            saved.append((current, qt, at, lse, act, slope))
            current = after

    x, qt, at, lse, act, slope = saved[1]
    early, late = [None, None], [None, None]
    if fast:
        early[0], early[1], late[0], late[1], grad, *_ = backward_call(
            norm_rows, trig, kv, hidden_in, out_grad, x, qts, ats, lses,
            [saved[0][4], act], [saved[0][5], slope], attn_all, feed_all,
        )
    else:
        norms = norm_full[1]
        pack, dout, mlp = mix_back_call(
            out_grad, x, norms, at, act, slope, attn_all[1], feed_all[1]
        )
        gqt, dkv = attend_back_call(qt, dout, at, lse, kv, trig)
        early[1] = plain_scatter(pack, depth)
        grad, pack, sums = norm_back_call(False, out_grad, x, norms, mlp, gqt, attn_all[1])
        late[1] = plain_scatter(pack, depth)
        x, qt, at, lse, act, slope = saved[0]
        norms = norm_full[0]
        pack, dout, mlp = mix_back_call(
            grad, x, norms, at, act, slope, attn_all[0], feed_all[0]
        )
        early[0] = plain_scatter(pack, depth)
        gqt, dkv = attend_back_call(qt, dout, at, lse, kv, trig, dkv)
        dkv = merge_call(dkv)
        grad, pack = norm_back_call(
            True, grad, x, norms, mlp, gqt, attn_all[0], dkv, trig, sums
        )

    arrays = (
        (query_weight, query_first, query_second),
        (keyval_weight, keyval_first, keyval_second),
        (output_weight, output_first, output_second),
        (up_weight, up_first, up_second),
        (down_weight, down_first, down_second),
        (norm_params, norm_first, norm_second),
    )
    if fast:
        arrays = arrays[:4] + (tuple(jnp.swapaxes(a, 1, 2) for a in arrays[4]),) + arrays[5:]
        totals = norms_call(early, late, arrays)
        *nexts, update_norms, trust_ratios, grad = lamb_call(totals, grad, early, late, arrays)
        nexts[16:20] = [jnp.swapaxes(a, 1, 2) for a in nexts[16:20]]
        return (current, grad, *nexts, update_norms[0, :17], trust_ratios[0, :17])
    late[0] = plain_scatter(pack, depth)
    hidden = up_weight.shape[2]
    query_g = jnp.stack([late[layer][:, :QW] for layer in range(2)])
    keyval_g = late[0][:, QW : QW + 2 * HD]
    output_g = jnp.stack([early[layer][:, 2 * hidden : 2 * hidden + QW].T for layer in range(2)])
    up_g = jnp.stack([early[layer][:, :hidden] for layer in range(2)])
    down_g = jnp.stack([early[layer][:, hidden : 2 * hidden].T for layer in range(2)])
    norm_g = late[0][:, QW + 2 * HD : QW + 2 * HD + 8].T.reshape(2, 4, depth)

    grads = (query_g, keyval_g, output_g, up_g, down_g, norm_g)
    parts = [lamb_parts(*array, grad) for array, grad in zip(arrays, grads)]
    updates = tuple((part[2] for part in parts))
    weight_total, update_total = lax.psum(
        (param_squares(masters, leader), param_squares(updates, leader)), ("dp", "tensor")
    )
    weight_norm = jnp.sqrt(weight_total)
    update_norms = jnp.sqrt(update_total)
    trust_ratios = weight_norm / update_norms
    nexts = apply_trust(masters, updates, trust_ratios)
    outs = [current, grad]
    for index in range(6):
        low = nexts[index].astype(BF16)
        outs += [parts[index][0], parts[index][1], nexts[index], low]
    return tuple(outs) + (update_norms, trust_ratios)


def solution(mesh):
    fast = mesh.shape["dp"] == 8 and mesh.shape["tensor"] == 4
    columns = P(None, "dp", "tensor")
    across = P(None, "tensor", "dp")
    flat = P("dp", None)
    norm = P(None, None, "dp")
    state = P(("dp", "tensor"), None)
    in_specs = (
        (state, state, P("dp"), columns, flat, across, columns, across, norm)
        + (columns, columns, flat, flat, across, across, columns, columns, across, across)
        + (norm, norm)
    )
    out_specs = (
        (state, state)
        + (columns,) * 4
        + (flat,) * 4
        + (across,) * 4
        + (columns,) * 4
        + (across,) * 4
        + (norm,) * 4
        + (P(), P())
    )
    return jax.shard_map(
        functools.partial(shards, fast),
        mesh=mesh,
        in_specs=in_specs,
        out_specs=out_specs,
        check_vma=False,
    )
```
